128 devices in a mesh: ctx: 32 (over z, y_lo, x), tp: 4 (over y_hi, core).
Axes of the slice: x: 4, y: 4 (y_hi: 2, y_lo: 2; y = y_hi * 2 + y_lo), z: 4, core: 2. Of those that a mesh axis runs over, the one named last changes fastest.
Arguments:
- tokens: bfloat16 [16384, 1024], P('ctx'), may hold values from -6 to 6
- sub_blocks: int32 [4, 32], replicated, may hold values from 0 to 31, each once within a row
- w_qkv: bfloat16 [1024, 3, 1024], P(None, None, 'tp'), may hold values from -0.1875 to 0.1875
- qv_bias: bfloat16 [2, 1024], P(None, 'tp'), may hold values from -2 to 2
- w_out: bfloat16 [1024, 1024], P('tp'), may hold values from -3 to 3
- w_up: bfloat16 [1024, 4096], P(None, 'tp'), may hold values from -0.1875 to 0.1875
- up_bias: bfloat16 [4096], P('tp'), may hold values from -2 to 2
- w_down: bfloat16 [4096, 1024], P('tp'), may hold values from -0.09375 to 0.09375
- ln_gains: bfloat16 [2, 1024], replicated, may hold values from 0.099609375 to 1.8984375
- row_biases: bfloat16 [4, 1024], replicated, may hold values from -2 to 2
- cotangent: bfloat16 [16384, 1024], P('ctx'), may hold values from -6 to 6
Outputs:
- layer_out: float32 [16384, 1024], P('ctx')
- input_grad: float32 [16384, 1024], P('ctx')
- rms_rows: float32 [3, 16384], P(None, 'ctx')
- grad_qkv: float32 [1024, 3, 1024], P('ctx', None, 'tp')
- grad_qv_bias: float32 [2, 1024], P(None, ('tp', 'ctx'))
- grad_out: float32 [1024, 1024], P('tp', 'ctx')
- grad_up: float32 [1024, 4096], P('ctx', 'tp')
- grad_up_bias: float32 [4096], P(('tp', 'ctx'))
- grad_down: float32 [4096, 1024], P('tp', 'ctx')
- grad_gains: float32 [2, 1024], P(None, 'ctx')
- grad_shifts: float32 [4, 1024], P(None, 'ctx')
The draws below stay inside these ranges and needn't reach their ends.
Inputs may be any that keep to these rules, and one draw needn't show every extreme that they name: Each row is a permutation: device d of ctx holds sub-block sub_blocks[g, d] (positions sub_blocks[g, d] * 128 to sub_blocks[g, d] * 128 + 127) of sequence g.
All inputs are finite; a program needn't handle non-finite values.
Results may differ from the reference program's by a relative error of at most 0.013.
Values may be sent and summed in bfloat16 or wider, within the bound.
No kernel may reach another device: no remote copies, remote signals or barrier semaphores. Data moves between devices by JAX's collectives and lax.ppermute only.
A program may use at most 256 MiB of HBM per device.

```python
import jax
import jax.numpy as jnp
from jax import lax

D = 1024
HEADS = 16
HEAD = 64
FF = 4096
PROMPT = 2048
CONT = 256
GLEN = 4096
BLK = 512
TOKENS = 16384
GROUPS = 4
SUB = 128
N_CTX = 32


def spiked(drawn, rng, source, target, blocks, factor):
    def block_of(axis_at):
        return (jnp.arange(drawn.shape[axis_at]) // (drawn.shape[axis_at] // blocks)).reshape((-1,) + (1,) * (drawn.ndim - 1 - axis_at))

    near = jax.random.permutation(rng, blocks)[block_of(target)]
    second = (block_of(target) + blocks // 2) % blocks
    return jnp.where((block_of(source) == near) | (block_of(source) == second), factor * drawn, drawn)


def shard_levels(stream_key, extent, shards, least, largest):
    def one(axis_at, shards_of):
        steps = jax.random.uniform(jax.random.fold_in(jax.random.fold_in(stream_key, 6), axis_at), (shards_of,), jnp.float32, least / len(shards), largest / len(shards))
        return jnp.repeat(jnp.exp(steps), extent[axis_at] // shards_of).reshape((-1,) + (1,) * (len(extent) - axis_at - 1))

    level = one(*shards[0])
    for cut in shards[1:]:
        level = level * one(*cut)
    return level


def bell_draw(own_key, extent, deviation, most, shards=(), kind=jnp.bfloat16):
    entries = deviation * jax.random.normal(own_key, extent, jnp.float32)
    if shards:
        entries = entries * shard_levels(own_key, extent, shards, -0.22, 0.18)
    return jnp.clip(entries, -most, most).astype(kind)


def gaussian_with(stream_key, shape, deviation, most, shards, heavy, held_as=jnp.bfloat16):
    result = deviation * jax.random.normal(stream_key, shape, jnp.float32)
    if shards:
        result = result * shard_levels(stream_key, shape, shards, -0.22, 0.18)
    return jnp.clip(spiked(result, jax.random.fold_in(stream_key, 3), *heavy), -most, most).astype(held_as)


def setup_inputs(seed: int = 0) -> dict:
    key_list = jax.random.split(jax.random.key(seed), 12)
    return {
        "tokens": bell_draw(key_list[0], (TOKENS, D), 1.0, 6.0, ((0, 32),)),
        "sub_blocks": jax.vmap(lambda own: jax.random.permutation(own, N_CTX))(jax.random.split(key_list[1], GROUPS)).reshape((GROUPS, N_CTX)).astype(jnp.int32),
        "w_qkv": bell_draw(key_list[2], (D, 3, D), D ** -0.5, 0.1875, ((2, 4),)),
        "qv_bias": bell_draw(key_list[3], (2, D), 0.3, 2.0, ((1, 4),)),
        "w_out": bell_draw(key_list[4], (D, D), (D * 16 // GLEN) ** -0.5, 3.0, ((0, 4),)),
        "w_up": bell_draw(key_list[5], (D, FF), D ** -0.5, 0.1875, ((1, 4),)),
        "up_bias": bell_draw(key_list[6], (FF,), 0.3, 2.0, ((0, 4),)),
        "w_down": bell_draw(key_list[7], (FF, D), FF ** -0.5, 0.09375, ((0, 4),)),
        "ln_gains": jnp.clip(1.0 + 0.18 * jax.random.normal(key_list[8], (2, D), jnp.float32), 0.099609375, 1.8984375).astype(jnp.bfloat16),
        "row_biases": bell_draw(key_list[9], (4, D), 0.3, 2.0),
        "cotangent": gaussian_with(key_list[10], (TOKENS, D), 1.0, 6.0, ((0, 32),), (0, 1, 32, 2.75)),
    }


EPSILON = 1e-05
RMS_EPSILON = 1e-06
HIGHEST = lax.Precision.HIGHEST

@jax.custom_vjp
def low(v):
    return lax.optimization_barrier(v.astype(jnp.bfloat16)).astype(jnp.float32)

@jax.custom_vjp
def low_back(v):
    return v

def low_keep(v):
    return (low(v), None)

def low_pass(kept, grad):
    return (grad,)

def back_keep(v):
    return (v, None)

def back_low(kept, grad):
    return (low(grad),)
low.defvjp(low_keep, low_pass)
low_back.defvjp(back_keep, back_low)

def norm_rows(values, gain, shift):
    centre = lax.optimization_barrier(jnp.mean(values, axis=-1, keepdims=True))
    centred = values - centre
    spread = lax.optimization_barrier(jnp.mean(centred * centred, axis=-1, keepdims=True))
    return centred * lax.rsqrt(spread + EPSILON) * gain + shift

def visible(query_pos, key_pos):
    causal = key_pos <= query_pos
    prompt_key = key_pos < PROMPT
    cont_query = query_pos >= PROMPT
    same_cont = (key_pos - PROMPT) // CONT == (query_pos - PROMPT) // CONT
    return causal & (prompt_key | cont_query & same_cont)

def group_layer(params, tokens):
    w_qkv, qv_bias, w_out, w_up, up_bias, w_down, ln_gains, row_biases = params
    score_scale = HEAD ** (-0.5)
    normed = low(norm_rows(tokens, ln_gains[0], row_biases[0]))
    projected = jnp.dot(normed, w_qkv.reshape(D, 3 * D), precision=HIGHEST).reshape(GLEN, 3, HEADS, HEAD)
    queries = low_back(low(projected[:, 0] + qv_bias[0].reshape(HEADS, HEAD)))
    key_rows = low_back(low(projected[:, 1]))
    values = low_back(low(projected[:, 2] + qv_bias[1].reshape(HEADS, HEAD)))
    block_rows = min(512, GLEN)
    positions = jnp.arange(GLEN, dtype=jnp.int32)

    def attend(block_index):
        first_row = block_index * block_rows
        query_rows = lax.dynamic_slice_in_dim(queries, first_row, block_rows, 0)
        query_pos = first_row + jnp.arange(block_rows, dtype=jnp.int32)
        scores = low_back(jnp.einsum('qhd,khd->hqk', query_rows, key_rows, precision=HIGHEST))
        allowed = visible(query_pos[None, :, None], positions[None, None, :])
        weights = jnp.where(allowed, jnp.exp(scores * score_scale), 0.0)
        attention = low(weights / lax.optimization_barrier(jnp.sum(weights, axis=-1, keepdims=True)))
        return jnp.einsum('hqk,khd->qhd', attention, values, precision=HIGHEST)
    mixed_rows = lax.map(jax.checkpoint(attend), jnp.arange(GLEN // block_rows, dtype=jnp.int32))
    head_rows = low_back(low(mixed_rows.reshape(GLEN, D)))
    attn_branch = low_back(jnp.dot(head_rows, w_out, precision=HIGHEST) + row_biases[1])
    residual = tokens + attn_branch
    normed_two = low(norm_rows(residual, ln_gains[1], row_biases[2]))
    hidden = low_back(jnp.dot(normed_two, w_up, precision=HIGHEST) + up_bias)
    active = low(jax.nn.gelu(hidden, approximate=False))
    mlp_branch = jnp.dot(active, w_down, precision=HIGHEST) + row_biases[3]
    return (residual + mlp_branch, attn_branch, mlp_branch)

def reference(tokens, sub_blocks, w_qkv, qv_bias, w_out, w_up, up_bias, w_down, ln_gains, row_biases, cotangent):
    holder = jnp.argsort(sub_blocks, axis=1).astype(jnp.int32)
    positions = jnp.arange(GLEN, dtype=jnp.int32)
    group_ids = jnp.arange(GROUPS, dtype=jnp.int32)
    logical_rows = holder[:, positions // SUB] * BLK + group_ids[:, None] * SUB + positions[None, :] % SUB
    device_rows = jnp.arange(TOKENS, dtype=jnp.int32)
    row_group = device_rows % BLK // SUB
    back_index = row_group * GLEN + sub_blocks[row_group, device_rows // BLK] * SUB + device_rows % SUB
    params = tuple((member.astype(jnp.float32) for member in (w_qkv, qv_bias, w_out, w_up, up_bias, w_down, ln_gains, row_biases)))
    checked_layer = jax.checkpoint(group_layer)

    def full_layer(weights, inputs):

        def per_group(carried, indices):
            return (carried, checked_layer(weights, inputs[indices]))
        unused, results = lax.scan(per_group, jnp.zeros((), jnp.float32), logical_rows)
        return tuple((member.reshape(GROUPS * GLEN, D)[back_index] for member in results))
    results, pullback = jax.vjp(full_layer, params, tokens.astype(jnp.float32))
    layer_out, attn_out, mlp_out = results
    nothing = jnp.zeros_like(attn_out)
    grad_params, input_grad = pullback((cotangent.astype(jnp.float32), nothing, nothing))
    rms_rows = jnp.stack([jnp.sqrt(lax.optimization_barrier(jnp.mean(member * member, axis=-1)) + RMS_EPSILON) for member in (layer_out, attn_out, mlp_out)])
    grad_qkv, grad_qv_bias, grad_out, grad_up, grad_up_bias, grad_down, grad_gains, grad_shifts = grad_params
    return (layer_out, input_grad, rms_rows, grad_qkv, grad_qv_bias, grad_out, grad_up, grad_up_bias, grad_down, grad_gains, grad_shifts)
```

```python
from functools import partial

import jax
import jax.numpy as jnp
from jax import lax
from jax.experimental import pallas as pl
from jax.experimental.pallas import tpu as pltpu
from jax.sharding import PartitionSpec as P

HEAD = 64
SUBS = 32
HALF = 64
GROUPS = 4
ROWS = GROUPS * HALF
LOCAL = 256
TILE = 256
CHUNK = 512
EPSILON = 1e-05
RMS_EPSILON = 1e-06
LOG_SHRINK = 10 * 0.6931471805599453
SHRINK = 2.0**-10
CORE_SWAP = [(0, 1), (1, 0), (2, 3), (3, 2)]
YHI_SWAP = [(0, 2), (2, 0), (1, 3), (3, 1)]
NT = (((1,), (1,)), ((), ()))
TN = (((0,), (0,)), ((), ()))
bf16 = jnp.bfloat16
f32 = jnp.float32


def norm_parts(values):
    centre = jnp.mean(values, axis=-1, keepdims=True)
    centred = values - centre
    spread = jnp.mean(centred * centred, axis=-1, keepdims=True)
    inverse = lax.rsqrt(spread + EPSILON)
    return centred * inverse, inverse


def norm_back(grad_normed, unit_rows, inverse, gain):
    grad_unit = grad_normed * gain
    first_mean = jnp.mean(grad_unit, axis=-1, keepdims=True)
    second_mean = jnp.mean(grad_unit * unit_rows, axis=-1, keepdims=True)
    return inverse * (grad_unit - first_mean - unit_rows * second_mean)


def kernel_call(body, outs, scratch=(), scalars=1, ins=1, flops=0, name=None):
    smem = pl.BlockSpec(memory_space=pltpu.SMEM)
    vmem = pl.BlockSpec(memory_space=pltpu.VMEM)
    return pl.pallas_call(
        body,
        out_shape=[jax.ShapeDtypeStruct(s, d) for s, d in outs],
        in_specs=[smem] * scalars + [vmem] * ins,
        out_specs=[vmem] * len(outs),
        scratch_shapes=[pltpu.VMEM(s, d) for s, d in scratch],
        compiler_params=pltpu.CompilerParams(vmem_limit_bytes=40 * 2**20),
        cost_estimate=pl.CostEstimate(flops=flops, bytes_accessed=4 * 2**20, transcendentals=0),
        name=name,
    )


def fold(rows):
    return jnp.concatenate([rows[:32], rows[32:]], axis=1)


def unfold(packed):
    return jnp.concatenate([packed[:, :HEAD], packed[:, HEAD:]], axis=0)


def project_kernel(core_ref, x_ref, own_w, oth_w, gains, shifts, own_b, oth_b, send_ref, low_ref):
    core = core_ref[0]
    x = x_ref[:, core].reshape(ROWS, -1).astype(f32)
    unit, _ = norm_parts(x)
    low = (unit * gains[0:1].astype(f32) + shifts[0:1].astype(f32)).astype(bf16)
    low_ref[...] = low
    for w_ref, b_ref, half in ((own_w, own_b, core), (oth_w, oth_b, 1 - core)):
        made = jnp.dot(low, w_ref[...], preferred_element_type=f32)
        q = made[:, :LOCAL] + b_ref[0:1].astype(f32)
        k = made[:, LOCAL : 2 * LOCAL]
        v = made[:, 2 * LOCAL :] + b_ref[1:2].astype(f32)
        for g in range(GROUPS):
            for h in range(4):
                rows = slice(g * HALF, (g + 1) * HALF)
                cols = slice(h * HEAD, (h + 1) * HEAD)
                block = g * 8 + half * 4 + h
                send_ref[block, 0:64, :] = jnp.concatenate(
                    [q[rows, cols], k[rows, cols]], axis=1
                ).astype(bf16)
                send_ref[block, 64:96, :] = fold(v[rows, cols]).astype(bf16)


def pair_masks(core, transposed):
    shape = (CHUNK, TILE) if transposed else (TILE, CHUNK)
    q = lax.broadcasted_iota(jnp.int32, shape, 1 if transposed else 0)
    key = lax.broadcasted_iota(jnp.int32, shape, 0 if transposed else 1)
    other = key >= TILE
    k = jnp.where(other, key - TILE, key)
    q_sub = lax.shift_right_logical(q, 6)
    k_sub = lax.shift_right_logical(k, 6)
    prompt = (other & (q_sub + core > k_sub)) | (jnp.logical_not(other) & (q >= k))
    cont = prompt & (lax.shift_right_logical(q, 7) == lax.shift_right_logical(k, 7))
    return prompt, cont


def chunks_of(tile, prompt, cont):
    if tile < 4:
        return [(j, None) for j in range(tile)] + [(tile, prompt)]
    return [(j, None) for j in range(4)] + [(tile, cont)]


def attend_kernel(sc_ref, own_ref, oth_ref, out_ref, lse_ref, q_s, k_s, v_s):
    core = sc_ref[SUBS]
    const = jnp.full((HALF, HEAD), SHRINK, bf16)
    for p in range(SUBS):
        d = sc_ref[p]
        at = p // 4 * CHUNK + p % 4 * HALF
        q_s[p * HALF : (p + 1) * HALF, :] = own_ref[d, 0:64, :HEAD] * jnp.asarray(0.125, bf16)
        for ref, start in ((own_ref, at), (oth_ref, at + TILE)):
            k_s[start : start + HALF, :] = ref[d, 0:64, HEAD:]
            v = unfold(ref[d, 64:96, :]) * jnp.asarray(SHRINK, bf16)
            v_s[start : start + HALF, :] = jnp.concatenate([v, const], axis=1)
    prompt, cont = pair_masks(core, False)
    for t in range(8):
        q = q_s[t * TILE : (t + 1) * TILE, :]
        total = None
        for j, mask in chunks_of(t, prompt, cont):
            keys = slice(j * CHUNK, (j + 1) * CHUNK)
            s = lax.dot_general(q, k_s[keys, :], NT, preferred_element_type=f32)
            w = jnp.exp(s)
            if mask is not None:
                w = jnp.where(mask, w, 0.0)
            part = jnp.dot(w.astype(bf16), v_s[keys, :], preferred_element_type=f32)
            total = part if total is None else total + part
        mixed = total[:, :HEAD] / total[:, HEAD:]
        lse_ref[t : t + 1, :] = jnp.log(total.T[HEAD : HEAD + 1, :]) + LOG_SHRINK
        for i in range(4):
            out_ref[sc_ref[t * 4 + i]] = fold(mixed[i * HALF : (i + 1) * HALF]).astype(bf16)


def attend_back_kernel(
    sc_ref, own_ref, oth_ref, do_ref, o_ref, lse_ref,
    dq_ref, keep_ref, send_ref,
    q_s, do_s, vk_s, kt_s, inner_s, acc_s,
):
    core = sc_ref[SUBS]
    zero = jnp.zeros((HALF, HEAD), bf16)
    for p in range(SUBS):
        d = sc_ref[p]
        at = p // 4 * CHUNK + p % 4 * HALF
        rows = slice(p * HALF, (p + 1) * HALF)
        q = own_ref[d, 0:64, :HEAD] * jnp.asarray(0.125, bf16)
        q_s[rows, :] = jnp.concatenate([zero, q], axis=1)
        grad = unfold(do_ref[d])
        do_s[rows, :] = jnp.concatenate([grad, zero], axis=1)
        for ref, start in ((own_ref, at), (oth_ref, at + TILE)):
            vk_s[start : start + HALF, :] = jnp.concatenate(
                [unfold(ref[d, 64:96, :]), ref[d, 0:64, HEAD:]], axis=1
            )
    for j in range(8):
        keys = slice(j * CHUNK, (j + 1) * CHUNK)
        kt_s[:, keys] = vk_s[keys, :].T[HEAD:, :]
    for t in range(8):
        both = []
        for i in range(4):
            d = sc_ref[t * 4 + i]
            both.append(unfold(do_ref[d].astype(f32) * o_ref[d].astype(f32)))
        inner_s[t : t + 1, :] = jnp.sum(jnp.concatenate(both, axis=0).T, axis=0, keepdims=True)
    prompt, cont = pair_masks(core, True)
    started = set()
    for t in range(8):
        tile = slice(t * TILE, (t + 1) * TILE)
        q = q_s[tile, :]
        grad = do_s[tile, :]
        lse = lse_ref[t : t + 1, :]
        inner = inner_s[t : t + 1, :]
        dq = None
        for j, mask in chunks_of(t, prompt, cont):
            keys = slice(j * CHUNK, (j + 1) * CHUNK)
            vk = vk_s[keys, :]
            s = lax.dot_general(vk, q, NT, preferred_element_type=f32)
            a = jnp.exp(s - lse)
            if mask is not None:
                a = jnp.where(mask, a, 0.0)
            dp = lax.dot_general(vk, grad, NT, preferred_element_type=f32)
            ds = (a * (dp - inner)).astype(bf16)
            part = jnp.dot(a.astype(bf16), grad, preferred_element_type=f32) + jnp.dot(
                ds, q, preferred_element_type=f32
            )
            if j in started:
                acc_s[keys, :] += part
            else:
                acc_s[keys, :] = part
                started.add(j)
            dq_part = jnp.dot(kt_s[:, keys], ds, preferred_element_type=f32)
            dq = dq_part if dq is None else dq + dq_part
        dq_ref[tile, :] = (dq * 0.125).T.astype(bf16)
    for j in range(8):
        keep_ref[j * TILE : (j + 1) * TILE, :] = acc_s[j * CHUNK : j * CHUNK + TILE, :]
        send_ref[j * TILE : (j + 1) * TILE, :] = acc_s[
            j * CHUNK + TILE : (j + 1) * CHUNK, :
        ].astype(bf16)


def pack_grads_kernel(sc_ref, dq_ref, keep_ref, recv_ref, out_ref):
    for p in range(SUBS):
        rows = slice(p * HALF, (p + 1) * HALF)
        summed = (keep_ref[rows, :] + recv_ref[rows, :].astype(f32)).astype(bf16)
        d = sc_ref[p]
        out_ref[d, 0:64, :] = jnp.concatenate([dq_ref[rows, :], summed[:, HEAD:]], axis=1)
        out_ref[d, 64:96, :] = fold(summed[:, :HEAD])


def out_kernel(core_ref, recv_ref, own_w, oth_w, own_ref, oth_ref, part_ref):
    core = core_ref[0]
    for half, ref in ((core, own_ref), (1 - core, oth_ref)):
        for g in range(GROUPS):
            heads = [unfold(recv_ref[g * 8 + half * 4 + h]) for h in range(4)]
            ref[g * HALF : (g + 1) * HALF, :] = jnp.concatenate(heads, axis=1)
    part = jnp.dot(own_ref[...], own_w[...], preferred_element_type=f32) + jnp.dot(
        oth_ref[...], oth_w[...], preferred_element_type=f32
    )
    part_ref[...] = part.astype(bf16)


def head_grads_kernel(core_ref, grad_ref, own_w, oth_w, send_ref):
    core = core_ref[0]
    for half, w_ref in ((core, own_w), (1 - core, oth_w)):
        made = lax.dot_general(grad_ref[...], w_ref[...], NT, preferred_element_type=f32)
        for g in range(GROUPS):
            for h in range(4):
                block = made[g * HALF : (g + 1) * HALF, h * HEAD : (h + 1) * HEAD]
                send_ref[g * 8 + half * 4 + h] = fold(block).astype(bf16)


def token_grads_kernel(core_ref, recv_ref, own_w, oth_w, own_ref, oth_ref, part_ref):
    core = core_ref[0]
    part = None
    for half, w_ref, ref in ((core, own_w, own_ref), (1 - core, oth_w, oth_ref)):
        for g in range(GROUPS):
            rows = slice(g * HALF, (g + 1) * HALF)
            blocks = [recv_ref.at[g * 8 + half * 4 + h] for h in range(4)]
            pieces = (
                [b[0:64, :HEAD] for b in blocks]
                + [b[0:64, HEAD:] for b in blocks]
                + [unfold(b[64:96, :]) for b in blocks]
            )
            ref[rows, :] = jnp.concatenate(pieces, axis=1)
        made = lax.dot_general(ref[...], w_ref[...], NT, preferred_element_type=f32)
        part = made if part is None else part + made
    part_ref[...] = part.astype(bf16)


def per_device(
    tokens,
    sub_blocks,
    w_qkv,
    qv_bias,
    w_out,
    w_up,
    up_bias,
    w_down,
    ln_gains,
    row_biases,
    cotangent,
):
    width = tokens.shape[1]
    ctx = lax.axis_index("ctx").astype(jnp.int32)
    core = (lax.axis_index("tp") % 2).astype(jnp.int32)
    core_s = core.reshape(1)

    def swap(x):
        return lax.ppermute(x, "tp", CORE_SWAP)

    def across(x):
        return lax.ppermute(x, "tp", YHI_SWAP)

    def exchange(x):
        return lax.all_to_all(x, "ctx", 0, 0, tiled=True)

    def halves(whole):
        shaped = whole.reshape((GROUPS, 2, HALF) + whole.shape[1:])
        own = lax.dynamic_index_in_dim(shaped, core, 1, False)
        oth = lax.dynamic_index_in_dim(shaped, 1 - core, 1, False)
        return own.reshape((ROWS, -1)), oth.reshape((ROWS, -1))

    def join(own, oth):
        own = own.reshape(GROUPS, 1, HALF, -1)
        oth = oth.reshape(GROUPS, 1, HALF, -1)
        low = jnp.where(core == 0, own, oth)
        high = jnp.where(core == 0, oth, own)
        return jnp.concatenate([low, high], axis=1).reshape(2 * ROWS, -1)

    own_row = lax.dynamic_index_in_dim(sub_blocks, ctx // 8, 0, False)
    order = jnp.arange(SUBS, dtype=jnp.int32)
    holder = jnp.sum(
        jnp.where(own_row[:, None] == order[None, :], order[:, None], 0), axis=0
    ).astype(jnp.int32)
    scalars = jnp.concatenate([holder, core_s])

    gains = ln_gains.astype(f32)
    shifts = row_biases.astype(f32)
    w_own = w_qkv.reshape(width, 3 * LOCAL)
    w_oth = swap(w_own)
    b_oth = swap(qv_bias)
    wo_own = w_out
    wo_oth = swap(w_out)

    send, normed_own = kernel_call(
        project_kernel,
        [((SUBS, 96, 128), bf16), ((ROWS, width), bf16)],
        ins=7,
        flops=2 * ROWS * width * 6 * LOCAL,
        name="project",
    )(core_s, tokens.reshape(GROUPS, 2, HALF, width), w_own, w_oth, ln_gains, row_biases, qv_bias, b_oth)
    mine = exchange(send)
    theirs = swap(mine)

    mixed, lse = kernel_call(
        attend_kernel,
        [((SUBS, 32, 128), bf16), ((8, TILE), f32)],
        [((2048, HEAD), bf16), ((4096, HEAD), bf16), ((4096, 128), bf16)],
        ins=2,
        flops=10**9,
        name="attend",
    )(scalars, mine, theirs)
    mixed_back = exchange(mixed)
    heads_own, heads_oth, attn_part = kernel_call(
        out_kernel,
        [((ROWS, LOCAL), bf16), ((ROWS, LOCAL), bf16), ((ROWS, width), bf16)],
        ins=3,
        flops=2 * ROWS * width * 2 * LOCAL,
        name="project_out",
    )(core_s, mixed_back, wo_own, wo_oth)
    attn_sum = attn_part.astype(f32) + across(attn_part).astype(f32)

    x_own, x_oth = halves(tokens)
    cot_own, cot_oth = halves(cotangent)
    cot_rows = jnp.concatenate([cot_own, cot_oth], axis=0)
    inputs = x_own.astype(f32)
    attn_branch = attn_sum + shifts[1]
    residual = inputs + attn_branch
    unit_two, inverse_two = norm_parts(residual)
    normed_two_own = (unit_two * gains[1] + shifts[2]).astype(bf16)
    normed_two = jnp.concatenate([normed_two_own, swap(normed_two_own)], axis=0)

    hidden = jnp.dot(normed_two, w_up, preferred_element_type=f32) + up_bias.astype(f32)
    active, gelu_back = jax.vjp(partial(jax.nn.gelu, approximate=False), hidden)
    active_low = active.astype(bf16)
    grad_active = lax.dot_general(cot_rows, w_down, NT, preferred_element_type=f32)
    grad_hidden = gelu_back(grad_active)[0].astype(bf16)
    gn_two_part = lax.dot_general(grad_hidden, w_up, NT, preferred_element_type=f32).astype(bf16)
    gn_two_chip = (
        gn_two_part[:ROWS].astype(f32) + swap(gn_two_part[ROWS:]).astype(f32)
    ).astype(bf16)
    gn_two_chip = lax.optimization_barrier(gn_two_chip)
    grad_normed_two = gn_two_chip.astype(f32) + across(gn_two_chip).astype(f32)

    grad_rows_out = cot_own.astype(f32)
    grad_residual = grad_rows_out + norm_back(grad_normed_two, unit_two, inverse_two, gains[1])
    grad_attn = grad_residual.astype(bf16)
    (grad_heads,) = kernel_call(
        head_grads_kernel,
        [((SUBS, 32, 128), bf16)],
        ins=3,
        flops=2 * ROWS * width * 2 * LOCAL,
        name="head_grads",
    )(core_s, grad_attn, wo_own, wo_oth)
    grad_mixed = exchange(grad_heads)

    mlp_part = jnp.dot(active_low, w_down, preferred_element_type=f32).astype(bf16)
    mlp_chip = (mlp_part[:ROWS].astype(f32) + swap(mlp_part[ROWS:]).astype(f32)).astype(bf16)
    mlp_chip = lax.optimization_barrier(mlp_chip)
    mlp_branch = mlp_chip.astype(f32) + across(mlp_chip).astype(f32) + shifts[3]
    layer_own = residual + mlp_branch
    layer_out = join(layer_own, swap(layer_own))
    rms_own = jnp.stack(
        [
            jnp.sqrt(jnp.mean(member * member, axis=-1) + RMS_EPSILON)
            for member in (layer_own, attn_branch, mlp_branch)
        ]
    )
    rms_oth = swap(rms_own)
    rms_pair = jnp.stack([rms_own.reshape(3, GROUPS, HALF), rms_oth.reshape(3, GROUPS, HALF)], axis=2)
    rms_rows = jnp.where(core == 0, rms_pair, rms_pair[:, :, ::-1]).reshape(3, 2 * ROWS)

    def owner_sum(grad):
        moved = exchange(grad.astype(bf16)).reshape(SUBS, width // SUBS, -1)
        return jnp.sum(moved.astype(f32), axis=0)

    grad_up = owner_sum(lax.dot_general(normed_two, grad_hidden, TN, preferred_element_type=f32))
    grad_down = owner_sum(lax.dot_general(cot_rows, active_low, TN, preferred_element_type=f32)).T
    grad_attn_rows = jnp.concatenate([grad_attn, swap(grad_attn)], axis=0)
    head_rows = jnp.concatenate([heads_own, swap(heads_oth)], axis=0)
    grad_out = owner_sum(
        lax.dot_general(grad_attn_rows, head_rows, TN, preferred_element_type=f32)
    ).T
    grad_up_bias = jnp.sum(grad_hidden.astype(f32), axis=0)

    dq, kept, given = kernel_call(
        attend_back_kernel,
        [((2048, HEAD), bf16), ((2048, 128), f32), ((2048, 128), bf16)],
        [
            ((2048, 128), bf16),
            ((2048, 128), bf16),
            ((4096, 128), bf16),
            ((HEAD, 4096), bf16),
            ((8, TILE), f32),
            ((4096, 128), f32),
        ],
        ins=5,
        flops=3 * 10**9,
        name="attend_back",
    )(scalars, mine, theirs, grad_mixed, mixed, lse)
    (packed,) = kernel_call(
        pack_grads_kernel, [((SUBS, 96, 128), bf16)], ins=3, flops=10**6, name="pack_grads"
    )(scalars, dq, kept, swap(given))
    grads_back = exchange(packed)
    rows_own, rows_oth, gn_one_part = kernel_call(
        token_grads_kernel,
        [((ROWS, 3 * LOCAL), bf16), ((ROWS, 3 * LOCAL), bf16), ((ROWS, width), bf16)],
        ins=3,
        flops=2 * ROWS * width * 6 * LOCAL,
        name="token_grads",
    )(core_s, grads_back, w_own, w_oth)
    grad_normed_one = gn_one_part.astype(f32) + across(gn_one_part).astype(f32)
    unit_one, inverse_one = norm_parts(inputs)
    input_own = grad_residual + norm_back(grad_normed_one, unit_one, inverse_one, gains[0])
    input_grad = join(input_own, swap(input_own))

    unit_oth, _ = norm_parts(x_oth.astype(f32))
    normed_oth = (unit_oth * gains[0] + shifts[0]).astype(bf16)
    normed_rows = jnp.concatenate([normed_own, normed_oth], axis=0)
    grad_rows = jnp.concatenate([rows_own, swap(rows_oth)], axis=0)
    grad_qkv = owner_sum(
        lax.dot_general(normed_rows, grad_rows, TN, preferred_element_type=f32)
    ).reshape(width // SUBS, 3, LOCAL)
    row_sums = jnp.sum(grad_rows.astype(f32), axis=0).reshape(3, LOCAL)

    vectors = jnp.stack(
        [
            jnp.sum(grad_normed_one * unit_one, axis=0),
            jnp.sum(grad_normed_two * unit_two, axis=0),
            jnp.sum(grad_normed_one, axis=0),
            jnp.sum(grad_attn.astype(f32), axis=0),
            jnp.sum(grad_normed_two, axis=0),
            jnp.sum(grad_rows_out, axis=0),
        ]
    )

    def by_owner(rows):
        return rows.reshape(rows.shape[0], SUBS, -1).transpose(1, 0, 2).reshape(SUBS, -1)

    small = jnp.concatenate(
        [
            by_owner(vectors),
            by_owner(grad_up_bias[None]),
            by_owner(jnp.stack([row_sums[0], row_sums[2]])),
            jnp.zeros((SUBS, 16), f32),
        ],
        axis=1,
    )
    small = jnp.sum(exchange(small), axis=0)
    vector_sums = (small[:192] + swap(small[:192])).reshape(6, 32)
    return (
        layer_out,
        input_grad,
        rms_rows,
        grad_qkv,
        small[224:240].reshape(2, 8),
        grad_out,
        grad_up,
        small[192:224],
        grad_down,
        vector_sums[:2],
        vector_sums[2:],
    )


def solution(mesh):
    return jax.shard_map(
        per_device,
        mesh=mesh,
        in_specs=(
            P("ctx", None),
            P(),
            P(None, None, "tp"),
            P(None, "tp"),
            P("tp", None),
            P(None, "tp"),
            P("tp"),
            P("tp", None),
            P(),
            P(),
            P("ctx", None),
        ),
        out_specs=(
            P("ctx", None),
            P("ctx", None),
            P(None, "ctx"),
            P("ctx", None, "tp"),
            P(None, ("tp", "ctx")),
            P("tp", "ctx"),
            P("ctx", "tp"),
            P(("tp", "ctx")),
            P("tp", "ctx"),
            P(None, "ctx"),
            P(None, "ctx"),
        ),
        check_vma=False,
    )
```

```python
from functools import partial

import jax
import jax.numpy as jnp
from jax import lax
from jax.experimental import pallas as pl
from jax.experimental.pallas import tpu as pltpu
from jax.sharding import PartitionSpec as P

HEAD = 64
SUBS = 32
HALF = 64
GROUPS = 4
ROWS = GROUPS * HALF
LOCAL = 256
TILE = 256
CHUNK = 512
EPSILON = 1e-05
RMS_EPSILON = 1e-06
LOG_SHRINK = 10 * 0.6931471805599453
SHRINK = 2.0**-10
CORE_SWAP = [(0, 1), (1, 0), (2, 3), (3, 2)]
YHI_SWAP = [(0, 2), (2, 0), (1, 3), (3, 1)]
CROSS_SWAP = [(0, 3), (3, 0), (1, 2), (2, 1)]
YLO_SWAP = [(j, j ^ 4) for j in range(SUBS)]
PLANES = [[z * 8 + y * 4 + x for z in range(4) for x in range(4)] for y in range(2)]
NT = (((1,), (1,)), ((), ()))
TN = (((0,), (0,)), ((), ()))
bf16 = jnp.bfloat16
f32 = jnp.float32


def norm_parts(values):
    centre = jnp.mean(values, axis=-1, keepdims=True)
    centred = values - centre
    spread = jnp.mean(centred * centred, axis=-1, keepdims=True)
    inverse = lax.rsqrt(spread + EPSILON)
    return centred * inverse, inverse


def norm_back(grad_normed, unit_rows, inverse, gain):
    grad_unit = grad_normed * gain
    first_mean = jnp.mean(grad_unit, axis=-1, keepdims=True)
    second_mean = jnp.mean(grad_unit * unit_rows, axis=-1, keepdims=True)
    return inverse * (grad_unit - first_mean - unit_rows * second_mean)


def kernel_call(body, outs, scratch=(), scalars=1, ins=1, flops=0, name=None):
    smem = pl.BlockSpec(memory_space=pltpu.SMEM)
    vmem = pl.BlockSpec(memory_space=pltpu.VMEM)
    return pl.pallas_call(
        body,
        out_shape=[jax.ShapeDtypeStruct(s, d) for s, d in outs],
        in_specs=[smem] * scalars + [vmem] * ins,
        out_specs=[vmem] * len(outs),
        scratch_shapes=[pltpu.VMEM(s, d) for s, d in scratch],
        compiler_params=pltpu.CompilerParams(vmem_limit_bytes=40 * 2**20),
        cost_estimate=pl.CostEstimate(flops=flops, bytes_accessed=4 * 2**20, transcendentals=0),
        name=name,
    )


def fold(rows):
    return jnp.concatenate([rows[:32], rows[32:]], axis=1)


def unfold(packed):
    return jnp.concatenate([packed[:, :HEAD], packed[:, HEAD:]], axis=0)


def project_own_kernel(core_ref, x_ref, w_ref, gains, shifts, b_ref, send_ref, low_ref):
    x = x_ref[:, core_ref[0]].reshape(ROWS, -1).astype(f32)
    unit, _ = norm_parts(x)
    low = (unit * gains[0:1].astype(f32) + shifts[0:1].astype(f32)).astype(bf16)
    low_ref[...] = low
    for g, h, qk, v in projected(low, w_ref, b_ref):
        send_ref[g * 4 + h, 0:64, :] = qk
        send_ref[g * 4 + h, 64:96, :] = v


def project_oth_kernel(core_ref, low_ref, w_ref, b_ref, first_ref, send_ref):
    core = core_ref[0]
    for g in range(GROUPS):
        for h in range(4):
            send_ref[g * 8 + core * 4 + h] = first_ref[g * 4 + h]
    for g, h, qk, v in projected(low_ref[...], w_ref, b_ref):
        block = g * 8 + (1 - core) * 4 + h
        send_ref[block, 0:64, :] = qk
        send_ref[block, 64:96, :] = v


def projected(low, w_ref, b_ref):
    q = jnp.dot(low, w_ref[0], preferred_element_type=f32) + b_ref[0:1].astype(f32)
    k = jnp.dot(low, w_ref[1], preferred_element_type=f32)
    v = jnp.dot(low, w_ref[2], preferred_element_type=f32) + b_ref[1:2].astype(f32)
    for g in range(GROUPS):
        for h in range(4):
            rows = slice(g * HALF, (g + 1) * HALF)
            cols = slice(h * HEAD, (h + 1) * HEAD)
            qk = jnp.concatenate([q[rows, cols], k[rows, cols]], axis=1)
            yield g, h, qk.astype(bf16), fold(v[rows, cols]).astype(bf16)


def pair_masks(core, transposed):
    shape = (CHUNK, TILE) if transposed else (TILE, CHUNK)
    q = lax.broadcasted_iota(jnp.int32, shape, 1 if transposed else 0)
    key = lax.broadcasted_iota(jnp.int32, shape, 0 if transposed else 1)
    other = key >= TILE
    k = jnp.where(other, key - TILE, key)
    q_sub = lax.shift_right_logical(q, 6)
    k_sub = lax.shift_right_logical(k, 6)
    prompt = (other & (q_sub + core > k_sub)) | (jnp.logical_not(other) & (q >= k))
    cont = prompt & (lax.shift_right_logical(q, 7) == lax.shift_right_logical(k, 7))
    return prompt, cont


def chunks_of(tile, prompt, cont):
    if tile < 4:
        return [(j, None) for j in range(tile)] + [(tile, prompt)]
    return [(j, None) for j in range(4)] + [(tile, cont)]


def attend_kernel(sc_ref, own_ref, oth_ref, out_ref, lse_ref, q_s, k_s, v_s):
    core = sc_ref[SUBS]
    const = jnp.full((HALF, HEAD), SHRINK, bf16)
    for p in range(SUBS):
        d = sc_ref[p]
        at = p // 4 * CHUNK + p % 4 * HALF
        q_s[p * HALF : (p + 1) * HALF, :] = own_ref[d, 0:64, :HEAD] * jnp.asarray(0.125, bf16)
        for ref, start in ((own_ref, at), (oth_ref, at + TILE)):
            k_s[start : start + HALF, :] = ref[d, 0:64, HEAD:]
            v = unfold(ref[d, 64:96, :]) * jnp.asarray(SHRINK, bf16)
            v_s[start : start + HALF, :] = jnp.concatenate([v, const], axis=1)
    prompt, cont = pair_masks(core, False)
    for t in range(8):
        q = q_s[t * TILE : (t + 1) * TILE, :]
        total = None
        for j, mask in chunks_of(t, prompt, cont):
            keys = slice(j * CHUNK, (j + 1) * CHUNK)
            s = lax.dot_general(q, k_s[keys, :], NT, preferred_element_type=f32)
            w = jnp.exp(s)
            if mask is not None:
                w = jnp.where(mask, w, 0.0)
            part = jnp.dot(w.astype(bf16), v_s[keys, :], preferred_element_type=f32)
            total = part if total is None else total + part
        mixed = total[:, :HEAD] / total[:, HEAD:]
        lse_ref[t : t + 1, :] = jnp.log(total.T[HEAD : HEAD + 1, :]) + LOG_SHRINK
        for i in range(4):
            out_ref[sc_ref[t * 4 + i]] = fold(mixed[i * HALF : (i + 1) * HALF]).astype(bf16)


def attend_back_kernel(
    sc_ref, own_ref, oth_ref, do_ref, o_ref, lse_ref,
    dq_ref, keep_ref, send_ref,
    q_s, do_s, vk_s, kt_s, inner_s, acc_s,
):
    core = sc_ref[SUBS]
    zero = jnp.zeros((HALF, HEAD), bf16)
    for p in range(SUBS):
        d = sc_ref[p]
        at = p // 4 * CHUNK + p % 4 * HALF
        rows = slice(p * HALF, (p + 1) * HALF)
        q = own_ref[d, 0:64, :HEAD] * jnp.asarray(0.125, bf16)
        q_s[rows, :] = jnp.concatenate([zero, q], axis=1)
        grad = unfold(do_ref[d])
        do_s[rows, :] = jnp.concatenate([grad, zero], axis=1)
        for ref, start in ((own_ref, at), (oth_ref, at + TILE)):
            vk_s[start : start + HALF, :] = jnp.concatenate(
                [unfold(ref[d, 64:96, :]), ref[d, 0:64, HEAD:]], axis=1
            )
    for j in range(8):
        keys = slice(j * CHUNK, (j + 1) * CHUNK)
        kt_s[:, keys] = vk_s[keys, :].T[HEAD:, :]
    for t in range(8):
        both = []
        for i in range(4):
            d = sc_ref[t * 4 + i]
            both.append(unfold(do_ref[d].astype(f32) * o_ref[d].astype(f32)))
        inner_s[t : t + 1, :] = jnp.sum(jnp.concatenate(both, axis=0).T, axis=0, keepdims=True)
    prompt, cont = pair_masks(core, True)
    started = set()
    for t in range(8):
        tile = slice(t * TILE, (t + 1) * TILE)
        q = q_s[tile, :]
        grad = do_s[tile, :]
        lse = lse_ref[t : t + 1, :]
        inner = inner_s[t : t + 1, :]
        dq = None
        for j, mask in chunks_of(t, prompt, cont):
            keys = slice(j * CHUNK, (j + 1) * CHUNK)
            vk = vk_s[keys, :]
            s = lax.dot_general(vk, q, NT, preferred_element_type=f32)
            a = jnp.exp(s - lse)
            if mask is not None:
                a = jnp.where(mask, a, 0.0)
            dp = lax.dot_general(vk, grad, NT, preferred_element_type=f32)
            ds = (a * (dp - inner)).astype(bf16)
            part = jnp.dot(a.astype(bf16), grad, preferred_element_type=f32) + jnp.dot(
                ds, q, preferred_element_type=f32
            )
            if j in started:
                acc_s[keys, :] += part
            else:
                acc_s[keys, :] = part
                started.add(j)
            dq_part = jnp.dot(kt_s[:, keys], ds, preferred_element_type=f32)
            dq = dq_part if dq is None else dq + dq_part
        dq_ref[tile, :] = (dq * 0.125).T.astype(bf16)
    for j in range(8):
        keep_ref[j * TILE : (j + 1) * TILE, :] = acc_s[j * CHUNK : j * CHUNK + TILE, :]
        send_ref[j * TILE : (j + 1) * TILE, :] = acc_s[
            j * CHUNK + TILE : (j + 1) * CHUNK, :
        ].astype(bf16)


def pack_grads_kernel(sc_ref, dq_ref, keep_ref, recv_ref, out_ref):
    for p in range(SUBS):
        rows = slice(p * HALF, (p + 1) * HALF)
        summed = (keep_ref[rows, :] + recv_ref[rows, :].astype(f32)).astype(bf16)
        d = sc_ref[p]
        out_ref[d, 0:64, :] = jnp.concatenate([dq_ref[rows, :], summed[:, HEAD:]], axis=1)
        out_ref[d, 64:96, :] = fold(summed[:, :HEAD])


def out_kernel(core_ref, recv_ref, own_w, oth_w, own_ref, oth_ref, part_ref):
    core = core_ref[0]
    for half, ref in ((core, own_ref), (1 - core, oth_ref)):
        for g in range(GROUPS):
            heads = [unfold(recv_ref[g * 8 + half * 4 + h]) for h in range(4)]
            ref[g * HALF : (g + 1) * HALF, :] = jnp.concatenate(heads, axis=1)
    part = jnp.dot(own_ref[...], own_w[...], preferred_element_type=f32) + jnp.dot(
        oth_ref[...], oth_w[...], preferred_element_type=f32
    )
    part_ref[...] = part.astype(bf16)


def second_norm_kernel(core_ref, part_ref, recv_ref, x_ref, gains, shifts, residual_ref, low_ref):
    x = x_ref[:, core_ref[0]].reshape(ROWS, -1).astype(f32)
    branch = (part_ref[...].astype(f32) + recv_ref[...].astype(f32)) + shifts[1:2].astype(f32)
    residual = x + branch
    residual_ref[...] = residual
    unit, _ = norm_parts(residual)
    low_ref[...] = (unit * gains[1:2].astype(f32) + shifts[2:3].astype(f32)).astype(bf16)


def feed_kernel(rows_ref, cot_ref, up_ref, bias_ref, down_ref, active_ref, grad_ref, back_ref):
    total = None
    for c in range(4):
        cols = slice(c * 256, (c + 1) * 256)
        up = up_ref[:, cols]
        hidden = jnp.dot(rows_ref[...], up, preferred_element_type=f32) + bias_ref[
            0:1, cols
        ].astype(f32)
        grad_active = lax.dot_general(
            cot_ref[...], down_ref[cols, :], NT, preferred_element_type=f32
        )
        share = 0.5 + 0.5 * lax.erf(hidden * 0.7071067811865476)
        density = jnp.exp(hidden * hidden * -0.5) * 0.3989422804014327
        active_ref[:, cols] = (hidden * share).astype(bf16)
        grad = (grad_active * (share + hidden * density)).astype(bf16)
        grad_ref[:, cols] = grad
        part = lax.dot_general(grad, up, NT, preferred_element_type=f32)
        total = part if total is None else total + part
    back_ref[...] = total.astype(back_ref.dtype)


def residual_grads_kernel(
    core_ref, own_ref, recv_ref, residual_ref, cot_ref, gains, own_w, oth_w,
    grad_ref, low_ref, send_ref, sums_ref,
):
    core = core_ref[0]
    unit, inverse = norm_parts(residual_ref[...])
    grad_normed = own_ref[...].astype(f32) + recv_ref[...].astype(f32)
    cot = cot_ref[...].astype(f32)
    grad = cot + norm_back(grad_normed, unit, inverse, gains[1:2].astype(f32))
    grad_ref[...] = grad
    low = grad.astype(bf16)
    low_ref[...] = low
    for half, w_ref in ((core, own_w), (1 - core, oth_w)):
        made = lax.dot_general(low, w_ref[...], NT, preferred_element_type=f32)
        for g in range(GROUPS):
            for h in range(4):
                block = made[g * HALF : (g + 1) * HALF, h * HEAD : (h + 1) * HEAD]
                send_ref[g * 8 + half * 4 + h] = fold(block).astype(bf16)
    sums = [grad_normed * unit, low.astype(f32), grad_normed, cot]
    for i, rows in enumerate(sums):
        sums_ref[i : i + 1, :] = 0.5 * jnp.sum(rows, axis=0, keepdims=True)


def token_grads_kernel(core_ref, recv_ref, own_w, oth_w, own_ref, oth_ref, part_ref):
    core = core_ref[0]
    part = None
    for half, w_ref, ref in ((core, own_w, own_ref), (1 - core, oth_w, oth_ref)):
        for g in range(GROUPS):
            rows = slice(g * HALF, (g + 1) * HALF)
            blocks = [recv_ref.at[g * 8 + half * 4 + h] for h in range(4)]
            pieces = (
                [b[0:64, :HEAD] for b in blocks]
                + [b[0:64, HEAD:] for b in blocks]
                + [unfold(b[64:96, :]) for b in blocks]
            )
            ref[rows, :] = jnp.concatenate(pieces, axis=1)
        for i in range(3):
            made = lax.dot_general(
                ref[:, i * LOCAL : (i + 1) * LOCAL], w_ref[i], NT, preferred_element_type=f32
            )
            part = made if part is None else part + made
    part_ref[...] = part.astype(bf16)


def first_sums_kernel(core_ref, part_ref, x_ref, sums_ref):
    x = x_ref[:, core_ref[0]].reshape(ROWS, -1).astype(f32)
    unit, _ = norm_parts(x)
    part = part_ref[...].astype(f32)
    sums_ref[0:1, :] = jnp.sum(part * unit, axis=0, keepdims=True)
    sums_ref[1:2, :] = jnp.sum(part, axis=0, keepdims=True)


def input_grads_kernel(core_ref, part_ref, recv_ref, grad_ref, x_ref, gains, out_ref):
    x = x_ref[:, core_ref[0]].reshape(ROWS, -1).astype(f32)
    unit, inverse = norm_parts(x)
    grad_normed = part_ref[...].astype(f32) + recv_ref[...].astype(f32)
    out_ref[...] = grad_ref[...] + norm_back(grad_normed, unit, inverse, gains[0:1].astype(f32))


def join_kernel(core_ref, own_ref, oth_ref, out_ref, sems):
    core = core_ref[0]
    copies = []
    for g in range(GROUPS):
        rows = pl.ds(g * HALF, HALF)
        for i, (ref, half) in enumerate(((own_ref, core), (oth_ref, 1 - core))):
            copies.append(
                pltpu.make_async_copy(ref.at[rows], out_ref.at[g, half], sems.at[2 * g + i])
            )
    for copy in copies:
        copy.start()
    for copy in copies:
        copy.wait()


def join_rows(core_s, own, oth):
    width = own.shape[1]
    hbm = pl.BlockSpec(memory_space=pl.ANY)
    joined = pl.pallas_call(
        join_kernel,
        out_shape=jax.ShapeDtypeStruct((GROUPS, 2, HALF, width), own.dtype),
        in_specs=[pl.BlockSpec(memory_space=pltpu.SMEM), hbm, hbm],
        out_specs=hbm,
        scratch_shapes=[pltpu.SemaphoreType.DMA((2 * GROUPS,))],
        name="join_rows",
    )(core_s, own, oth)
    return joined.reshape(2 * ROWS, width)


def weight_grads_kernel(pairs, columns, *refs):
    out_ref = refs[-1]
    start = 0
    for i in range(pairs):
        a_own, a_oth, b_own, b_oth = refs[4 * i : 4 * i + 4]
        made = lax.dot_general(a_own[...], b_own[...], TN, preferred_element_type=f32)
        made += lax.dot_general(a_oth[...], b_oth[...], TN, preferred_element_type=f32)
        made = made.astype(bf16)
        stop = start + made.shape[1]
        if columns:
            out_ref[:, start:stop] = made
        else:
            for x in range(4):
                out_ref[0, x, 0, :, start:stop] = made[x * 32 : (x + 1) * 32]
        start = stop
    if columns:
        rows = refs[4 * pairs][...]
        rows = jnp.concatenate([rows, jnp.zeros((128 - rows.shape[0], 128), f32)], axis=0)
        out_ref[:, start:] = rows.T.astype(bf16)


def weight_grads(pairs, vectors=None):
    width = pairs[0][0].shape[1]
    steps = width // 128
    columns = sum(p[2].shape[1] for p in pairs)
    args, specs = [], []
    for a_own, a_oth, b_own, b_oth in pairs:
        args += [a_own, a_oth, b_own, b_oth]
        specs += [pl.BlockSpec((ROWS, 128), lambda m: (0, m))] * 2
        specs += [pl.BlockSpec(b_own.shape, lambda m: (0, 0))] * 2
    if vectors is None:
        shape = (4, 4, 2, 32, columns)
        out = pl.BlockSpec((1, 4, 1, 32, columns), lambda m: (m // 2, 0, m % 2, 0, 0))
    else:
        args.append(vectors)
        specs.append(pl.BlockSpec((vectors.shape[0], 128), lambda m: (0, m)))
        shape = (width, columns + 128)
        out = pl.BlockSpec((128, columns + 128), lambda m: (m, 0))
    return pl.pallas_call(
        partial(weight_grads_kernel, len(pairs), vectors is not None),
        grid=(steps,),
        out_shape=jax.ShapeDtypeStruct(shape, bf16),
        in_specs=specs,
        out_specs=out,
        compiler_params=pltpu.CompilerParams(vmem_limit_bytes=32 * 2**20),
        cost_estimate=pl.CostEstimate(
            flops=4 * ROWS * width * columns, bytes_accessed=4 * 2**20, transcendentals=0
        ),
        name="weight_grads",
    )(*args)


def per_device(
    tokens,
    sub_blocks,
    w_qkv,
    qv_bias,
    w_out,
    w_up,
    up_bias,
    w_down,
    ln_gains,
    row_biases,
    cotangent,
):
    width = tokens.shape[1]
    ctx = lax.axis_index("ctx").astype(jnp.int32)
    core = (lax.axis_index("tp") % 2).astype(jnp.int32)
    y_low = ctx // 4 % 2
    core_s = core.reshape(1)

    def swap(x):
        return lax.ppermute(x, "tp", CORE_SWAP)

    def across(x):
        return lax.ppermute(x, "tp", YHI_SWAP)

    def exchange(x):
        return lax.all_to_all(x, "ctx", 0, 0, tiled=True)

    def after(x, *others):
        return lax.optimization_barrier((x,) + others)[0]

    def halves(whole):
        shaped = whole.reshape((GROUPS, 2, HALF) + whole.shape[1:])
        own = lax.dynamic_index_in_dim(shaped, core, 1, False)
        oth = lax.dynamic_index_in_dim(shaped, 1 - core, 1, False)
        return own.reshape((ROWS, -1)), oth.reshape((ROWS, -1))

    def plane_sum(blocks):
        columns = blocks.shape[-1]
        moved = lax.all_to_all(
            blocks.reshape(-1, columns), "ctx", 0, 0, axis_index_groups=PLANES, tiled=True
        )
        summed = jnp.sum(moved.reshape(16, 2, 32, columns).astype(f32), axis=0)
        own = lax.dynamic_index_in_dim(summed, y_low, 0, False)
        oth = lax.dynamic_index_in_dim(summed, 1 - y_low, 0, False).astype(bf16)
        return own + lax.ppermute(oth, "ctx", YLO_SWAP).astype(f32)

    own_row = lax.dynamic_index_in_dim(sub_blocks, ctx // 8, 0, False)
    order = jnp.arange(SUBS, dtype=jnp.int32)
    holder = jnp.sum(
        jnp.where(own_row[:, None] == order[None, :], order[:, None], 0), axis=0
    ).astype(jnp.int32)
    scalars = jnp.concatenate([holder, core_s])

    gains = ln_gains.astype(f32)
    shifts = row_biases.astype(f32)
    split_tokens = tokens.reshape(GROUPS, 2, HALF, width)
    w_own = w_qkv.transpose(1, 0, 2)
    w_oth = swap(w_own)
    b_oth = swap(qv_bias)
    wo_own = w_out
    wo_oth = swap(w_out)
    cot_own, cot_oth = halves(cotangent)

    first, normed_own = kernel_call(
        project_own_kernel,
        [((16, 96, 128), bf16), ((ROWS, width), bf16)],
        ins=5,
        flops=2 * ROWS * width * 3 * LOCAL,
        name="project_own",
    )(core_s, split_tokens, w_own, ln_gains, row_biases, qv_bias)
    (send,) = kernel_call(
        project_oth_kernel,
        [((SUBS, 96, 128), bf16)],
        ins=4,
        flops=2 * ROWS * width * 3 * LOCAL,
        name="project_oth",
    )(core_s, normed_own, w_oth, b_oth, first)
    mine = exchange(send)
    theirs = swap(mine)

    mixed, lse = kernel_call(
        attend_kernel,
        [((SUBS, 32, 128), bf16), ((8, TILE), f32)],
        [((2048, HEAD), bf16), ((4096, HEAD), bf16), ((4096, 128), bf16)],
        ins=2,
        flops=10**9,
        name="attend",
    )(scalars, mine, theirs)
    mixed_back = exchange(mixed)
    heads_own, heads_oth, attn_part = kernel_call(
        out_kernel,
        [((ROWS, LOCAL), bf16), ((ROWS, LOCAL), bf16), ((ROWS, width), bf16)],
        ins=3,
        flops=2 * ROWS * width * 2 * LOCAL,
        name="project_out",
    )(core_s, mixed_back, wo_own, wo_oth)
    attn_recv = across(attn_part)
    residual, normed_two_own = kernel_call(
        second_norm_kernel,
        [((ROWS, width), f32), ((ROWS, width), bf16)],
        ins=5,
        flops=10**6,
        name="second_norm",
    )(core_s, attn_part, attn_recv, split_tokens, ln_gains, row_biases)
    normed_two_oth = swap(normed_two_own)

    def feed(rows, cot, kind):
        return kernel_call(
            feed_kernel,
            [((ROWS, width), bf16), ((ROWS, width), bf16), ((ROWS, width), kind)],
            scalars=0,
            ins=5,
            flops=6 * ROWS * width * width,
            name="feed",
        )(rows, cot, w_up, up_bias.reshape(1, -1), w_down)

    active_own, grad_hidden_own, gn_two_own = feed(normed_two_own, cot_own, f32)
    active_oth, grad_hidden_oth, gn_two_oth = feed(normed_two_oth, cot_oth, bf16)
    gn_two_chip = (gn_two_own + swap(gn_two_oth).astype(f32)).astype(bf16)
    gn_two_chip = lax.optimization_barrier(gn_two_chip)
    gn_two_recv = across(gn_two_chip)
    up_blocks = weight_grads(
        [
            (
                after(normed_two_own, gn_two_chip),
                normed_two_oth,
                grad_hidden_own,
                grad_hidden_oth,
            )
        ]
    )
    grad_up = plane_sum(up_blocks)

    grad_residual, grad_attn, grad_heads, second_sums = kernel_call(
        residual_grads_kernel,
        [
            ((ROWS, width), f32),
            ((ROWS, width), bf16),
            ((SUBS, 32, 128), bf16),
            ((4, width), f32),
        ],
        ins=7,
        flops=2 * ROWS * width * 2 * LOCAL,
        name="residual_grads",
    )(core_s, gn_two_chip, gn_two_recv, residual, cot_own, ln_gains, wo_own, wo_oth)
    grad_mixed = exchange(grad_heads)

    active_own, active_oth, heads_own, heads_oth, grad_attn = lax.optimization_barrier(
        (active_own, active_oth, heads_own, heads_oth, grad_attn, grad_heads)
    )[:5]
    mlp_oth = jnp.dot(active_oth, w_down, preferred_element_type=f32).astype(bf16)
    mlp_own = jnp.dot(active_own, w_down, preferred_element_type=f32)
    mlp_chip = (mlp_own + swap(mlp_oth).astype(f32)).astype(bf16)
    grad_attn_oth = swap(grad_attn)
    head_rows_oth = swap(heads_oth)
    down_blocks = weight_grads(
        [
            (cot_own, cot_oth, active_own, active_oth),
            (grad_attn, grad_attn_oth, heads_own, head_rows_oth),
        ]
    )
    grad_mixed, mlp_chip, down_blocks = lax.optimization_barrier(
        (grad_mixed, mlp_chip, down_blocks)
    )
    mlp_recv = across(mlp_chip)
    grad_down_out = plane_sum(down_blocks)
    grad_down = grad_down_out[:, :width].T
    grad_out = grad_down_out[:, width:].T

    dq, kept, given = kernel_call(
        attend_back_kernel,
        [((2048, HEAD), bf16), ((2048, 128), f32), ((2048, 128), bf16)],
        [
            ((2048, 128), bf16),
            ((2048, 128), bf16),
            ((4096, 128), bf16),
            ((HEAD, 4096), bf16),
            ((8, TILE), f32),
            ((4096, 128), f32),
        ],
        ins=5,
        flops=3 * 10**9,
        name="attend_back",
    )(scalars, mine, theirs, grad_mixed, mixed, lse)
    (packed,) = kernel_call(
        pack_grads_kernel, [((SUBS, 96, 128), bf16)], ins=3, flops=10**6, name="pack_grads"
    )(scalars, dq, kept, swap(given))
    grads_back = exchange(packed)

    mlp_chip, mlp_recv = lax.optimization_barrier((mlp_chip, mlp_recv, packed))[:2]
    mlp_branch = (mlp_chip.astype(f32) + mlp_recv.astype(f32)) + shifts[3]
    attn_branch = (attn_part.astype(f32) + attn_recv.astype(f32)) + shifts[1]
    layer_own = residual + mlp_branch
    layer_out = join_rows(core_s, layer_own, swap(layer_own))
    rms_own = jnp.stack(
        [
            jnp.sqrt(jnp.mean(member * member, axis=-1) + RMS_EPSILON)
            for member in (layer_own, attn_branch, mlp_branch)
        ]
    )
    rms_oth = swap(rms_own)
    rms_own = rms_own.reshape(3, GROUPS, 1, HALF)
    rms_oth = rms_oth.reshape(3, GROUPS, 1, HALF)
    rms_rows = jnp.concatenate(
        [jnp.where(core == 0, rms_own, rms_oth), jnp.where(core == 0, rms_oth, rms_own)], axis=2
    ).reshape(3, 2 * ROWS)
    _, x_oth = halves(tokens)
    unit_oth, _ = norm_parts(x_oth.astype(f32))
    normed_oth = (unit_oth * gains[0] + shifts[0]).astype(bf16)
    up_bias_sums = jnp.sum(grad_hidden_own.astype(f32), axis=0) + jnp.sum(
        grad_hidden_oth.astype(f32), axis=0
    )

    rows_own, rows_oth, gn_one_part = kernel_call(
        token_grads_kernel,
        [((ROWS, 3 * LOCAL), bf16), ((ROWS, 3 * LOCAL), bf16), ((ROWS, width), bf16)],
        ins=3,
        flops=2 * ROWS * width * 6 * LOCAL,
        name="token_grads",
    )(core_s, grads_back, w_own, w_oth)
    gn_one_recv = across(gn_one_part)
    rows_recv = swap(rows_oth)
    (first_sums,) = kernel_call(
        first_sums_kernel, [((2, width), f32)], ins=2, flops=10**6, name="first_sums"
    )(core_s, gn_one_part, split_tokens)
    row_sums = jnp.sum(rows_own.astype(f32), axis=0) + jnp.sum(rows_recv.astype(f32), axis=0)

    def spread(row):
        return jnp.pad(row.reshape(SUBS, -1), ((0, 0), (0, 24))).reshape(1, width)

    vectors = jnp.concatenate(
        [
            first_sums,
            second_sums,
            up_bias_sums[None],
            spread(row_sums[:LOCAL]),
            spread(row_sums[2 * LOCAL :]),
            jnp.zeros((7, width), f32),
        ],
        axis=0,
    )
    qkv_blocks = weight_grads([(normed_own, normed_oth, rows_own, rows_recv)], vectors)
    moved = exchange(qkv_blocks).reshape(SUBS, 32, -1)
    summed = jnp.sum(moved.astype(f32), axis=0)
    grad_qkv = summed[:, : 3 * LOCAL].reshape(32, 3, LOCAL)
    small = summed[:, 3 * LOCAL : 3 * LOCAL + 16].T
    six = small[:6]
    six = (six + swap(six)) + (across(six) + lax.ppermute(six, "tp", CROSS_SWAP))

    (input_own,) = kernel_call(
        input_grads_kernel, [((ROWS, width), f32)], ins=5, flops=10**6, name="input_grads"
    )(core_s, gn_one_part, gn_one_recv, grad_residual, split_tokens, ln_gains)
    input_grad = join_rows(core_s, input_own, swap(input_own))
    return (
        layer_out,
        input_grad,
        rms_rows,
        grad_qkv,
        small[7:9, :8],
        grad_out,
        grad_up,
        small[6],
        grad_down,
        jnp.stack([six[0], six[2]]),
        jnp.stack([six[1], six[3], six[4], six[5]]),
    )


def solution(mesh):
    return jax.shard_map(
        per_device,
        mesh=mesh,
        in_specs=(
            P("ctx", None),
            P(),
            P(None, None, "tp"),
            P(None, "tp"),
            P("tp", None),
            P(None, "tp"),
            P("tp"),
            P("tp", None),
            P(),
            P(),
            P("ctx", None),
        ),
        out_specs=(
            P("ctx", None),
            P("ctx", None),
            P(None, "ctx"),
            P("ctx", None, "tp"),
            P(None, ("tp", "ctx")),
            P("tp", "ctx"),
            P("ctx", "tp"),
            P(("tp", "ctx")),
            P("tp", "ctx"),
            P(None, "ctx"),
            P(None, "ctx"),
        ),
        check_vma=False,
    )
```

```python
import jax
import jax.numpy as jnp
from jax import lax
from jax.experimental import pallas as pl
from jax.experimental.pallas import tpu as pltpu
from jax.sharding import PartitionSpec as P

HEAD = 64
SUBS = 32
HALF = 64
GROUPS = 4
ROWS = GROUPS * HALF
LOCAL = 256
P_ONE = 640
P_TWO = 256
LIMIT = 36
TILE = 256
CHUNK = 512
EPSILON = 1e-05
RMS_EPSILON = 1e-06
LOG_SHRINK = 10 * 0.6931471805599453
SHRINK = 2.0**-10
CORE_SWAP = [(0, 1), (1, 0), (2, 3), (3, 2)]
YHI_SWAP = [(0, 2), (2, 0), (1, 3), (3, 1)]
YLO_SWAP = [(j, j ^ 4) for j in range(SUBS)]
PLANES = [[z * 8 + y * 4 + x for z in range(4) for x in range(4)] for y in range(2)]
NT = (((1,), (1,)), ((), ()))
TN = (((0,), (0,)), ((), ()))
bf16 = jnp.bfloat16
f32 = jnp.float32


def norm_parts(values):
    centre = jnp.mean(values, axis=-1, keepdims=True)
    centred = values - centre
    spread = jnp.mean(centred * centred, axis=-1, keepdims=True)
    inverse = lax.rsqrt(spread + EPSILON)
    return centred * inverse, inverse


def norm_back(grad_normed, unit_rows, inverse, gain):
    grad_unit = grad_normed * gain
    first_mean = jnp.mean(grad_unit, axis=-1, keepdims=True)
    second_mean = jnp.mean(grad_unit * unit_rows, axis=-1, keepdims=True)
    return inverse * (grad_unit - first_mean - unit_rows * second_mean)


def hold(arrays):
    return [pltpu.with_memory_space_constraint(x, pltpu.HBM) for x in arrays]


def pieces_of(ref, stage, sems, first, pieces):
    step = ref.shape[0] // pieces
    return [
        pltpu.make_async_copy(
            ref.at[pl.ds(i * step, step)], stage.at[pl.ds(i * step, step)], sems.at[first + i]
        )
        for i in range(pieces)
    ]


def with_copies(body, n_in, n_late, n_out, stored, brought, lazy):
    def kernel(*refs):
        ins, outs = list(refs[:n_in]), list(refs[n_in + n_late : n_in + n_late + n_out])
        rest = refs[n_in + n_late + n_out :]
        arriving = {}
        if brought:
            stages, in_sems, rest = rest[: len(brought)], rest[len(brought)], rest[len(brought) + 1 :]
            first = 0
            for stage, (o, pieces) in zip(stages, brought):
                arriving[o] = pieces_of(ins[o], stage, in_sems, first, pieces)
                ins[o] = stage
                first += pieces
            for copies in arriving.values():
                for copy in copies:
                    copy.start()
        stages, rest = rest[: len(stored)], rest[len(stored) :]
        copies = []
        if stored:
            sems, rest = rest[0], rest[1:]
            copies = [
                pltpu.make_async_copy(stage, outs[o], sems.at[i])
                for i, (stage, o) in enumerate(zip(stages, stored))
            ]
        for stage, o in zip(stages, stored):
            outs[o] = stage
        leaving = dict(zip(stored, copies))
        if lazy:
            body(arriving, leaving, *ins, *outs, *rest)
        else:
            for arrivals in arriving.values():
                for copy in arrivals:
                    copy.wait()
            body(*ins, *outs, *rest)
        for copy in leaving.values():
            copy.start()
        for copy in copies:
            copy.wait()

    return kernel


def kernel_call(
    body, outs, scratch=(), scalars=1, name=None, stored=(), late=(), brought=(), lazy=False
):
    smem = pl.BlockSpec(memory_space=pltpu.SMEM)
    vmem = pl.BlockSpec(memory_space=pltpu.VMEM)
    hbm = pl.BlockSpec(memory_space=pltpu.HBM)
    shapes = [pltpu.VMEM(s, d) for s, d in scratch]
    if stored:
        shapes = (
            [pltpu.VMEM(*outs[o]) for o in stored]
            + [pltpu.SemaphoreType.DMA((len(stored),))]
            + shapes
        )

    def call(*args):
        args, more, specs = list(args), [], [smem] * scalars + [vmem] * (len(args) - scalars)
        for o, _ in brought:
            specs[o] = hbm
            more.append(pltpu.VMEM(args[o].shape, args[o].dtype))
            (args[o],) = hold([args[o]])
        if brought:
            more.append(pltpu.SemaphoreType.DMA((sum(pieces for _, pieces in brought),)))
        return pl.pallas_call(
            with_copies(body, len(args), len(late), len(outs), stored, brought, lazy),
            out_shape=[
                pltpu.HBM(s, d) if o in stored else jax.ShapeDtypeStruct(s, d)
                for o, (s, d) in enumerate(outs)
            ],
            in_specs=specs + [hbm] * len(late),
            out_specs=[hbm if o in stored else vmem for o in range(len(outs))],
            scratch_shapes=more + shapes,
            compiler_params=pltpu.CompilerParams(vmem_limit_bytes=LIMIT * 2**20),
            cost_estimate=pl.CostEstimate(flops=1, bytes_accessed=1, transcendentals=0),
            name=name,
        )(*args, *hold(late))

    return call


def held(x, *late):
    hbm = pl.BlockSpec(memory_space=pltpu.HBM)
    return pl.pallas_call(
        lambda *refs: None,
        out_shape=pltpu.HBM(x.shape, x.dtype),
        in_specs=[hbm] + [pl.BlockSpec(memory_space=pl.ANY)] * len(late),
        out_specs=hbm,
        input_output_aliases={0: 0},
        cost_estimate=pl.CostEstimate(flops=1, bytes_accessed=1, transcendentals=0),
        name="held",
    )(*hold([x]), *late)


def fold(rows):
    return jnp.concatenate([rows[:32], rows[32:]], axis=1)


def unfold(packed):
    return jnp.concatenate([packed[:, :HEAD], packed[:, HEAD:]], axis=0)


def project_own_kernel(arriving, leaving, core_ref, x_ref, w_ref, gains, shifts, b_ref, send_ref, low_ref):
    for o in (1, 3, 4, 5):
        for copy in arriving[o]:
            copy.wait()
    x = x_ref[:, core_ref[0]].reshape(ROWS, -1).astype(f32)
    unit, _ = norm_parts(x)
    low = (unit * gains[0:1].astype(f32) + shifts[0:1].astype(f32)).astype(bf16)
    low_ref[...] = low
    for w in arriving[2]:
        w.wait()
    for g, h, qk, v in projected(low, w_ref, b_ref):
        send_ref[g * 4 + h, 0:64, :] = qk
        send_ref[g * 4 + h, 64:96, :] = v


def project_oth_kernel(core_ref, low_ref, w_ref, b_ref, first_ref, send_ref):
    core = core_ref[0]
    for g in range(GROUPS):
        for h in range(4):
            send_ref[g * 8 + core * 4 + h] = first_ref[g * 4 + h]
    for g, h, qk, v in projected(low_ref[...], w_ref, b_ref):
        block = g * 8 + (1 - core) * 4 + h
        send_ref[block, 0:64, :] = qk
        send_ref[block, 64:96, :] = v


def projected(low, w_ref, b_ref):
    q = jnp.dot(low, w_ref[0], preferred_element_type=f32) + b_ref[0:1].astype(f32)
    k = jnp.dot(low, w_ref[1], preferred_element_type=f32)
    v = jnp.dot(low, w_ref[2], preferred_element_type=f32) + b_ref[1:2].astype(f32)
    for g in range(GROUPS):
        for h in range(4):
            rows = slice(g * HALF, (g + 1) * HALF)
            cols = slice(h * HEAD, (h + 1) * HEAD)
            qk = jnp.concatenate([q[rows, cols], k[rows, cols]], axis=1)
            yield g, h, qk.astype(bf16), fold(v[rows, cols]).astype(bf16)


def pair_masks(core, transposed):
    shape = (CHUNK, TILE) if transposed else (TILE, CHUNK)
    q = lax.broadcasted_iota(jnp.int32, shape, 1 if transposed else 0)
    key = lax.broadcasted_iota(jnp.int32, shape, 0 if transposed else 1)
    other = key >= TILE
    k = jnp.where(other, key - TILE, key)
    q_sub = lax.shift_right_logical(q, 6)
    k_sub = lax.shift_right_logical(k, 6)
    prompt = (other & (q_sub + core > k_sub)) | (jnp.logical_not(other) & (q >= k))
    cont = prompt & (lax.shift_right_logical(q, 7) == lax.shift_right_logical(k, 7))
    return prompt, cont


def chunks_of(tile, prompt, cont):
    if tile < 4:
        return [(j, None) for j in range(tile)] + [(tile, prompt)]
    return [(j, None) for j in range(4)] + [(tile, cont)]


def attend_kernel(sc_ref, own_ref, oth_ref, out_ref, lse_ref, q_s, k_s, v_s):
    core = sc_ref[SUBS]
    const = jnp.full((HALF, HEAD), SHRINK, bf16)
    for p in range(SUBS):
        d = sc_ref[p]
        at = p // 4 * CHUNK + p % 4 * HALF
        q_s[p * HALF : (p + 1) * HALF, :] = own_ref[d, 0:64, :HEAD] * jnp.asarray(0.125, bf16)
        for ref, start in ((own_ref, at), (oth_ref, at + TILE)):
            k_s[start : start + HALF, :] = ref[d, 0:64, HEAD:]
            v = unfold(ref[d, 64:96, :]) * jnp.asarray(SHRINK, bf16)
            v_s[start : start + HALF, :] = jnp.concatenate([v, const], axis=1)
    prompt, cont = pair_masks(core, False)
    for t in range(8):
        q = q_s[t * TILE : (t + 1) * TILE, :]
        total = None
        for j, mask in chunks_of(t, prompt, cont):
            keys = slice(j * CHUNK, (j + 1) * CHUNK)
            s = lax.dot_general(q, k_s[keys, :], NT, preferred_element_type=f32)
            w = jnp.exp(s)
            if mask is not None:
                w = jnp.where(mask, w, 0.0)
            part = jnp.dot(w.astype(bf16), v_s[keys, :], preferred_element_type=f32)
            total = part if total is None else total + part
        mixed = total[:, :HEAD] / total[:, HEAD:]
        lse_ref[t : t + 1, :] = jnp.log(total.T[HEAD : HEAD + 1, :]) + LOG_SHRINK
        for i in range(4):
            out_ref[sc_ref[t * 4 + i]] = fold(mixed[i * HALF : (i + 1) * HALF]).astype(bf16)


def attend_back_kernel(
    sc_ref, own_ref, oth_ref, do_ref, o_ref, lse_ref,
    dq_ref, keep_ref, send_ref,
    q_s, do_s, vk_s, kt_s, inner_s, acc_s,
):
    core = sc_ref[SUBS]
    zero = jnp.zeros((HALF, HEAD), bf16)
    for p in range(SUBS):
        d = sc_ref[p]
        at = p // 4 * CHUNK + p % 4 * HALF
        rows = slice(p * HALF, (p + 1) * HALF)
        q = own_ref[d, 0:64, :HEAD] * jnp.asarray(0.125, bf16)
        q_s[rows, :] = jnp.concatenate([zero, q], axis=1)
        grad = unfold(do_ref[d])
        do_s[rows, :] = jnp.concatenate([grad, zero], axis=1)
        for ref, start in ((own_ref, at), (oth_ref, at + TILE)):
            vk_s[start : start + HALF, :] = jnp.concatenate(
                [unfold(ref[d, 64:96, :]), ref[d, 0:64, HEAD:]], axis=1
            )
    for j in range(8):
        keys = slice(j * CHUNK, (j + 1) * CHUNK)
        kt_s[:, keys] = vk_s[keys, :].T[HEAD:, :]
    for t in range(8):
        both = []
        for i in range(4):
            d = sc_ref[t * 4 + i]
            both.append(unfold(do_ref[d].astype(f32) * o_ref[d].astype(f32)))
        inner_s[t : t + 1, :] = jnp.sum(jnp.concatenate(both, axis=0).T, axis=0, keepdims=True)
    prompt, cont = pair_masks(core, True)
    started = set()
    for t in range(8):
        tile = slice(t * TILE, (t + 1) * TILE)
        q = q_s[tile, :]
        grad = do_s[tile, :]
        lse = lse_ref[t : t + 1, :]
        inner = inner_s[t : t + 1, :]
        dq = None
        for j, mask in chunks_of(t, prompt, cont):
            keys = slice(j * CHUNK, (j + 1) * CHUNK)
            vk = vk_s[keys, :]
            s = lax.dot_general(vk, q, NT, preferred_element_type=f32)
            a = jnp.exp(s - lse)
            if mask is not None:
                a = jnp.where(mask, a, 0.0)
            dp = lax.dot_general(vk, grad, NT, preferred_element_type=f32)
            ds = (a * (dp - inner)).astype(bf16)
            part = jnp.dot(a.astype(bf16), grad, preferred_element_type=f32) + jnp.dot(
                ds, q, preferred_element_type=f32
            )
            if j in started:
                acc_s[keys, :] += part
            else:
                acc_s[keys, :] = part
                started.add(j)
            dq_part = jnp.dot(kt_s[:, keys], ds, preferred_element_type=f32)
            dq = dq_part if dq is None else dq + dq_part
        dq_ref[tile, :] = (dq * 0.125).T.astype(bf16)
    for j in range(8):
        keep_ref[j * TILE : (j + 1) * TILE, :] = acc_s[j * CHUNK : j * CHUNK + TILE, :]
        send_ref[j * TILE : (j + 1) * TILE, :] = acc_s[
            j * CHUNK + TILE : (j + 1) * CHUNK, :
        ].astype(bf16)


def pack_grads_kernel(sc_ref, dq_ref, keep_ref, recv_ref, out_ref):
    for p in range(SUBS):
        rows = slice(p * HALF, (p + 1) * HALF)
        summed = (keep_ref[rows, :] + recv_ref[rows, :].astype(f32)).astype(bf16)
        d = sc_ref[p]
        out_ref[d, 0:64, :] = jnp.concatenate([dq_ref[rows, :], summed[:, HEAD:]], axis=1)
        out_ref[d, 64:96, :] = fold(summed[:, :HEAD])


def out_kernel(core_ref, recv_ref, own_w, oth_w, own_ref, oth_ref, part_ref):
    core = core_ref[0]
    for half, ref in ((core, own_ref), (1 - core, oth_ref)):
        for g in range(GROUPS):
            heads = [unfold(recv_ref[g * 8 + half * 4 + h]) for h in range(4)]
            ref[g * HALF : (g + 1) * HALF, :] = jnp.concatenate(heads, axis=1)
    part = jnp.dot(own_ref[...], own_w[...], preferred_element_type=f32) + jnp.dot(
        oth_ref[...], oth_w[...], preferred_element_type=f32
    )
    part_ref[...] = part.astype(bf16)


def split_kernel(core_ref, rows_ref, own_ref, oth_ref):
    own_ref[...] = rows_ref[:, core_ref[0]].reshape(own_ref.shape)
    oth_ref[...] = rows_ref[:, 1 - core_ref[0]].reshape(oth_ref.shape)


def first_norm_kernel(core_ref, x_ref, gains, shifts, own_ref, oth_ref):
    for half, low_ref in ((core_ref[0], own_ref), (1 - core_ref[0], oth_ref)):
        unit, _ = norm_parts(x_ref[:, half].reshape(ROWS, -1).astype(f32))
        low_ref[...] = (unit * gains[0:1].astype(f32) + shifts[0:1].astype(f32)).astype(bf16)


def layer_kernel(
    residual_ref, part_ref, part_recv_ref, mlp_ref, mlp_recv_ref, shifts, layer_ref, rms_ref
):
    attn = (part_ref[...].astype(f32) + part_recv_ref[...].astype(f32)) + shifts[1:2].astype(f32)
    mlp = (mlp_ref[...].astype(f32) + mlp_recv_ref[...].astype(f32)) + shifts[3:4].astype(f32)
    layer = residual_ref[...] + mlp
    layer_ref[...] = layer
    for i, rows in enumerate((layer, attn, mlp)):
        squares = rows * rows
        folded = sum(squares[:, c : c + 128] for c in range(0, squares.shape[1], 128))
        mean = jnp.sum(folded.T, axis=0, keepdims=True) / squares.shape[1]
        rms_ref[i : i + 1, :] = jnp.sqrt(mean + RMS_EPSILON)


def rms_join_kernel(core_ref, own_ref, oth_ref, out_ref):
    first = core_ref[0] == 0
    own, oth = own_ref[...], oth_ref[...]
    low, high = jnp.where(first, own, oth), jnp.where(first, oth, own)
    pieces = []
    for g in range(GROUPS):
        pieces += [rows[:, g * HALF : (g + 1) * HALF] for rows in (low, high)]
    out_ref[...] = jnp.concatenate(pieces, axis=1)


def second_norm_kernel(core_ref, part_ref, recv_ref, x_ref, gains, shifts, residual_ref, low_ref):
    x = x_ref[:, core_ref[0]].reshape(ROWS, -1).astype(f32)
    branch = (part_ref[...].astype(f32) + recv_ref[...].astype(f32)) + shifts[1:2].astype(f32)
    residual = x + branch
    residual_ref[...] = residual
    unit, _ = norm_parts(residual)
    low_ref[...] = (unit * gains[1:2].astype(f32) + shifts[2:3].astype(f32)).astype(bf16)


def put_blocks(stage, to, made, planes):
    if planes:
        for j in range(SUBS):
            at = (j // 8 * 8 + j % 4 * 2 + j // 4 % 2) * 32
            stage[at : at + 32, to] = made[j * 32 : (j + 1) * 32]
    else:
        stage[:, to] = made


def fetch_kernel(first_ref, second_ref, first_out, second_out, sems):
    copies = []
    for i, (ref, out) in enumerate(((first_ref, first_out), (second_ref, second_out))):
        for j in range(4):
            rows = pl.ds(j * 256, 256)
            copies.append(pltpu.make_async_copy(ref.at[rows], out.at[rows], sems.at[4 * i + j]))
    for copy in copies:
        copy.start()
    for copy in copies:
        copy.wait()


def fetch(first, second, late):
    hbm = pl.BlockSpec(memory_space=pltpu.HBM)
    vmem = pl.BlockSpec(memory_space=pltpu.VMEM)
    return pl.pallas_call(
        lambda a, b, unused, *rest: fetch_kernel(a, b, *rest),
        out_shape=[pltpu.VMEM(x.shape, x.dtype) for x in (first, second)],
        in_specs=[hbm] * 3,
        out_specs=[vmem] * 2,
        scratch_shapes=[pltpu.SemaphoreType.DMA((8,))],
        compiler_params=pltpu.CompilerParams(vmem_limit_bytes=LIMIT * 2**20),
        cost_estimate=pl.CostEstimate(flops=1, bytes_accessed=1, transcendentals=0),
        name="fetch",
    )(*hold((first, second, late)))


def feed_kernel(
    arriving, leaving, own_ref, oth_ref, own_cot, oth_cot, up_ref, bias_ref, down_ref,
    own_active, oth_active, own_grad, oth_grad, own_back, oth_back, sums_ref, own_mlp, oth_mlp, blocks_ref,
):
    halves = (
        (oth_ref, oth_cot, oth_active, oth_grad, oth_back),
        (own_ref, own_cot, own_active, own_grad, own_back),
    )
    sums = []
    for rows_ref, cot_ref, active_ref, grad_ref, back_ref in halves:
        total = None
        for c in range(4):
            cols = slice(c * 256, (c + 1) * 256)
            up = up_ref[:, cols]
            bias = jnp.concatenate([bias_ref[2 * c + b : 2 * c + b + 1] for b in range(2)], axis=1)
            hidden = jnp.dot(rows_ref[...], up, preferred_element_type=f32) + bias.astype(f32)
            grad_active = lax.dot_general(
                cot_ref[...], down_ref[cols, :], NT, preferred_element_type=f32
            )
            share = 0.5 + 0.5 * lax.erf(hidden * 0.7071067811865476)
            density = jnp.exp(hidden * hidden * -0.5) * 0.3989422804014327
            active_ref[:, cols] = (hidden * share).astype(bf16)
            grad = (grad_active * (share + hidden * density)).astype(bf16)
            grad_ref[:, cols] = grad
            sums.append(jnp.sum(grad.astype(f32), axis=0, keepdims=True))
            part = lax.dot_general(grad, up, NT, preferred_element_type=f32)
            total = part if total is None else total + part
        back_ref[...] = total.astype(back_ref.dtype)
    for c in range(4):
        sums_ref[0:1, c * 256 : (c + 1) * 256] = sums[c] + sums[4 + c]
    for o in range(7):
        leaving.pop(o).start()
    for c in range(0, P_ONE, 256):
        cols = slice(c, min(c + 256, P_ONE))
        made = lax.dot_general(own_ref[...], own_grad[:, cols], TN, preferred_element_type=f32)
        made += lax.dot_general(oth_ref[...], oth_grad[:, cols], TN, preferred_element_type=f32)
        put_blocks(blocks_ref, cols, made.astype(bf16), True)
    leaving.pop(9).start()
    for o, active_ref, out_ref in ((8, oth_active, oth_mlp), (7, own_active, own_mlp)):
        made = jnp.dot(active_ref[...], down_ref[...], preferred_element_type=f32)
        out_ref[...] = made.astype(out_ref.dtype)
        leaving.pop(o).start()


def residual_grads_kernel(
    core_ref, own_ref, recv_ref, residual_ref, cot_ref, gains, own_w, oth_w,
    grad_ref, low_ref, send_ref, sums_ref,
):
    core = core_ref[0]
    unit, inverse = norm_parts(residual_ref[...])
    grad_normed = own_ref[...].astype(f32) + recv_ref[...].astype(f32)
    cot = cot_ref[...].astype(f32)
    grad = cot + norm_back(grad_normed, unit, inverse, gains[1:2].astype(f32))
    grad_ref[...] = grad
    low = grad.astype(bf16)
    low_ref[...] = low
    for half, w_ref in ((core, own_w), (1 - core, oth_w)):
        made = lax.dot_general(low, w_ref[...], NT, preferred_element_type=f32)
        for g in range(GROUPS):
            for h in range(4):
                block = made[g * HALF : (g + 1) * HALF, h * HEAD : (h + 1) * HEAD]
                send_ref[g * 8 + half * 4 + h] = fold(block).astype(bf16)
    sums = [grad_normed * unit, low.astype(f32), grad_normed, cot]
    for i, rows in enumerate(sums):
        sums_ref[i : i + 1, :] = jnp.sum(rows, axis=0, keepdims=True)


def token_grads_kernel(arriving, leaving, core_ref, recv_ref, own_w, oth_w, own_ref, oth_ref, part_ref):
    core = core_ref[0]
    part = None
    for copy in arriving[1]:
        copy.wait()
    for half, w_ref, ref in ((core, own_w, own_ref), (1 - core, oth_w, oth_ref)):
        for g in range(GROUPS):
            rows = slice(g * HALF, (g + 1) * HALF)
            blocks = [recv_ref.at[g * 8 + half * 4 + h] for h in range(4)]
            pieces = (
                [b[0:64, :HEAD] for b in blocks]
                + [b[0:64, HEAD:] for b in blocks]
                + [unfold(b[64:96, :]) for b in blocks]
            )
            ref[rows, :] = jnp.concatenate(pieces, axis=1)
        for i in range(3):
            arriving[2 if w_ref is own_w else 3][i].wait()
            made = lax.dot_general(
                ref[:, i * LOCAL : (i + 1) * LOCAL], w_ref[i], NT, preferred_element_type=f32
            )
            part = made if part is None else part + made
    part_ref[...] = part.astype(bf16)


def input_grads_kernel(
    core_ref, part_ref, recv_ref, grad_ref, x_ref, gains, second_ref, out_ref, sums_ref
):
    x = x_ref[:, core_ref[0]].reshape(ROWS, -1).astype(f32)
    unit, inverse = norm_parts(x)
    grad_normed = part_ref[...].astype(f32) + recv_ref[...].astype(f32)
    out_ref[...] = grad_ref[...] + norm_back(grad_normed, unit, inverse, gains[0:1].astype(f32))
    sums_ref[0:1, :] = jnp.sum(grad_normed * unit, axis=0, keepdims=True)
    sums_ref[1:2, :] = jnp.sum(grad_normed, axis=0, keepdims=True)
    sums_ref[2:6, :] = second_ref[...]
    sums_ref[6:8, :] = jnp.zeros((2, x.shape[1]), f32)


def join_kernel(core_ref, own_ref, oth_ref, out_ref, sems):
    core = core_ref[0]
    copies = []
    for i, (ref, half) in enumerate(((own_ref, core), (oth_ref, 1 - core))):
        for g in range(GROUPS):
            rows = pl.ds(g * HALF, HALF)
            at = i * GROUPS + g
            copies.append(pltpu.make_async_copy(ref.at[rows], out_ref.at[g, half], sems.at[at]))
    for copy in copies:
        copy.start()
    for copy in copies:
        copy.wait()


def join_rows(core_s, own, oth):
    width = own.shape[1]
    vmem = pl.BlockSpec(memory_space=pltpu.VMEM)
    joined = pl.pallas_call(
        join_kernel,
        out_shape=pltpu.HBM((GROUPS, 2, HALF, width), own.dtype),
        in_specs=[pl.BlockSpec(memory_space=pltpu.SMEM), vmem, vmem],
        out_specs=pl.BlockSpec(memory_space=pltpu.HBM),
        scratch_shapes=[pltpu.SemaphoreType.DMA((2 * GROUPS,))],
        compiler_params=pltpu.CompilerParams(vmem_limit_bytes=8 * 2**20),
        cost_estimate=pl.CostEstimate(flops=1, bytes_accessed=1, transcendentals=0),
        name="join_rows",
    )(core_s, own, oth)
    return joined.reshape(2 * ROWS, width)


def weight_grads_kernel(spans, vectors, *refs):
    planes = not vectors
    out_ref, stage, sems = refs[-3:]
    copies = []

    def send(start, stop):
        to = slice(start, stop)
        copies.append(
            pltpu.make_async_copy(stage.at[:, to], out_ref.at[:, to], sems.at[len(copies)])
        )
        copies[-1].start()

    start = 0
    for i, (first, last) in enumerate(spans):
        a_own, a_oth, b_own, b_oth = refs[4 * i : 4 * i + 4]
        for c in range(first, last, 256):
            cols = slice(c, min(c + 256, last))
            made = lax.dot_general(a_own[...], b_own[:, cols], TN, preferred_element_type=f32)
            made += lax.dot_general(a_oth[...], b_oth[:, cols], TN, preferred_element_type=f32)
            stop = start + cols.stop - cols.start
            put_blocks(stage, slice(start, stop), made.astype(bf16), planes)
            send(start, stop)
            start = stop
    if vectors:
        own, oth, up_sums = [r[...] for r in refs[4 : 4 + vectors]]
        rows = (own + oth)[0:6]
        width = rows.shape[1]
        rows = jnp.concatenate(
            [rows, up_sums, jnp.zeros((121, width), f32)], axis=0
        ).T
        owner = lax.broadcasted_iota(jnp.int32, (width, LOCAL), 0) // (width // SUBS)
        feature = lax.broadcasted_iota(jnp.int32, (width, LOCAL), 1)
        at = lax.broadcasted_iota(jnp.int32, (LOCAL, 128), 1)
        wanted = lax.broadcasted_iota(jnp.int32, (LOCAL, 128), 0) % 8
        for first, place in ((0, 16), (2 * LOCAL, 24)):
            cols = slice(first, first + LOCAL)
            sums = jnp.sum(refs[2][:, cols].astype(f32), axis=0, keepdims=True)
            sums += jnp.sum(refs[3][:, cols].astype(f32), axis=0, keepdims=True)
            mine = jnp.where(owner == feature // 8, sums, 0.0).astype(bf16)
            pick = jnp.where(at == wanted + place, 1.0, 0.0).astype(bf16)
            rows += jnp.dot(mine, pick, preferred_element_type=f32)
        stage[:, start : start + 128] = rows.astype(bf16)
        send(start, start + 128)
    for copy in copies:
        copy.wait()


def weight_grads(parts, vectors=(), late=()):
    width = parts[0][0].shape[1]
    spans = [p[4] for p in parts]
    args = [x for p in parts for x in p[:4]] + list(vectors)
    columns = sum(last - first for first, last in spans)
    shape = (width, columns + (128 if vectors else 0))
    vmem = pl.BlockSpec(memory_space=pltpu.VMEM)
    hbm = pl.BlockSpec(memory_space=pltpu.HBM)

    def body(*refs):
        weight_grads_kernel(
            spans, len(vectors), *refs[: len(args)], *refs[len(args) + len(late) :]
        )

    return pl.pallas_call(
        body,
        out_shape=pltpu.HBM(shape, bf16),
        in_specs=[vmem] * len(args) + [hbm] * len(late),
        out_specs=hbm,
        scratch_shapes=[pltpu.VMEM(shape, bf16), pltpu.SemaphoreType.DMA((16,))],
        compiler_params=pltpu.CompilerParams(vmem_limit_bytes=LIMIT * 2**20),
        cost_estimate=pl.CostEstimate(flops=1, bytes_accessed=1, transcendentals=0),
        name="weight_grads",
        )(*args, *hold(late))


def plane_sum_kernel(y_ref, moved_ref, own_ref, oth_ref):
    for half, ref in ((y_ref[0], own_ref), (1 - y_ref[0], oth_ref)):
        ref[...] = jnp.sum(moved_ref[:, half].astype(f32), axis=0).astype(ref.dtype)


def finish_kernel(
    one_own, one_oth, two_own, two_oth, three_own, three_oth, up_ref, down_ref, out_ref
):
    one = one_own[...] + one_oth[...].astype(f32)
    two = two_own[...] + two_oth[...].astype(f32)
    three = three_own[...] + three_oth[...].astype(f32)
    width = up_ref.shape[1]
    up_ref[:, :P_ONE] = one
    up_ref[:, P_ONE:] = two[:, : width - P_ONE]
    down_ref[:, :P_TWO] = two[:, width - P_ONE :]
    down_ref[:, P_TWO:] = three[:, : width - P_TWO]
    out_ref[...] = three[:, width - P_TWO :]


def last_sums_kernel(moved_ref, qkv_ref, gains_ref, shifts_ref, up_ref, qv_ref):
    summed = jnp.sum(moved_ref[...].astype(f32), axis=0)
    for i in range(3):
        qkv_ref[i] = summed[:, i * LOCAL : (i + 1) * LOCAL]
    small = summed[:, 3 * LOCAL :].T
    gains_ref[0:1, :] = small[0:1]
    gains_ref[1:2, :] = small[2:3]
    shifts_ref[0:1, :] = small[1:2]
    shifts_ref[1:4, :] = small[3:6]
    up_ref[...] = small[6:7]
    qv_ref[0:1, :] = summed[0:1, 3 * LOCAL + 16 : 3 * LOCAL + 24]
    qv_ref[1:2, :] = summed[0:1, 3 * LOCAL + 24 : 3 * LOCAL + 32]


def per_device(
    tokens,
    sub_blocks,
    w_qkv,
    qv_bias,
    w_out,
    w_up,
    up_bias,
    w_down,
    ln_gains,
    row_biases,
    cotangent,
):
    width = tokens.shape[1]
    ctx = lax.axis_index("ctx").astype(jnp.int32)
    core = (lax.axis_index("tp") % 2).astype(jnp.int32)
    core_s = core.reshape(1)
    y_low = (ctx // 4 % 2).reshape(1)

    def swap(x):
        return lax.ppermute(x, "tp", CORE_SWAP)

    def across(x):
        return lax.ppermute(x, "tp", YHI_SWAP)

    def exchange(x):
        return lax.all_to_all(x, "ctx", 0, 0, tiled=True)

    def plane_exchange(blocks):
        return lax.all_to_all(blocks, "ctx", 0, 0, axis_index_groups=PLANES, tiled=True)

    def plane_sum(moved):
        own, oth = kernel_call(
            plane_sum_kernel,
            [((32, moved.shape[1]), f32), ((32, moved.shape[1]), bf16)],
            name="plane_sum",
        )(y_low, moved.reshape(16, 2, 32, -1))
        return own, lax.ppermute(oth, "ctx", YLO_SWAP)

    own_row = lax.dynamic_index_in_dim(sub_blocks, ctx // 8, 0, False)
    order = jnp.arange(SUBS, dtype=jnp.int32)
    holder = jnp.sum(
        jnp.where(own_row[:, None] == order[None, :], order[:, None], 0), axis=0
    ).astype(jnp.int32)
    scalars = jnp.concatenate([holder, core_s])

    split_tokens = tokens.reshape(GROUPS, 2, HALF, width)
    w_own = w_qkv.transpose(1, 0, 2)
    w_oth = swap(w_own)
    b_oth = swap(qv_bias)
    wo_own = w_out
    wo_oth = swap(w_out)

    first, low_own = kernel_call(
        project_own_kernel,
        [((16, 96, 128), bf16), ((ROWS, width), bf16)],
        name="project_own",
        brought=((1, 4), (2, 3), (3, 1), (4, 1), (5, 1)),
        lazy=True,
    )(core_s, split_tokens, w_own, ln_gains, row_biases, qv_bias)
    (send,) = kernel_call(
        project_oth_kernel,
        [((SUBS, 96, 128), bf16)],
        stored=(0,),
        name="project_oth",
    )(core_s, low_own, w_oth, b_oth, first)
    mine = exchange(send)
    theirs = swap(mine)

    mixed, lse = kernel_call(
        attend_kernel,
        [((SUBS, 32, 128), bf16), ((8, TILE), f32)],
        [((2048, HEAD), bf16), ((4096, HEAD), bf16), ((4096, 128), bf16)],
        stored=(0, 1),
        name="attend",
    )(scalars, mine, theirs)
    mixed_back = exchange(mixed)
    cot_own, cot_oth = kernel_call(
        split_kernel,
        [((ROWS, width), bf16), ((ROWS, width), bf16)],
        stored=(0, 1),
        name="split_rows",
        late=(mixed,),
    )(core_s, cotangent.reshape(GROUPS, 2, HALF, width))
    heads_own, heads_oth, attn_part = kernel_call(
        out_kernel,
        [((ROWS, LOCAL), bf16), ((ROWS, LOCAL), bf16), ((ROWS, width), bf16)],
        stored=(0, 1, 2),
        name="project_out",
        late=(cot_own,),
    )(core_s, mixed_back, wo_own, wo_oth)
    attn_recv = across(attn_part)
    residual, normed_two_own = kernel_call(
        second_norm_kernel,
        [((ROWS, width), f32), ((ROWS, width), bf16)],
        stored=(0,),
        name="second_norm",
    )(core_s, attn_part, attn_recv, split_tokens, ln_gains, row_biases)
    normed_two_oth = swap(normed_two_own)

    up_here, down_here = fetch(w_up, w_down, heads_own)
    (
        active_own,
        active_oth,
        grad_hidden_own,
        grad_hidden_oth,
        gn_two_own,
        gn_two_oth,
        up_sums,
        mlp_own,
        mlp_oth,
        blocks_one,
    ) = kernel_call(
        feed_kernel,
        [((ROWS, width), bf16)] * 4
        + [((ROWS, width), bf16), ((ROWS, width), bf16), ((1, width), f32)]
        + [((ROWS, width), bf16), ((ROWS, width), bf16), ((width, P_ONE), bf16)],
        scalars=0,
        stored=tuple(range(10)),
        lazy=True,
        name="feed",
    )(normed_two_own, normed_two_oth, cot_own, cot_oth, up_here, up_bias.reshape(8, -1), down_here)
    gn_two_chip = (gn_two_own.astype(f32) + swap(gn_two_oth).astype(f32)).astype(bf16)
    mlp_chip = (mlp_own.astype(f32) + swap(mlp_oth).astype(f32)).astype(bf16)
    up_parts = (normed_two_own, normed_two_oth, grad_hidden_own, grad_hidden_oth)
    down_parts = (cot_own, cot_oth, active_own, active_oth)
    gn_two_recv = across(gn_two_chip)
    moved_one = plane_exchange(blocks_one)
    blocks_two = weight_grads(
        [up_parts + ((P_ONE, width),), down_parts + ((0, P_TWO),)], late=(blocks_one,)
    )

    grad_residual, grad_attn, grad_heads, second_sums = kernel_call(
        residual_grads_kernel,
        [
            ((ROWS, width), f32),
            ((ROWS, width), bf16),
            ((SUBS, 32, 128), bf16),
            ((4, width), f32),
        ],
        stored=(0, 1, 2, 3),
        name="residual_grads",
        late=(blocks_two, mlp_chip),
    )(core_s, gn_two_chip, gn_two_recv, residual, cot_own, ln_gains, wo_own, wo_oth)
    grad_mixed = exchange(held(grad_heads, moved_one))

    blocks_three = weight_grads(
        [
            down_parts + ((P_TWO, width),),
            (grad_attn, swap(grad_attn), heads_own, swap(heads_oth), (0, LOCAL)),
        ]
    )
    moved_two = plane_exchange(held(blocks_two, blocks_three))

    mlp_recv = across(mlp_chip)

    dq, kept, given = kernel_call(
        attend_back_kernel,
        [((2048, HEAD), bf16), ((2048, 128), f32), ((2048, 128), bf16)],
        [
            ((2048, 128), bf16),
            ((2048, 128), bf16),
            ((4096, 128), bf16),
            ((HEAD, 4096), bf16),
            ((8, TILE), f32),
            ((4096, 128), f32),
        ],
        name="attend_back",
        brought=((1, 4), (2, 4), (3, 2), (4, 2), (5, 1)),
        late=(blocks_three,),
    )(scalars, mine, theirs, grad_mixed, mixed, lse)
    (packed,) = kernel_call(
        pack_grads_kernel,
        [((SUBS, 96, 128), bf16)],
        stored=(0,),
        name="pack_grads",
        late=(mlp_recv,),
    )(scalars, dq, kept, swap(given))
    packed = held(packed, moved_two)
    grads_back = exchange(packed)

    normed_own, normed_oth = kernel_call(
        first_norm_kernel,
        [((ROWS, width), bf16), ((ROWS, width), bf16)],
        name="first_norm",
        stored=(0, 1),
        late=(packed,),
    )(core_s, split_tokens, ln_gains, row_biases)
    sums_one = plane_sum(moved_one)
    sums_two = plane_sum(moved_two)

    rows_own, rows_oth, gn_one_part = kernel_call(
        token_grads_kernel,
        [((ROWS, 3 * LOCAL), bf16), ((ROWS, 3 * LOCAL), bf16), ((ROWS, width), bf16)],
        stored=(0, 1, 2),
        name="token_grads",
        brought=((1, 4), (2, 3), (3, 3)),
        lazy=True,
    )(core_s, grads_back, w_own, w_oth)
    gn_one_recv = across(gn_one_part)
    rows_recv = swap(rows_oth)
    moved_three = plane_exchange(
        held(blocks_three, sums_one[1], sums_two[1], normed_oth)
    )
    input_own, sums = kernel_call(
        input_grads_kernel,
        [((ROWS, width), f32), ((8, width), f32)],
        name="input_grads",
    )(core_s, gn_one_part, gn_one_recv, grad_residual, split_tokens, ln_gains, second_sums)
    blocks_four = weight_grads(
        [(normed_own, normed_oth, rows_own, rows_recv, (0, 3 * LOCAL))],
        (sums, swap(sums), up_sums),
    )
    blocks_four = held(blocks_four, moved_three)
    moved_four = exchange(blocks_four)

    layer_own, rms_own = kernel_call(
        layer_kernel,
        [((ROWS, width), f32), ((3, ROWS), f32)],
        scalars=0,
        name="layer_out",
        late=(blocks_four,),
    )(residual, attn_part, attn_recv, mlp_chip, mlp_recv, row_biases)
    layer_out = join_rows(core_s, layer_own, swap(layer_own))
    (rms_rows,) = kernel_call(
        rms_join_kernel, [((3, 2 * ROWS), f32)], name="rms_join"
    )(core_s, rms_own, swap(rms_own))
    input_grad = join_rows(core_s, input_own, swap(input_own))
    sums_three = plane_sum(moved_three)
    grad_up, grad_down, grad_out = kernel_call(
        finish_kernel,
        [((32, width), f32), ((32, width), f32), ((32, LOCAL), f32)],
        scalars=0,
        name="finish",
        late=(layer_out, input_grad, rms_rows),
    )(*sums_one, *sums_two, *sums_three)
    grad_qkv, grad_gains, grad_shifts, grad_up_bias, grad_qv_bias = kernel_call(
        last_sums_kernel,
        [
            ((3, 32, LOCAL), f32),
            ((2, 32), f32),
            ((4, 32), f32),
            ((1, 32), f32),
            ((2, 8), f32),
        ],
        scalars=0,
        name="last_sums",
        late=(grad_out,),
    )(moved_four.reshape(SUBS, 32, -1))
    return (
        layer_out,
        input_grad,
        rms_rows,
        grad_qkv.transpose(1, 0, 2),
        grad_qv_bias,
        grad_out.T,
        grad_up,
        grad_up_bias[0],
        grad_down.T,
        grad_gains,
        grad_shifts,
    )


def solution(mesh):
    return jax.shard_map(
        per_device,
        mesh=mesh,
        in_specs=(
            P("ctx", None),
            P(),
            P(None, None, "tp"),
            P(None, "tp"),
            P("tp", None),
            P(None, "tp"),
            P("tp"),
            P("tp", None),
            P(),
            P(),
            P("ctx", None),
        ),
        out_specs=(
            P("ctx", None),
            P("ctx", None),
            P(None, "ctx"),
            P("ctx", None, "tp"),
            P(None, ("tp", "ctx")),
            P("tp", "ctx"),
            P("ctx", "tp"),
            P(("tp", "ctx")),
            P("tp", "ctx"),
            P(None, "ctx"),
            P(None, "ctx"),
        ),
        check_vma=False,
    )
```

```python
import jax
import jax.numpy as jnp
from jax import lax
from jax.experimental import pallas as pl
from jax.experimental.pallas import tpu as pltpu
from jax.sharding import PartitionSpec as P

HEAD = 64
SUBS = 32
HALF = 64
GROUPS = 4
ROWS = GROUPS * HALF
LOCAL = 256
P_ONE = 640
P_TWO = 384
LIMIT = 36
TILE = 256
CHUNK = 512
EPSILON = 1e-05
RMS_EPSILON = 1e-06
LOG_SHRINK = 10 * 0.6931471805599453
SHRINK = 2.0**-10
CORE_SWAP = [(0, 1), (1, 0), (2, 3), (3, 2)]
YHI_SWAP = [(0, 2), (2, 0), (1, 3), (3, 1)]
YLO_SWAP = [(j, j ^ 4) for j in range(SUBS)]
CROSS_SWAP = [(0, 3), (3, 0), (1, 2), (2, 1)]
PLANES = [[z * 8 + y * 4 + x for z in range(4) for x in range(4)] for y in range(2)]
NT = (((1,), (1,)), ((), ()))
TN = (((0,), (0,)), ((), ()))
bf16 = jnp.bfloat16
f32 = jnp.float32


def norm_parts(values):
    centre = jnp.mean(values, axis=-1, keepdims=True)
    centred = values - centre
    spread = jnp.mean(centred * centred, axis=-1, keepdims=True)
    inverse = lax.rsqrt(spread + EPSILON)
    return centred * inverse, inverse


def norm_back(grad_normed, unit_rows, inverse, gain):
    grad_unit = grad_normed * gain
    first_mean = jnp.mean(grad_unit, axis=-1, keepdims=True)
    second_mean = jnp.mean(grad_unit * unit_rows, axis=-1, keepdims=True)
    return inverse * (grad_unit - first_mean - unit_rows * second_mean)


def hold(arrays):
    return [pltpu.with_memory_space_constraint(x, pltpu.HBM) for x in arrays]


def order(arrays):
    return [x if x.size * x.dtype.itemsize < 2**18 else hold([x])[0] for x in arrays]


def pieces_of(ref, stage, sems, first, pieces):
    step = ref.shape[0] // pieces
    return [
        pltpu.make_async_copy(
            ref.at[pl.ds(i * step, step)], stage.at[pl.ds(i * step, step)], sems.at[first + i]
        )
        for i in range(pieces)
    ]


def with_copies(body, n_in, n_late, n_out, stored, brought, lazy):
    def kernel(*refs):
        ins, outs = list(refs[:n_in]), list(refs[n_in + n_late : n_in + n_late + n_out])
        rest = refs[n_in + n_late + n_out :]
        arriving = {}
        if brought:
            stages, in_sems, rest = rest[: len(brought)], rest[len(brought)], rest[len(brought) + 1 :]
            first = 0
            for stage, (o, pieces) in zip(stages, brought):
                arriving[o] = pieces_of(ins[o], stage, in_sems, first, pieces)
                ins[o] = stage
                first += pieces
            for copies in arriving.values():
                for copy in copies:
                    copy.start()
        stages, rest = rest[: len(stored)], rest[len(stored) :]
        copies = []
        if stored:
            sems, rest = rest[0], rest[1:]
            copies = [
                pltpu.make_async_copy(stage, outs[o], sems.at[i])
                for i, (stage, o) in enumerate(zip(stages, stored))
            ]
        for stage, o in zip(stages, stored):
            outs[o] = stage
        leaving = dict(zip(stored, copies))
        if lazy:
            body(arriving, leaving, *ins, *outs, *rest)
        else:
            for arrivals in arriving.values():
                for copy in arrivals:
                    copy.wait()
            body(*ins, *outs, *rest)
        for copy in leaving.values():
            copy.start()
        for copy in copies:
            copy.wait()

    return kernel


def kernel_call(
    body, outs, scratch=(), scalars=1, name=None, stored=(), late=(), brought=(), lazy=False
):
    smem = pl.BlockSpec(memory_space=pltpu.SMEM)
    vmem = pl.BlockSpec(memory_space=pltpu.VMEM)
    hbm = pl.BlockSpec(memory_space=pltpu.HBM)
    shapes = [pltpu.VMEM(s, d) for s, d in scratch]
    if stored:
        shapes = (
            [pltpu.VMEM(*outs[o]) for o in stored]
            + [pltpu.SemaphoreType.DMA((len(stored),))]
            + shapes
        )

    def call(*args):
        args, more, specs = list(args), [], [smem] * scalars + [vmem] * (len(args) - scalars)
        for o, _ in brought:
            specs[o] = hbm
            more.append(pltpu.VMEM(args[o].shape, args[o].dtype))
            (args[o],) = hold([args[o]])
        if brought:
            more.append(pltpu.SemaphoreType.DMA((sum(pieces for _, pieces in brought),)))
        return pl.pallas_call(
            with_copies(body, len(args), len(late), len(outs), stored, brought, lazy),
            out_shape=[
                pltpu.HBM(s, d) if o in stored else jax.ShapeDtypeStruct(s, d)
                for o, (s, d) in enumerate(outs)
            ],
            in_specs=specs + [pl.BlockSpec(memory_space=pl.ANY)] * len(late),
            out_specs=[hbm if o in stored else vmem for o in range(len(outs))],
            scratch_shapes=more + shapes,
            compiler_params=pltpu.CompilerParams(vmem_limit_bytes=LIMIT * 2**20),
            cost_estimate=pl.CostEstimate(flops=1, bytes_accessed=1, transcendentals=0),
            name=name,
        )(*args, *order(late))

    return call


def held(x, *late):
    hbm = pl.BlockSpec(memory_space=pltpu.HBM)
    return pl.pallas_call(
        lambda *refs: None,
        out_shape=pltpu.HBM(x.shape, x.dtype),
        in_specs=[hbm] + [pl.BlockSpec(memory_space=pl.ANY)] * len(late),
        out_specs=hbm,
        input_output_aliases={0: 0},
        cost_estimate=pl.CostEstimate(flops=1, bytes_accessed=1, transcendentals=0),
        name="held",
    )(*hold([x]), *late)


def fold(rows):
    return jnp.concatenate([rows[:32], rows[32:]], axis=1)


def unfold(packed):
    return jnp.concatenate([packed[:, :HEAD], packed[:, HEAD:]], axis=0)


def project_own_kernel(arriving, leaving, core_ref, x_ref, w_ref, gains, shifts, b_ref, send_ref, low_ref):
    for o in (1, 3, 4, 5):
        for copy in arriving[o]:
            copy.wait()
    x = x_ref[:, core_ref[0]].reshape(ROWS, -1).astype(f32)
    unit, _ = norm_parts(x)
    low = (unit * gains[0:1].astype(f32) + shifts[0:1].astype(f32)).astype(bf16)
    low_ref[...] = low
    for w in arriving[2]:
        w.wait()
    for g, h, qk, v in projected(low, w_ref, b_ref):
        send_ref[g * 4 + h, 0:64, :] = qk
        send_ref[g * 4 + h, 64:96, :] = v


def project_oth_kernel(core_ref, low_ref, w_ref, b_ref, first_ref, send_ref):
    core = core_ref[0]
    for g in range(GROUPS):
        for h in range(4):
            send_ref[g * 8 + core * 4 + h] = first_ref[g * 4 + h]
    for g, h, qk, v in projected(low_ref[...], w_ref, b_ref):
        block = g * 8 + (1 - core) * 4 + h
        send_ref[block, 0:64, :] = qk
        send_ref[block, 64:96, :] = v


def projected(low, w_ref, b_ref):
    q = jnp.dot(low, w_ref[0], preferred_element_type=f32) + b_ref[0:1].astype(f32)
    k = jnp.dot(low, w_ref[1], preferred_element_type=f32)
    v = jnp.dot(low, w_ref[2], preferred_element_type=f32) + b_ref[1:2].astype(f32)
    for g in range(GROUPS):
        for h in range(4):
            rows = slice(g * HALF, (g + 1) * HALF)
            cols = slice(h * HEAD, (h + 1) * HEAD)
            qk = jnp.concatenate([q[rows, cols], k[rows, cols]], axis=1)
            yield g, h, qk.astype(bf16), fold(v[rows, cols]).astype(bf16)


def pair_masks(core, transposed):
    shape = (CHUNK, TILE) if transposed else (TILE, CHUNK)
    q = lax.broadcasted_iota(jnp.int32, shape, 1 if transposed else 0)
    key = lax.broadcasted_iota(jnp.int32, shape, 0 if transposed else 1)
    other = key >= TILE
    k = jnp.where(other, key - TILE, key)
    q_sub = lax.shift_right_logical(q, 6)
    k_sub = lax.shift_right_logical(k, 6)
    prompt = (other & (q_sub + core > k_sub)) | (jnp.logical_not(other) & (q >= k))
    cont = prompt & (lax.shift_right_logical(q, 7) == lax.shift_right_logical(k, 7))
    return prompt, cont


def chunks_of(tile, prompt, cont):
    if tile < 4:
        return [(j, None) for j in range(tile)] + [(tile, prompt)]
    return [(j, None) for j in range(4)] + [(tile, cont)]


def attend_kernel(sc_ref, own_ref, oth_ref, out_ref, lse_ref, q_s, k_s, v_s):
    core = sc_ref[SUBS]
    const = jnp.full((HALF, HEAD), SHRINK, bf16)
    for p in range(SUBS):
        d = sc_ref[p]
        at = p // 4 * CHUNK + p % 4 * HALF
        q_s[p * HALF : (p + 1) * HALF, :] = own_ref[d, 0:64, :HEAD] * jnp.asarray(0.125, bf16)
        for ref, start in ((own_ref, at), (oth_ref, at + TILE)):
            k_s[start : start + HALF, :] = ref[d, 0:64, HEAD:]
            v = unfold(ref[d, 64:96, :]) * jnp.asarray(SHRINK, bf16)
            v_s[start : start + HALF, :] = jnp.concatenate([v, const], axis=1)
    prompt, cont = pair_masks(core, False)
    for t in range(8):
        q = q_s[t * TILE : (t + 1) * TILE, :]
        total = None
        for j, mask in chunks_of(t, prompt, cont):
            keys = slice(j * CHUNK, (j + 1) * CHUNK)
            s = lax.dot_general(q, k_s[keys, :], NT, preferred_element_type=f32)
            w = jnp.exp(s)
            if mask is not None:
                w = jnp.where(mask, w, 0.0)
            part = jnp.dot(w.astype(bf16), v_s[keys, :], preferred_element_type=f32)
            total = part if total is None else total + part
        mixed = total[:, :HEAD] / total[:, HEAD:]
        lse_ref[t : t + 1, :] = jnp.log(total.T[HEAD : HEAD + 1, :]) + LOG_SHRINK
        for i in range(4):
            out_ref[sc_ref[t * 4 + i]] = fold(mixed[i * HALF : (i + 1) * HALF]).astype(bf16)


def attend_back_kernel(
    arriving, leaving, sc_ref, own_ref, oth_ref, do_ref, o_ref, lse_ref,
    dq_ref, keep_ref, send_ref,
    q_s, do_s, vk_s, kt_s, inner_s, acc_s,
):
    core = sc_ref[SUBS]
    zero = jnp.zeros((HALF, HEAD), bf16)
    for o in (1, 2, 3):
        for copy in arriving[o]:
            copy.wait()
    for p in range(SUBS):
        d = sc_ref[p]
        at = p // 4 * CHUNK + p % 4 * HALF
        rows = slice(p * HALF, (p + 1) * HALF)
        q = own_ref[d, 0:64, :HEAD] * jnp.asarray(0.125, bf16)
        q_s[rows, :] = jnp.concatenate([zero, q], axis=1)
        grad = unfold(do_ref[d])
        do_s[rows, :] = jnp.concatenate([grad, zero], axis=1)
        for ref, start in ((own_ref, at), (oth_ref, at + TILE)):
            vk_s[start : start + HALF, :] = jnp.concatenate(
                [unfold(ref[d, 64:96, :]), ref[d, 0:64, HEAD:]], axis=1
            )
    for j in range(8):
        keys = slice(j * CHUNK, (j + 1) * CHUNK)
        kt_s[:, keys] = vk_s[keys, :].T[HEAD:, :]
    for o in (4, 5):
        for copy in arriving[o]:
            copy.wait()
    for t in range(8):
        both = []
        for i in range(4):
            d = sc_ref[t * 4 + i]
            both.append(unfold(do_ref[d].astype(f32) * o_ref[d].astype(f32)))
        inner_s[t : t + 1, :] = jnp.sum(jnp.concatenate(both, axis=0).T, axis=0, keepdims=True)
    prompt, cont = pair_masks(core, True)
    started = set()
    for t in range(8):
        tile = slice(t * TILE, (t + 1) * TILE)
        q = q_s[tile, :]
        grad = do_s[tile, :]
        lse = lse_ref[t : t + 1, :]
        inner = inner_s[t : t + 1, :]
        dq = None
        for j, mask in chunks_of(t, prompt, cont):
            keys = slice(j * CHUNK, (j + 1) * CHUNK)
            vk = vk_s[keys, :]
            s = lax.dot_general(vk, q, NT, preferred_element_type=f32)
            a = jnp.exp(s - lse)
            if mask is not None:
                a = jnp.where(mask, a, 0.0)
            dp = lax.dot_general(vk, grad, NT, preferred_element_type=f32)
            ds = (a * (dp - inner)).astype(bf16)
            part = jnp.dot(a.astype(bf16), grad, preferred_element_type=f32) + jnp.dot(
                ds, q, preferred_element_type=f32
            )
            if j in started:
                acc_s[keys, :] += part
            else:
                acc_s[keys, :] = part
                started.add(j)
            dq_part = jnp.dot(kt_s[:, keys], ds, preferred_element_type=f32)
            dq = dq_part if dq is None else dq + dq_part
        dq_ref[tile, :] = (dq * 0.125).T.astype(bf16)
    for j in range(8):
        keep_ref[j * TILE : (j + 1) * TILE, :] = acc_s[j * CHUNK : j * CHUNK + TILE, :]
        send_ref[j * TILE : (j + 1) * TILE, :] = acc_s[
            j * CHUNK + TILE : (j + 1) * CHUNK, :
        ].astype(bf16)


def pack_grads_kernel(sc_ref, dq_ref, keep_ref, recv_ref, out_ref):
    for p in range(SUBS):
        rows = slice(p * HALF, (p + 1) * HALF)
        summed = (keep_ref[rows, :] + recv_ref[rows, :].astype(f32)).astype(bf16)
        d = sc_ref[p]
        out_ref[d, 0:64, :] = jnp.concatenate([dq_ref[rows, :], summed[:, HEAD:]], axis=1)
        out_ref[d, 64:96, :] = fold(summed[:, :HEAD])


def out_kernel(
    arriving, leaving, core_ref, recv_ref, own_w, oth_w, own_ref, oth_ref, part_ref
):
    core = core_ref[0]
    for half, ref in ((core, own_ref), (1 - core, oth_ref)):
        for g in range(GROUPS):
            heads = [unfold(recv_ref[g * 8 + half * 4 + h]) for h in range(4)]
            ref[g * HALF : (g + 1) * HALF, :] = jnp.concatenate(heads, axis=1)
    for o in (0, 1):
        leaving.pop(o).start()
    part = jnp.dot(own_ref[...], own_w[...], preferred_element_type=f32) + jnp.dot(
        oth_ref[...], oth_w[...], preferred_element_type=f32
    )
    part_ref[...] = part.astype(bf16)


def split_kernel(core_ref, rows_ref, own_ref, oth_ref):
    own_ref[...] = rows_ref[:, core_ref[0]].reshape(own_ref.shape)
    oth_ref[...] = rows_ref[:, 1 - core_ref[0]].reshape(oth_ref.shape)


def first_norm_kernel(core_ref, x_ref, gains, shifts, own_ref, oth_ref):
    for half, low_ref in ((core_ref[0], own_ref), (1 - core_ref[0], oth_ref)):
        unit, _ = norm_parts(x_ref[:, half].reshape(ROWS, -1).astype(f32))
        low_ref[...] = (unit * gains[0:1].astype(f32) + shifts[0:1].astype(f32)).astype(bf16)


def layer_kernel(
    residual_ref, part_ref, part_recv_ref, mlp_ref, mlp_recv_ref, shifts, layer_ref, rms_ref
):
    attn = (part_ref[...].astype(f32) + part_recv_ref[...].astype(f32)) + shifts[1:2].astype(f32)
    mlp = (mlp_ref[...].astype(f32) + mlp_recv_ref[...].astype(f32)) + shifts[3:4].astype(f32)
    layer = residual_ref[...] + mlp
    layer_ref[...] = layer
    for i, rows in enumerate((layer, attn, mlp)):
        squares = rows * rows
        folded = sum(squares[:, c : c + 128] for c in range(0, squares.shape[1], 128))
        mean = jnp.sum(folded.T, axis=0, keepdims=True) / squares.shape[1]
        rms_ref[i : i + 1, :] = jnp.sqrt(mean + RMS_EPSILON)


def rms_join_kernel(core_ref, own_ref, oth_ref, out_ref):
    first = core_ref[0] == 0
    own, oth = own_ref[...], oth_ref[...]
    low, high = jnp.where(first, own, oth), jnp.where(first, oth, own)
    pieces = []
    for g in range(GROUPS):
        pieces += [rows[:, g * HALF : (g + 1) * HALF] for rows in (low, high)]
    out_ref[...] = jnp.concatenate(pieces, axis=1)


def second_norm_kernel(
    arriving, leaving, core_ref, part_ref, recv_ref, x_ref, gains, shifts, residual_ref, low_ref
):
    x = x_ref[:, core_ref[0]].reshape(ROWS, -1).astype(f32)
    branch = (part_ref[...].astype(f32) + recv_ref[...].astype(f32)) + shifts[1:2].astype(f32)
    residual = x + branch
    residual_ref[...] = residual
    leaving.pop(0).start()
    unit, _ = norm_parts(residual)
    low_ref[...] = (unit * gains[1:2].astype(f32) + shifts[2:3].astype(f32)).astype(bf16)


def put_blocks(stage, to, made, planes):
    if planes:
        for j in range(SUBS):
            at = (j // 8 * 8 + j % 4 * 2 + j // 4 % 2) * 32
            stage[at : at + 32, to] = made[j * 32 : (j + 1) * 32]
    else:
        stage[:, to] = made


def fetch_kernel(first_ref, second_ref, first_out, second_out, sems):
    copies = []
    for i, (ref, out) in enumerate(((first_ref, first_out), (second_ref, second_out))):
        for j in range(4):
            rows = pl.ds(j * 256, 256)
            copies.append(pltpu.make_async_copy(ref.at[rows], out.at[rows], sems.at[4 * i + j]))
    for copy in copies:
        copy.start()
    for copy in copies:
        copy.wait()


def fetch(first, second, late):
    hbm = pl.BlockSpec(memory_space=pltpu.HBM)
    vmem = pl.BlockSpec(memory_space=pltpu.VMEM)
    return pl.pallas_call(
        lambda a, b, unused, *rest: fetch_kernel(a, b, *rest),
        out_shape=[pltpu.VMEM(x.shape, x.dtype) for x in (first, second)],
        in_specs=[hbm] * 3,
        out_specs=[vmem] * 2,
        scratch_shapes=[pltpu.SemaphoreType.DMA((8,))],
        compiler_params=pltpu.CompilerParams(vmem_limit_bytes=LIMIT * 2**20),
        cost_estimate=pl.CostEstimate(flops=1, bytes_accessed=1, transcendentals=0),
        name="fetch",
    )(*hold((first, second, late)))


def feed_kernel(
    arriving, leaving, own_ref, oth_ref, own_cot, oth_cot, up_ref, bias_ref, down_ref,
    own_active, oth_active, own_grad, oth_grad, own_back, oth_back, sums_ref, own_mlp, oth_mlp, blocks_ref,
):
    halves = (
        (oth_ref, oth_cot, oth_active, oth_grad, oth_back),
        (own_ref, own_cot, own_active, own_grad, own_back),
    )
    sums = []
    for rows_ref, cot_ref, active_ref, grad_ref, back_ref in halves:
        total = None
        for c in range(4):
            cols = slice(c * 256, (c + 1) * 256)
            up = up_ref[:, cols]
            bias = jnp.concatenate([bias_ref[2 * c + b : 2 * c + b + 1] for b in range(2)], axis=1)
            hidden = jnp.dot(rows_ref[...], up, preferred_element_type=f32) + bias.astype(f32)
            grad_active = lax.dot_general(
                cot_ref[...], down_ref[cols, :], NT, preferred_element_type=f32
            )
            share = 0.5 + 0.5 * lax.erf(hidden * 0.7071067811865476)
            density = jnp.exp(hidden * hidden * -0.5) * 0.3989422804014327
            active_ref[:, cols] = (hidden * share).astype(bf16)
            grad = (grad_active * (share + hidden * density)).astype(bf16)
            grad_ref[:, cols] = grad
            sums.append(jnp.sum(grad.astype(f32), axis=0, keepdims=True))
            part = lax.dot_general(grad, up, NT, preferred_element_type=f32)
            total = part if total is None else total + part
        back_ref[...] = total.astype(back_ref.dtype)
    for c in range(4):
        sums_ref[0:1, c * 256 : (c + 1) * 256] = sums[c] + sums[4 + c]
    for o in range(7):
        leaving.pop(o).start()
    for c in range(0, P_ONE, 256):
        cols = slice(c, min(c + 256, P_ONE))
        made = lax.dot_general(own_ref[...], own_grad[:, cols], TN, preferred_element_type=f32)
        made += lax.dot_general(oth_ref[...], oth_grad[:, cols], TN, preferred_element_type=f32)
        put_blocks(blocks_ref, cols, made.astype(bf16), True)
    leaving.pop(9).start()
    for o, active_ref, out_ref in ((8, oth_active, oth_mlp), (7, own_active, own_mlp)):
        made = jnp.dot(active_ref[...], down_ref[...], preferred_element_type=f32)
        out_ref[...] = made.astype(out_ref.dtype)
        leaving.pop(o).start()


def residual_grads_kernel(
    arriving, leaving, core_ref, own_ref, recv_ref, residual_ref, cot_ref, gains, own_w, oth_w,
    grad_ref, low_ref, send_ref, sums_ref,
):
    core = core_ref[0]
    unit, inverse = norm_parts(residual_ref[...])
    grad_normed = own_ref[...].astype(f32) + recv_ref[...].astype(f32)
    cot = cot_ref[...].astype(f32)
    grad = cot + norm_back(grad_normed, unit, inverse, gains[1:2].astype(f32))
    grad_ref[...] = grad
    low = grad.astype(bf16)
    low_ref[...] = low
    sums = [grad_normed * unit, low.astype(f32), grad_normed, cot]
    for i, rows in enumerate(sums):
        sums_ref[i : i + 1, :] = jnp.sum(rows, axis=0, keepdims=True)
    for o in (0, 1, 3):
        leaving.pop(o).start()
    for half, w_ref in ((core, own_w), (1 - core, oth_w)):
        made = lax.dot_general(low, w_ref[...], NT, preferred_element_type=f32)
        for g in range(GROUPS):
            for h in range(4):
                block = made[g * HALF : (g + 1) * HALF, h * HEAD : (h + 1) * HEAD]
                send_ref[g * 8 + half * 4 + h] = fold(block).astype(bf16)


def token_grads_kernel(arriving, leaving, core_ref, recv_ref, own_w, oth_w, own_ref, oth_ref, part_ref):
    core = core_ref[0]
    part = None
    for copy in arriving[1]:
        copy.wait()
    for half, w_ref, ref in ((core, own_w, own_ref), (1 - core, oth_w, oth_ref)):
        for g in range(GROUPS):
            rows = slice(g * HALF, (g + 1) * HALF)
            blocks = [recv_ref.at[g * 8 + half * 4 + h] for h in range(4)]
            pieces = (
                [b[0:64, :HEAD] for b in blocks]
                + [b[0:64, HEAD:] for b in blocks]
                + [unfold(b[64:96, :]) for b in blocks]
            )
            ref[rows, :] = jnp.concatenate(pieces, axis=1)
        leaving.pop(0 if ref is own_ref else 1).start()
        for i in range(3):
            arriving[2 if w_ref is own_w else 3][i].wait()
            made = lax.dot_general(
                ref[:, i * LOCAL : (i + 1) * LOCAL], w_ref[i], NT, preferred_element_type=f32
            )
            part = made if part is None else part + made
    part_ref[...] = part.astype(bf16)


def first_sums_kernel(core_ref, part_ref, x_ref, sums_ref):
    unit, _ = norm_parts(x_ref[:, core_ref[0]].reshape(ROWS, -1).astype(f32))
    part = part_ref[...].astype(f32)
    sums_ref[0:1, :] = jnp.sum(part * unit, axis=0, keepdims=True)
    sums_ref[1:2, :] = jnp.sum(part, axis=0, keepdims=True)
    sums_ref[2:8, :] = jnp.zeros((6, part.shape[1]), f32)


def input_grads_kernel(core_ref, part_ref, recv_ref, grad_ref, x_ref, gains, out_ref):
    x = x_ref[:, core_ref[0]].reshape(ROWS, -1).astype(f32)
    unit, inverse = norm_parts(x)
    grad_normed = part_ref[...].astype(f32) + recv_ref[...].astype(f32)
    out_ref[...] = grad_ref[...] + norm_back(grad_normed, unit, inverse, gains[0:1].astype(f32))


def join_kernel(core_ref, own_ref, oth_ref, out_ref, sems):
    core = core_ref[0]
    copies = []
    for i, (ref, half) in enumerate(((own_ref, core), (oth_ref, 1 - core))):
        for g in range(GROUPS):
            rows = pl.ds(g * HALF, HALF)
            at = i * GROUPS + g
            copies.append(pltpu.make_async_copy(ref.at[rows], out_ref.at[g, half], sems.at[at]))
    for copy in copies:
        copy.start()
    for copy in copies:
        copy.wait()


def join_rows(core_s, own, oth):
    width = own.shape[1]
    vmem = pl.BlockSpec(memory_space=pltpu.VMEM)
    joined = pl.pallas_call(
        join_kernel,
        out_shape=pltpu.HBM((GROUPS, 2, HALF, width), own.dtype),
        in_specs=[pl.BlockSpec(memory_space=pltpu.SMEM), vmem, vmem],
        out_specs=pl.BlockSpec(memory_space=pltpu.HBM),
        scratch_shapes=[pltpu.SemaphoreType.DMA((2 * GROUPS,))],
        compiler_params=pltpu.CompilerParams(vmem_limit_bytes=8 * 2**20),
        cost_estimate=pl.CostEstimate(flops=1, bytes_accessed=1, transcendentals=0),
        name="join_rows",
    )(core_s, own, oth)
    return joined.reshape(2 * ROWS, width)


def weight_grads_kernel(spans, planes, arriving, *refs):
    out_ref, stage, sems = refs[-3:]
    copies = []

    def send(start, stop):
        copies.append(
            pltpu.make_async_copy(
                stage.at[:, pl.ds(start, stop - start)],
                out_ref.at[:, pl.ds(start, stop - start)],
                sems.at[len(copies)],
            )
        )
        copies[-1].start()

    start = 0
    for i, (first, last) in enumerate(spans):
        a_own, a_oth, b_own, b_oth = refs[4 * i : 4 * i + 4]
        for o in range(4 * i, 4 * i + 4):
            for copy in arriving[o]:
                copy.wait()
        for c in range(first, last, 256):
            cols = slice(c, min(c + 256, last))
            made = lax.dot_general(a_own[...], b_own[:, cols], TN, preferred_element_type=f32)
            made += lax.dot_general(a_oth[...], b_oth[:, cols], TN, preferred_element_type=f32)
            stop = start + cols.stop - cols.start
            put_blocks(stage, slice(start, stop), made.astype(bf16), planes)
            send(start, stop)
            start = stop
    for copy in copies:
        copy.wait()


def vector_columns_kernel(
    into_ref, own_rows, oth_rows, own, core, across, cross, second, second_core, up_sums,
    out_ref, stage, sem,
):
    width = up_sums.shape[1]
    rows = ((own[...] + core[...]) + (across[...] + cross[...]))[0:2]
    rows = [rows, second[...] + second_core[...], up_sums[...], jnp.zeros((121, width), f32)]
    rows = jnp.concatenate(rows, axis=0).T
    owner = lax.broadcasted_iota(jnp.int32, (width, LOCAL), 0) // (width // SUBS)
    feature = lax.broadcasted_iota(jnp.int32, (width, LOCAL), 1)
    at = lax.broadcasted_iota(jnp.int32, (LOCAL, 128), 1)
    wanted = lax.broadcasted_iota(jnp.int32, (LOCAL, 128), 0) % 8
    for first, place in ((0, 16), (2 * LOCAL, 24)):
        cols = slice(first, first + LOCAL)
        sums = jnp.sum(own_rows[:, cols].astype(f32), axis=0, keepdims=True)
        sums += jnp.sum(oth_rows[:, cols].astype(f32), axis=0, keepdims=True)
        mine = jnp.where(owner == feature // 8, sums, 0.0).astype(bf16)
        pick = jnp.where(at == wanted + place, 1.0, 0.0).astype(bf16)
        rows += jnp.dot(mine, pick, preferred_element_type=f32)
    stage[...] = rows.astype(bf16)
    copy = pltpu.make_async_copy(stage, out_ref.at[:, pl.ds(3 * LOCAL, 128)], sem)
    copy.start()
    copy.wait()


def vector_columns(into, *arrays):
    hbm = pl.BlockSpec(memory_space=pltpu.HBM)
    vmem = pl.BlockSpec(memory_space=pltpu.VMEM)
    return pl.pallas_call(
        vector_columns_kernel,
        out_shape=pltpu.HBM(into.shape, into.dtype),
        in_specs=[hbm] + [vmem] * len(arrays),
        out_specs=hbm,
        scratch_shapes=[pltpu.VMEM((into.shape[0], 128), bf16), pltpu.SemaphoreType.DMA(())],
        input_output_aliases={0: 0},
        compiler_params=pltpu.CompilerParams(vmem_limit_bytes=LIMIT * 2**20),
        cost_estimate=pl.CostEstimate(flops=1, bytes_accessed=1, transcendentals=0),
        name="vector_columns",
    )(*hold([into]), *arrays)


def weight_grads(parts, late=(), planes=True, spare=0):
    width = parts[0][0].shape[1]
    spans = [p[4] for p in parts]
    args = [x for p in parts for x in p[:4]]
    columns = sum(last - first for first, last in spans)
    hbm = pl.BlockSpec(memory_space=pltpu.HBM)
    n = len(args)

    def body(*refs):
        out_ref, rest = refs[n + len(late)], refs[n + len(late) + 1 :]
        stages, in_sems, stage, sems = rest[:n], rest[n], rest[n + 1], rest[n + 2]
        arriving = [pieces_of(refs[i], stages[i], in_sems, 2 * i, 2) for i in range(n)]
        for copies in arriving:
            for copy in copies:
                copy.start()
        weight_grads_kernel(spans, planes, arriving, *stages, out_ref, stage, sems)

    return pl.pallas_call(
        body,
        out_shape=pltpu.HBM((width, columns + spare), bf16),
        in_specs=[hbm] * (n + len(late)),
        out_specs=hbm,
        scratch_shapes=[pltpu.VMEM(x.shape, x.dtype) for x in args]
        + [
            pltpu.SemaphoreType.DMA((2 * n,)),
            pltpu.VMEM((width, columns), bf16),
            pltpu.SemaphoreType.DMA((16,)),
        ],
        compiler_params=pltpu.CompilerParams(vmem_limit_bytes=LIMIT * 2**20),
        cost_estimate=pl.CostEstimate(flops=1, bytes_accessed=1, transcendentals=0),
        name="weight_grads",
    )(*hold(args + list(late)))


def plane_sum_kernel(y_ref, moved_ref, own_ref, oth_ref):
    for half, ref in ((y_ref[0], own_ref), (1 - y_ref[0], oth_ref)):
        ref[...] = jnp.sum(moved_ref[:, half].astype(f32), axis=0).astype(ref.dtype)


def last_sums_kernel(
    moved_ref, one_own, one_oth, two_own, two_oth, three_own, three_oth,
    up_ref, down_ref, out_ref, qkv_ref, gains_ref, shifts_ref, up_bias_ref, qv_ref,
):
    one = one_own[...] + one_oth[...].astype(f32)
    two = two_own[...] + two_oth[...].astype(f32)
    three = three_own[...] + three_oth[...].astype(f32)
    width = up_ref.shape[1]
    up_ref[:, :P_ONE] = one
    up_ref[:, P_ONE:] = two[:, : width - P_ONE]
    down_ref[:, :P_TWO] = two[:, width - P_ONE :]

    def summed(first, last):
        return jnp.sum(moved_ref[:, :, first:last].astype(f32), axis=0)

    down_ref[:, P_TWO:] = three[:, : width - P_TWO]
    out_ref[...] = three[:, width - P_TWO :]
    at = 0
    for i in range(3):
        qkv_ref[i] = summed(at + i * LOCAL, at + (i + 1) * LOCAL)
    rows = summed(at + 3 * LOCAL, at + 3 * LOCAL + 128)
    small = rows.T
    gains_ref[0:1, :] = small[0:1]
    gains_ref[1:2, :] = small[2:3]
    shifts_ref[0:1, :] = small[1:2]
    shifts_ref[1:4, :] = small[3:6]
    up_bias_ref[...] = small[6:7]
    qv_ref[0:1, :] = rows[0:1, 16:24]
    qv_ref[1:2, :] = rows[0:1, 24:32]


def per_device(
    tokens,
    sub_blocks,
    w_qkv,
    qv_bias,
    w_out,
    w_up,
    up_bias,
    w_down,
    ln_gains,
    row_biases,
    cotangent,
):
    width = tokens.shape[1]
    ctx = lax.axis_index("ctx").astype(jnp.int32)
    core = (lax.axis_index("tp") % 2).astype(jnp.int32)
    core_s = core.reshape(1)
    y_low = (ctx // 4 % 2).reshape(1)

    def swap(x):
        return lax.ppermute(x, "tp", CORE_SWAP)

    def across(x):
        return lax.ppermute(x, "tp", YHI_SWAP)

    def exchange(x):
        return lax.all_to_all(x, "ctx", 0, 0, tiled=True)

    def plane_exchange(blocks):
        return lax.all_to_all(blocks, "ctx", 0, 0, axis_index_groups=PLANES, tiled=True)

    def plane_sum(moved):
        own, oth = kernel_call(
            plane_sum_kernel,
            [((32, moved.shape[1]), f32), ((32, moved.shape[1]), bf16)],
            name="plane_sum",
        )(y_low, moved.reshape(16, 2, 32, -1))
        return own, lax.ppermute(oth, "ctx", YLO_SWAP)

    own_row = lax.dynamic_index_in_dim(sub_blocks, ctx // 8, 0, False)
    order = jnp.arange(SUBS, dtype=jnp.int32)
    holder = jnp.sum(
        jnp.where(own_row[:, None] == order[None, :], order[:, None], 0), axis=0
    ).astype(jnp.int32)
    scalars = jnp.concatenate([holder, core_s])

    split_tokens = tokens.reshape(GROUPS, 2, HALF, width)
    w_own = w_qkv.transpose(1, 0, 2)
    w_oth = swap(w_own)
    b_oth = swap(qv_bias)
    wo_own = w_out
    wo_oth = swap(w_out)

    first, low_own = kernel_call(
        project_own_kernel,
        [((16, 96, 128), bf16), ((ROWS, width), bf16)],
        name="project_own",
        brought=((1, 4), (2, 3), (3, 1), (4, 1), (5, 1)),
        lazy=True,
    )(core_s, split_tokens, w_own, ln_gains, row_biases, qv_bias)
    (send,) = kernel_call(
        project_oth_kernel,
        [((SUBS, 96, 128), bf16)],
        stored=(0,),
        name="project_oth",
    )(core_s, low_own, w_oth, b_oth, first)
    mine = exchange(send)
    theirs = swap(mine)

    mixed, lse = kernel_call(
        attend_kernel,
        [((SUBS, 32, 128), bf16), ((8, TILE), f32)],
        [((2048, HEAD), bf16), ((4096, HEAD), bf16), ((4096, 128), bf16)],
        stored=(0, 1),
        name="attend",
        brought=((1, 4), (2, 4)),
    )(scalars, mine, theirs)
    mixed_back = exchange(mixed)
    cot_own, cot_oth = kernel_call(
        split_kernel,
        [((ROWS, width), bf16), ((ROWS, width), bf16)],
        stored=(0, 1),
        name="split_rows",
        late=(mixed,),
    )(core_s, cotangent.reshape(GROUPS, 2, HALF, width))
    heads_own, heads_oth, attn_part = kernel_call(
        out_kernel,
        [((ROWS, LOCAL), bf16), ((ROWS, LOCAL), bf16), ((ROWS, width), bf16)],
        stored=(0, 1),
        lazy=True,
        name="project_out",
        late=(cot_own,),
    )(core_s, mixed_back, wo_own, wo_oth)
    attn_recv = across(attn_part)
    residual, normed_two_own = kernel_call(
        second_norm_kernel,
        [((ROWS, width), f32), ((ROWS, width), bf16)],
        stored=(0,),
        lazy=True,
        name="second_norm",
    )(core_s, attn_part, attn_recv, split_tokens, ln_gains, row_biases)
    normed_two_oth = swap(normed_two_own)

    up_here, down_here = fetch(w_up, w_down, heads_own)
    (
        active_own,
        active_oth,
        grad_hidden_own,
        grad_hidden_oth,
        gn_two_own,
        gn_two_oth,
        up_sums,
        mlp_own,
        mlp_oth,
        blocks_one,
    ) = kernel_call(
        feed_kernel,
        [((ROWS, width), bf16)] * 4
        + [((ROWS, width), bf16), ((ROWS, width), bf16), ((1, width), f32)]
        + [((ROWS, width), bf16), ((ROWS, width), bf16), ((width, P_ONE), bf16)],
        scalars=0,
        stored=tuple(range(10)),
        lazy=True,
        name="feed",
    )(normed_two_own, normed_two_oth, cot_own, cot_oth, up_here, up_bias.reshape(8, -1), down_here)
    gn_two_chip = (gn_two_own.astype(f32) + swap(gn_two_oth).astype(f32)).astype(bf16)
    mlp_chip = (mlp_own.astype(f32) + swap(mlp_oth).astype(f32)).astype(bf16)
    up_parts = (normed_two_own, normed_two_oth, grad_hidden_own, grad_hidden_oth)
    down_parts = (cot_own, cot_oth, active_own, active_oth)
    gn_two_recv = across(gn_two_chip)
    moved_one = plane_exchange(blocks_one)
    blocks_two = weight_grads(
        [up_parts + ((P_ONE, width),), down_parts + ((0, P_TWO),)], late=(blocks_one,)
    )

    grad_residual, grad_attn, grad_heads, second_sums = kernel_call(
        residual_grads_kernel,
        [
            ((ROWS, width), f32),
            ((ROWS, width), bf16),
            ((SUBS, 32, 128), bf16),
            ((4, width), f32),
        ],
        stored=(0, 1, 2, 3),
        lazy=True,
        name="residual_grads",
        late=(blocks_two, mlp_chip),
    )(core_s, gn_two_chip, gn_two_recv, residual, cot_own, ln_gains, wo_own, wo_oth)
    grad_mixed = exchange(held(grad_heads, moved_one))

    grad_attn_oth = swap(grad_attn)
    heads_recv = swap(heads_oth)
    moved_two = plane_exchange(blocks_two)

    mlp_recv = across(mlp_chip)

    dq, kept, given = kernel_call(
        attend_back_kernel,
        [((2048, HEAD), bf16), ((2048, 128), f32), ((2048, 128), bf16)],
        [
            ((2048, 128), bf16),
            ((2048, 128), bf16),
            ((4096, 128), bf16),
            ((HEAD, 4096), bf16),
            ((8, TILE), f32),
            ((4096, 128), f32),
        ],
        name="attend_back",
        brought=((1, 4), (2, 4), (3, 2), (4, 2), (5, 1)),
        lazy=True,
    )(scalars, mine, theirs, grad_mixed, mixed, lse)
    (packed,) = kernel_call(
        pack_grads_kernel,
        [((SUBS, 96, 128), bf16)],
        stored=(0,),
        name="pack_grads",
        late=(mlp_recv,),
    )(scalars, dq, kept, swap(given))
    packed = held(packed, moved_two)
    grads_back = exchange(packed)

    blocks_three = weight_grads(
        [
            down_parts + ((P_TWO, width),),
            (grad_attn, grad_attn_oth, heads_own, heads_recv, (0, LOCAL)),
        ],
        late=(packed,),
    )
    second_core = swap(second_sums)
    normed_own, normed_oth = kernel_call(
        first_norm_kernel,
        [((ROWS, width), bf16), ((ROWS, width), bf16)],
        name="first_norm",
        stored=(0, 1),
        late=(packed,),
    )(core_s, split_tokens, ln_gains, row_biases)
    sums_one = plane_sum(moved_one)
    sums_two = plane_sum(moved_two)

    rows_own, rows_oth, gn_one_part = kernel_call(
        token_grads_kernel,
        [((ROWS, 3 * LOCAL), bf16), ((ROWS, 3 * LOCAL), bf16), ((ROWS, width), bf16)],
        stored=(0, 1),
        name="token_grads",
        brought=((1, 4), (2, 3), (3, 3)),
        lazy=True,
    )(core_s, grads_back, w_own, w_oth)
    rows_recv = swap(rows_oth)
    moved_three = plane_exchange(
        held(blocks_three, normed_own, sums_one[1], sums_two[1], second_core)
    )
    (first_sums,) = kernel_call(first_sums_kernel, [((8, width), f32)], name="first_sums")(
        core_s, gn_one_part, split_tokens
    )
    sums_parts = (
        first_sums,
        swap(first_sums),
        across(first_sums),
        lax.ppermute(first_sums, "tp", CROSS_SWAP),
    )
    blocks_last = weight_grads(
        [(normed_own, normed_oth, rows_own, rows_recv, (0, 3 * LOCAL))], planes=False, spare=128
    )
    blocks_last = vector_columns(
        blocks_last, rows_own, rows_recv, *sums_parts, second_sums, second_core, up_sums
    )
    gn_one_recv = across(gn_one_part)
    blocks_last = held(blocks_last, moved_three, gn_one_recv)
    moved_last = exchange(blocks_last)

    layer_own, rms_own = kernel_call(
        layer_kernel,
        [((ROWS, width), f32), ((3, ROWS), f32)],
        scalars=0,
        name="layer_out",
        late=(blocks_last,),
    )(residual, attn_part, attn_recv, mlp_chip, mlp_recv, row_biases)
    layer_out = join_rows(core_s, layer_own, swap(layer_own))
    (rms_rows,) = kernel_call(
        rms_join_kernel, [((3, 2 * ROWS), f32)], name="rms_join"
    )(core_s, rms_own, swap(rms_own))
    (input_own,) = kernel_call(input_grads_kernel, [((ROWS, width), f32)], name="input_grads")(
        core_s, gn_one_part, gn_one_recv, grad_residual, split_tokens, ln_gains
    )
    input_grad = join_rows(core_s, input_own, swap(input_own))
    (
        grad_up,
        grad_down,
        grad_out,
        grad_qkv,
        grad_gains,
        grad_shifts,
        grad_up_bias,
        grad_qv_bias,
    ) = kernel_call(
        last_sums_kernel,
        [
            ((32, width), f32),
            ((32, width), f32),
            ((32, LOCAL), f32),
            ((3, 32, LOCAL), f32),
            ((2, 32), f32),
            ((4, 32), f32),
            ((1, 32), f32),
            ((2, 8), f32),
        ],
        scalars=0,
        name="last_sums",
        late=(layer_out, input_grad, rms_rows),
    )(moved_last.reshape(SUBS, 32, -1), *sums_one, *sums_two, *plane_sum(moved_three))
    return (
        layer_out,
        input_grad,
        rms_rows,
        grad_qkv.transpose(1, 0, 2),
        grad_qv_bias,
        grad_out.T,
        grad_up,
        grad_up_bias[0],
        grad_down.T,
        grad_gains,
        grad_shifts,
    )


def solution(mesh):
    return jax.shard_map(
        per_device,
        mesh=mesh,
        in_specs=(
            P("ctx", None),
            P(),
            P(None, None, "tp"),
            P(None, "tp"),
            P("tp", None),
            P(None, "tp"),
            P("tp"),
            P("tp", None),
            P(),
            P(),
            P("ctx", None),
        ),
        out_specs=(
            P("ctx", None),
            P("ctx", None),
            P(None, "ctx"),
            P("ctx", None, "tp"),
            P(None, ("tp", "ctx")),
            P("tp", "ctx"),
            P("ctx", "tp"),
            P(("tp", "ctx")),
            P("tp", "ctx"),
            P(None, "ctx"),
            P(None, "ctx"),
        ),
        check_vma=False,
    )
```

```python
import jax
import jax.numpy as jnp
from jax import lax
from jax.experimental import pallas as pl
from jax.experimental.pallas import tpu as pltpu
from jax.sharding import PartitionSpec as P

HEAD = 64
SUBS = 32
HALF = 64
GROUPS = 4
ROWS = GROUPS * HALF
LOCAL = 256
P_ONE = 640
P_TWO = 384
LIMIT = 36
TILE = 256
CHUNK = 512
EPSILON = 1e-05
RMS_EPSILON = 1e-06
LOG_SHRINK = 10 * 0.6931471805599453
SHRINK = 2.0**-10
CORE_SWAP = [(0, 1), (1, 0), (2, 3), (3, 2)]
YHI_SWAP = [(0, 2), (2, 0), (1, 3), (3, 1)]
YLO_SWAP = [(j, j ^ 4) for j in range(SUBS)]
CROSS_SWAP = [(0, 3), (3, 0), (1, 2), (2, 1)]
PLANES = [[z * 8 + y * 4 + x for z in range(4) for x in range(4)] for y in range(2)]
NT = (((1,), (1,)), ((), ()))
TN = (((0,), (0,)), ((), ()))
bf16 = jnp.bfloat16
f32 = jnp.float32


def norm_parts(values):
    centre = jnp.mean(values, axis=-1, keepdims=True)
    centred = values - centre
    spread = jnp.mean(centred * centred, axis=-1, keepdims=True)
    inverse = lax.rsqrt(spread + EPSILON)
    return centred * inverse, inverse


def norm_back(grad_normed, unit_rows, inverse, gain):
    grad_unit = grad_normed * gain
    first_mean = jnp.mean(grad_unit, axis=-1, keepdims=True)
    second_mean = jnp.mean(grad_unit * unit_rows, axis=-1, keepdims=True)
    return inverse * (grad_unit - first_mean - unit_rows * second_mean)


def hold(arrays):
    return [pltpu.with_memory_space_constraint(x, pltpu.HBM) for x in arrays]


def order(arrays):
    return [x if x.size * x.dtype.itemsize < 2**18 else hold([x])[0] for x in arrays]


def pieces_of(ref, stage, sems, first, pieces):
    step = ref.shape[0] // pieces
    return [
        pltpu.make_async_copy(
            ref.at[pl.ds(i * step, step)], stage.at[pl.ds(i * step, step)], sems.at[first + i]
        )
        for i in range(pieces)
    ]


def with_copies(body, n_in, n_late, n_out, stored, brought, lazy):
    def kernel(*refs):
        ins, outs = list(refs[:n_in]), list(refs[n_in + n_late : n_in + n_late + n_out])
        rest = refs[n_in + n_late + n_out :]
        arriving = {}
        if brought:
            stages, in_sems, rest = rest[: len(brought)], rest[len(brought)], rest[len(brought) + 1 :]
            first = 0
            for stage, (o, pieces) in zip(stages, brought):
                arriving[o] = pieces_of(ins[o], stage, in_sems, first, pieces)
                ins[o] = stage
                first += pieces
            for copies in arriving.values():
                for copy in copies:
                    copy.start()
        stages, rest = rest[: len(stored)], rest[len(stored) :]
        copies = []
        if stored:
            sems, rest = rest[0], rest[1:]
            copies = [
                pltpu.make_async_copy(stage, outs[o], sems.at[i])
                for i, (stage, o) in enumerate(zip(stages, stored))
            ]
        for stage, o in zip(stages, stored):
            outs[o] = stage
        leaving = dict(zip(stored, copies))
        if lazy:
            body(arriving, leaving, *ins, *outs, *rest)
        else:
            for arrivals in arriving.values():
                for copy in arrivals:
                    copy.wait()
            body(*ins, *outs, *rest)
        for copy in leaving.values():
            copy.start()
        for copy in copies:
            copy.wait()

    return kernel


def kernel_call(
    body, outs, scratch=(), scalars=1, name=None, stored=(), late=(), brought=(), lazy=False, direct=()
):
    smem = pl.BlockSpec(memory_space=pltpu.SMEM)
    vmem = pl.BlockSpec(memory_space=pltpu.VMEM)
    hbm = pl.BlockSpec(memory_space=pltpu.HBM)
    shapes = [x if hasattr(x, "memory_space") or not isinstance(x, tuple) else pltpu.VMEM(*x) for x in scratch]
    if stored:
        shapes = (
            [pltpu.VMEM(*outs[o]) for o in stored]
            + [pltpu.SemaphoreType.DMA((len(stored),))]
            + shapes
        )

    def call(*args):
        args, more, specs = list(args), [], [smem] * scalars + [vmem] * (len(args) - scalars)
        for o, _ in brought:
            specs[o] = hbm
            more.append(pltpu.VMEM(args[o].shape, args[o].dtype))
            (args[o],) = hold([args[o]])
        if brought:
            more.append(pltpu.SemaphoreType.DMA((sum(pieces for _, pieces in brought),)))
        return pl.pallas_call(
            with_copies(body, len(args), len(late), len(outs), stored, brought, lazy),
            out_shape=[
                pltpu.HBM(s, d) if o in stored + direct else jax.ShapeDtypeStruct(s, d)
                for o, (s, d) in enumerate(outs)
            ],
            in_specs=specs + [pl.BlockSpec(memory_space=pl.ANY)] * len(late),
            out_specs=[hbm if o in stored + direct else vmem for o in range(len(outs))],
            scratch_shapes=more + shapes,
            compiler_params=pltpu.CompilerParams(vmem_limit_bytes=LIMIT * 2**20),
            cost_estimate=pl.CostEstimate(flops=1, bytes_accessed=1, transcendentals=0),
            name=name,
        )(*args, *order(late))

    return call


def held(x, *late):
    hbm = pl.BlockSpec(memory_space=pltpu.HBM)
    return pl.pallas_call(
        lambda *refs: None,
        out_shape=pltpu.HBM(x.shape, x.dtype),
        in_specs=[hbm] + [pl.BlockSpec(memory_space=pl.ANY)] * len(late),
        out_specs=hbm,
        input_output_aliases={0: 0},
        cost_estimate=pl.CostEstimate(flops=1, bytes_accessed=1, transcendentals=0),
        name="held",
    )(*hold([x]), *late)


def fold(rows):
    return jnp.concatenate([rows[:32], rows[32:]], axis=1)


def unfold(packed):
    return jnp.concatenate([packed[:, :HEAD], packed[:, HEAD:]], axis=0)


def project_own_kernel(arriving, leaving, core_ref, x_ref, w_ref, gains, shifts, b_ref, send_ref, low_ref):
    for o in (1, 3, 4, 5):
        for copy in arriving[o]:
            copy.wait()
    x = x_ref[:, core_ref[0]].reshape(ROWS, -1).astype(f32)
    unit, _ = norm_parts(x)
    low = (unit * gains[0:1].astype(f32) + shifts[0:1].astype(f32)).astype(bf16)
    low_ref[...] = low
    for w in arriving[2]:
        w.wait()
    for g, h, qk, v in projected(low, w_ref, b_ref):
        send_ref[g * 4 + h, 0:64, :] = qk
        send_ref[g * 4 + h, 64:96, :] = v


def project_oth_kernel(core_ref, low_ref, w_ref, b_ref, first_ref, send_ref):
    core = core_ref[0]
    for g in range(GROUPS):
        for h in range(4):
            send_ref[g * 8 + core * 4 + h] = first_ref[g * 4 + h]
    for g, h, qk, v in projected(low_ref[...], w_ref, b_ref):
        block = g * 8 + (1 - core) * 4 + h
        send_ref[block, 0:64, :] = qk
        send_ref[block, 64:96, :] = v


def projected(low, w_ref, b_ref):
    q = jnp.dot(low, w_ref[0], preferred_element_type=f32) + b_ref[0:1].astype(f32)
    k = jnp.dot(low, w_ref[1], preferred_element_type=f32)
    v = jnp.dot(low, w_ref[2], preferred_element_type=f32) + b_ref[1:2].astype(f32)
    for g in range(GROUPS):
        for h in range(4):
            rows = slice(g * HALF, (g + 1) * HALF)
            cols = slice(h * HEAD, (h + 1) * HEAD)
            qk = jnp.concatenate([q[rows, cols], k[rows, cols]], axis=1)
            yield g, h, qk.astype(bf16), fold(v[rows, cols]).astype(bf16)


def pair_masks(core, transposed):
    shape = (CHUNK, TILE) if transposed else (TILE, CHUNK)
    q = lax.broadcasted_iota(jnp.int32, shape, 1 if transposed else 0)
    key = lax.broadcasted_iota(jnp.int32, shape, 0 if transposed else 1)
    other = key >= TILE
    k = jnp.where(other, key - TILE, key)
    q_sub = lax.shift_right_logical(q, 6)
    k_sub = lax.shift_right_logical(k, 6)
    prompt = (other & (q_sub + core > k_sub)) | (jnp.logical_not(other) & (q >= k))
    cont = prompt & (lax.shift_right_logical(q, 7) == lax.shift_right_logical(k, 7))
    return prompt, cont


def chunks_of(tile, prompt, cont):
    if tile < 4:
        return [(j, None) for j in range(tile)] + [(tile, prompt)]
    return [(j, None) for j in range(4)] + [(tile, cont)]


def places(sc_ref, d):
    p = sc_ref[SUBS + 1 + d]
    at = lax.shift_right_logical(p, 2) * CHUNK + (p & 3) * HALF
    return pl.ds(pl.multiple_of(p * HALF, HALF), HALF), pl.multiple_of(at, HALF)


def attend_kernel(
    sc_ref, own_ref, oth_ref, own_kept, oth_kept, out_ref, lse_ref, q_s, k_s, v_s, kept_sems
):
    keeping = [
        pltpu.make_async_copy(ref, kept, kept_sems.at[i])
        for i, (ref, kept) in enumerate(((own_ref, own_kept), (oth_ref, oth_kept)))
    ]
    for copy in keeping:
        copy.start()
    core = sc_ref[SUBS]
    const = jnp.full((HALF, HEAD), SHRINK, bf16)
    for p in range(SUBS):
        d = sc_ref[p]
        at = p // 4 * CHUNK + p % 4 * HALF
        q_s[p * HALF : (p + 1) * HALF, :] = own_ref[d, 0:64, :HEAD] * jnp.asarray(0.125, bf16)
        for ref, start in ((own_ref, at), (oth_ref, at + TILE)):
            k_s[start : start + HALF, :] = ref[d, 0:64, HEAD:]
            v = unfold(ref[d, 64:96, :]) * jnp.asarray(SHRINK, bf16)
            v_s[start : start + HALF, :] = jnp.concatenate([v, const], axis=1)
    prompt, cont = pair_masks(core, False)
    for t in range(8):
        q = q_s[t * TILE : (t + 1) * TILE, :]
        total = None
        for j, mask in chunks_of(t, prompt, cont):
            keys = slice(j * CHUNK, (j + 1) * CHUNK)
            s = lax.dot_general(q, k_s[keys, :], NT, preferred_element_type=f32)
            w = jnp.exp(s)
            if mask is not None:
                w = jnp.where(mask, w, 0.0)
            part = jnp.dot(w.astype(bf16), v_s[keys, :], preferred_element_type=f32)
            total = part if total is None else total + part
        mixed = total[:, :HEAD] / total[:, HEAD:]
        lse_ref[t : t + 1, :] = jnp.log(total.T[HEAD : HEAD + 1, :]) + LOG_SHRINK
        for i in range(4):
            out_ref[sc_ref[t * 4 + i]] = fold(mixed[i * HALF : (i + 1) * HALF]).astype(bf16)
    for copy in keeping:
        copy.wait()


def attend_back_kernel(
    arriving, leaving, sc_ref, own_ref, oth_ref, do_ref, o_ref, lse_ref,
    dq_ref, keep_ref, send_ref,
    q_s, do_s, vk_s, kt_s, inner_s, acc_s,
):
    core = sc_ref[SUBS]
    zero = jnp.zeros((HALF, HEAD), bf16)
    for o, ref, shift in ((1, own_ref, 0), (2, oth_ref, TILE)):
        for d in range(SUBS):
            if d % 8 == 0:
                arriving[o][d // 8].wait()
            rows, at = places(sc_ref, d)
            if o == 1:
                q = ref[d, 0:64, :HEAD] * jnp.asarray(0.125, bf16)
                q_s[rows, :] = jnp.concatenate([zero, q], axis=1)
            vk_s[pl.ds(at + shift, HALF), :] = jnp.concatenate(
                [unfold(ref[d, 64:96, :]), ref[d, 0:64, HEAD:]], axis=1
            )
    for d in range(SUBS):
        if d % 16 == 0:
            arriving[3][d // 16].wait()
        rows, _ = places(sc_ref, d)
        do_s[rows, :] = jnp.concatenate([unfold(do_ref[d]), zero], axis=1)
    for j in range(8):
        keys = slice(j * CHUNK, (j + 1) * CHUNK)
        kt_s[:, keys] = vk_s[keys, :].T[HEAD:, :]
    for o in (4, 5):
        for copy in arriving[o]:
            copy.wait()
    for t in range(8):
        both = []
        for i in range(4):
            d = sc_ref[t * 4 + i]
            both.append(unfold(do_ref[d].astype(f32) * o_ref[d].astype(f32)))
        inner_s[t : t + 1, :] = jnp.sum(jnp.concatenate(both, axis=0).T, axis=0, keepdims=True)
    prompt, cont = pair_masks(core, True)
    started = set()
    for t in range(8):
        tile = slice(t * TILE, (t + 1) * TILE)
        q = q_s[tile, :]
        grad = do_s[tile, :]
        lse = lse_ref[t : t + 1, :]
        inner = inner_s[t : t + 1, :]
        dq = None
        for j, mask in chunks_of(t, prompt, cont):
            keys = slice(j * CHUNK, (j + 1) * CHUNK)
            vk = vk_s[keys, :]
            s = lax.dot_general(vk, q, NT, preferred_element_type=f32)
            a = jnp.exp(s - lse)
            if mask is not None:
                a = jnp.where(mask, a, 0.0)
            dp = lax.dot_general(vk, grad, NT, preferred_element_type=f32)
            ds = (a * (dp - inner)).astype(bf16)
            part = jnp.dot(a.astype(bf16), grad, preferred_element_type=f32) + jnp.dot(
                ds, q, preferred_element_type=f32
            )
            if j in started:
                acc_s[keys, :] += part
            else:
                acc_s[keys, :] = part
                started.add(j)
            dq_part = jnp.dot(kt_s[:, keys], ds, preferred_element_type=f32)
            dq = dq_part if dq is None else dq + dq_part
        dq_ref[tile, :] = (dq * 0.125).T.astype(bf16)
    for j in range(8):
        keep_ref[j * TILE : (j + 1) * TILE, :] = acc_s[j * CHUNK : j * CHUNK + TILE, :]
        send_ref[j * TILE : (j + 1) * TILE, :] = acc_s[
            j * CHUNK + TILE : (j + 1) * CHUNK, :
        ].astype(bf16)


def pack_grads_kernel(sc_ref, dq_ref, keep_ref, recv_ref, out_ref):
    for p in range(SUBS):
        rows = slice(p * HALF, (p + 1) * HALF)
        summed = (keep_ref[rows, :] + recv_ref[rows, :].astype(f32)).astype(bf16)
        d = sc_ref[p]
        out_ref[d, 0:64, :] = jnp.concatenate([dq_ref[rows, :], summed[:, HEAD:]], axis=1)
        out_ref[d, 64:96, :] = fold(summed[:, :HEAD])


def out_kernel(
    arriving, leaving, core_ref, recv_ref, own_w, oth_w, own_ref, oth_ref, part_ref
):
    core = core_ref[0]
    for half, ref in ((core, own_ref), (1 - core, oth_ref)):
        for g in range(GROUPS):
            heads = [unfold(recv_ref[g * 8 + half * 4 + h]) for h in range(4)]
            ref[g * HALF : (g + 1) * HALF, :] = jnp.concatenate(heads, axis=1)
    for o in (0, 1):
        leaving.pop(o).start()
    part = jnp.dot(own_ref[...], own_w[...], preferred_element_type=f32) + jnp.dot(
        oth_ref[...], oth_w[...], preferred_element_type=f32
    )
    part_ref[...] = part.astype(bf16)


def split_kernel(core_ref, rows_ref, own_ref, oth_ref):
    own_ref[...] = rows_ref[:, core_ref[0]].reshape(own_ref.shape)
    oth_ref[...] = rows_ref[:, 1 - core_ref[0]].reshape(oth_ref.shape)


def first_norm_kernel(core_ref, x_ref, gains, shifts, own_ref, oth_ref):
    for half, low_ref in ((core_ref[0], own_ref), (1 - core_ref[0], oth_ref)):
        unit, _ = norm_parts(x_ref[:, half].reshape(ROWS, -1).astype(f32))
        low_ref[...] = (unit * gains[0:1].astype(f32) + shifts[0:1].astype(f32)).astype(bf16)


def layer_kernel(
    residual_ref, part_ref, part_recv_ref, mlp_ref, mlp_recv_ref, shifts, layer_ref, rms_ref
):
    attn = (part_ref[...].astype(f32) + part_recv_ref[...].astype(f32)) + shifts[1:2].astype(f32)
    mlp = (mlp_ref[...].astype(f32) + mlp_recv_ref[...].astype(f32)) + shifts[3:4].astype(f32)
    layer = residual_ref[...] + mlp
    layer_ref[...] = layer
    for i, rows in enumerate((layer, attn, mlp)):
        squares = rows * rows
        folded = sum(squares[:, c : c + 128] for c in range(0, squares.shape[1], 128))
        mean = jnp.sum(folded.T, axis=0, keepdims=True) / squares.shape[1]
        rms_ref[i : i + 1, :] = jnp.sqrt(mean + RMS_EPSILON)


def rms_join_kernel(core_ref, own_ref, oth_ref, out_ref):
    first = core_ref[0] == 0
    own, oth = own_ref[...], oth_ref[...]
    low, high = jnp.where(first, own, oth), jnp.where(first, oth, own)
    pieces = []
    for g in range(GROUPS):
        pieces += [rows[:, g * HALF : (g + 1) * HALF] for rows in (low, high)]
    out_ref[...] = jnp.concatenate(pieces, axis=1)


def second_norm_kernel(
    arriving, leaving, core_ref, part_ref, recv_ref, x_ref, gains, shifts, residual_ref, low_ref
):
    x = x_ref[:, core_ref[0]].reshape(ROWS, -1).astype(f32)
    branch = (part_ref[...].astype(f32) + recv_ref[...].astype(f32)) + shifts[1:2].astype(f32)
    residual = x + branch
    residual_ref[...] = residual
    leaving.pop(0).start()
    unit, _ = norm_parts(residual)
    low_ref[...] = (unit * gains[1:2].astype(f32) + shifts[2:3].astype(f32)).astype(bf16)


def put_blocks(stage, to, made, planes):
    if planes:
        for j in range(SUBS):
            at = (j // 8 * 8 + j % 4 * 2 + j // 4 % 2) * 32
            stage[at : at + 32, to] = made[j * 32 : (j + 1) * 32]
    else:
        stage[:, to] = made


def fetch_kernel(first_ref, second_ref, first_out, second_out, done_ref, sems):
    done_ref[...] = jnp.zeros_like(done_ref)
    copies = []
    for i, (ref, out) in enumerate(((first_ref, first_out), (second_ref, second_out))):
        for j in range(4):
            rows = pl.ds(j * 256, 256)
            copies.append(pltpu.make_async_copy(ref.at[rows], out.at[rows], sems.at[4 * i + j]))
    for copy in copies:
        copy.start()
    for copy in copies:
        copy.wait()


def fetch(first, second, late):
    hbm = pl.BlockSpec(memory_space=pltpu.HBM)
    vmem = pl.BlockSpec(memory_space=pltpu.VMEM)
    return pl.pallas_call(
        lambda a, b, unused, *rest: fetch_kernel(a, b, *rest),
        out_shape=[pltpu.VMEM(x.shape, x.dtype) for x in (first, second)]
        + [jax.ShapeDtypeStruct((8, 128), f32)],
        in_specs=[hbm] * 3,
        out_specs=[vmem] * 3,
        scratch_shapes=[pltpu.SemaphoreType.DMA((8,))],
        compiler_params=pltpu.CompilerParams(vmem_limit_bytes=LIMIT * 2**20),
        cost_estimate=pl.CostEstimate(flops=1, bytes_accessed=1, transcendentals=0),
        name="fetch",
    )(*hold((first, second, late)))


def feed_half(rows_ref, cot_ref, up_ref, bias_ref, down_ref, active_ref, grad_ref, back_ref, sums_ref):
    total = None
    for c in range(4):
        cols = slice(c * 256, (c + 1) * 256)
        up = up_ref[:, cols]
        bias = jnp.concatenate([bias_ref[2 * c + b : 2 * c + b + 1] for b in range(2)], axis=1)
        hidden = jnp.dot(rows_ref[...], up, preferred_element_type=f32) + bias.astype(f32)
        grad_active = lax.dot_general(
            cot_ref[...], down_ref[cols, :], NT, preferred_element_type=f32
        )
        share = 0.5 + 0.5 * lax.erf(hidden * 0.7071067811865476)
        density = jnp.exp(hidden * hidden * -0.5) * 0.3989422804014327
        active_ref[:, cols] = (hidden * share).astype(bf16)
        grad = (grad_active * (share + hidden * density)).astype(bf16)
        grad_ref[:, cols] = grad
        sums_ref[0:1, cols] = jnp.sum(grad.astype(f32), axis=0, keepdims=True)
        part = lax.dot_general(grad, up, NT, preferred_element_type=f32)
        total = part if total is None else total + part
    back_ref[...] = total.astype(back_ref.dtype)


def feed_own_kernel(arriving, leaving, *refs):
    feed_half(*refs)


def feed_oth_kernel(
    arriving, leaving, rows_ref, cot_ref, up_ref, bias_ref, down_ref, own_ref, own_grad,
    active_ref, grad_ref, back_ref, sums_ref, blocks_ref,
):
    feed_half(
        rows_ref, cot_ref, up_ref, bias_ref, down_ref, active_ref, grad_ref, back_ref, sums_ref
    )
    for o in range(4):
        leaving.pop(o).start()
    for copy in arriving[6]:
        copy.wait()
    for c in range(0, P_ONE, 256):
        cols = slice(c, min(c + 256, P_ONE))
        made = lax.dot_general(own_ref[...], own_grad[:, cols], TN, preferred_element_type=f32)
        made += lax.dot_general(rows_ref[...], grad_ref[:, cols], TN, preferred_element_type=f32)
        put_blocks(blocks_ref, cols, made.astype(bf16), True)
    leaving.pop(4).start()


def feed_out_kernel(arriving, leaving, own_ref, oth_ref, down_ref, own_out, oth_out):
    for o in (0, 1, 2):
        for copy in arriving[o]:
            copy.wait()
    for o, ref, out_ref in ((0, own_ref, own_out), (1, oth_ref, oth_out)):
        made = jnp.dot(ref[...], down_ref[...], preferred_element_type=f32)
        out_ref[...] = made.astype(bf16)
        leaving.pop(o).start()


def residual_grads_kernel(
    arriving, leaving, core_ref, own_ref, recv_ref, residual_ref, cot_ref, gains, own_w, oth_w,
    grad_ref, low_ref, send_ref, sums_ref,
):
    core = core_ref[0]
    unit, inverse = norm_parts(residual_ref[...])
    grad_normed = own_ref[...].astype(f32) + recv_ref[...].astype(f32)
    cot = cot_ref[...].astype(f32)
    grad = cot + norm_back(grad_normed, unit, inverse, gains[1:2].astype(f32))
    grad_ref[...] = grad
    low = grad.astype(bf16)
    low_ref[...] = low
    sums = [grad_normed * unit, low.astype(f32), grad_normed, cot]
    for i, rows in enumerate(sums):
        sums_ref[i : i + 1, :] = jnp.sum(rows, axis=0, keepdims=True)
    for o in (0, 1, 3):
        leaving.pop(o).start()
    for half, w_ref in ((core, own_w), (1 - core, oth_w)):
        made = lax.dot_general(low, w_ref[...], NT, preferred_element_type=f32)
        for g in range(GROUPS):
            for h in range(4):
                block = made[g * HALF : (g + 1) * HALF, h * HEAD : (h + 1) * HEAD]
                send_ref[g * 8 + half * 4 + h] = fold(block).astype(bf16)


def token_grads_kernel(arriving, leaving, core_ref, recv_ref, own_w, oth_w, own_ref, oth_ref, part_ref):
    core = core_ref[0]
    part = None
    for copy in arriving[1]:
        copy.wait()
    for half, w_ref, ref in ((core, own_w, own_ref), (1 - core, oth_w, oth_ref)):
        for g in range(GROUPS):
            rows = slice(g * HALF, (g + 1) * HALF)
            blocks = [recv_ref.at[g * 8 + half * 4 + h] for h in range(4)]
            pieces = (
                [b[0:64, :HEAD] for b in blocks]
                + [b[0:64, HEAD:] for b in blocks]
                + [unfold(b[64:96, :]) for b in blocks]
            )
            ref[rows, :] = jnp.concatenate(pieces, axis=1)
        leaving.pop(0 if ref is own_ref else 1).start()
        for i in range(3):
            arriving[2 if w_ref is own_w else 3][i].wait()
            made = lax.dot_general(
                ref[:, i * LOCAL : (i + 1) * LOCAL], w_ref[i], NT, preferred_element_type=f32
            )
            part = made if part is None else part + made
    part_ref[...] = part.astype(bf16)


def first_sums_kernel(core_ref, part_ref, x_ref, sums_ref):
    unit, _ = norm_parts(x_ref[:, core_ref[0]].reshape(ROWS, -1).astype(f32))
    part = part_ref[...].astype(f32)
    sums_ref[0:1, :] = jnp.sum(part * unit, axis=0, keepdims=True)
    sums_ref[1:2, :] = jnp.sum(part, axis=0, keepdims=True)
    sums_ref[2:8, :] = jnp.zeros((6, part.shape[1]), f32)


def input_grads_kernel(core_ref, part_ref, recv_ref, grad_ref, x_ref, gains, out_ref):
    x = x_ref[:, core_ref[0]].reshape(ROWS, -1).astype(f32)
    unit, inverse = norm_parts(x)
    grad_normed = part_ref[...].astype(f32) + recv_ref[...].astype(f32)
    out_ref[...] = grad_ref[...] + norm_back(grad_normed, unit, inverse, gains[0:1].astype(f32))


def join_kernel(core_ref, own_ref, oth_ref, out_ref, sems):
    core = core_ref[0]
    copies = []
    for i, (ref, half) in enumerate(((own_ref, core), (oth_ref, 1 - core))):
        for g in range(GROUPS):
            rows = pl.ds(g * HALF, HALF)
            at = i * GROUPS + g
            copies.append(pltpu.make_async_copy(ref.at[rows], out_ref.at[g, half], sems.at[at]))
    for copy in copies:
        copy.start()
    for copy in copies:
        copy.wait()


def join_rows(core_s, own, oth):
    width = own.shape[1]
    vmem = pl.BlockSpec(memory_space=pltpu.VMEM)
    joined = pl.pallas_call(
        join_kernel,
        out_shape=pltpu.HBM((GROUPS, 2, HALF, width), own.dtype),
        in_specs=[pl.BlockSpec(memory_space=pltpu.SMEM), vmem, vmem],
        out_specs=pl.BlockSpec(memory_space=pltpu.HBM),
        scratch_shapes=[pltpu.SemaphoreType.DMA((2 * GROUPS,))],
        compiler_params=pltpu.CompilerParams(vmem_limit_bytes=8 * 2**20),
        cost_estimate=pl.CostEstimate(flops=1, bytes_accessed=1, transcendentals=0),
        name="join_rows",
    )(core_s, own, oth)
    return joined.reshape(2 * ROWS, width)


def weight_grads_kernel(spans, planes, arriving, *refs):
    out_ref, stage, sems = refs[-3:]
    copies = []

    def send(start, stop):
        copies.append(
            pltpu.make_async_copy(
                stage.at[:, pl.ds(start, stop - start)],
                out_ref.at[:, pl.ds(start, stop - start)],
                sems.at[len(copies)],
            )
        )
        copies[-1].start()

    start = 0
    for i, (first, last) in enumerate(spans):
        a_own, a_oth, b_own, b_oth = refs[4 * i : 4 * i + 4]
        for o in range(4 * i, 4 * i + 4):
            for copy in arriving[o]:
                copy.wait()
        for c in range(first, last, 256):
            cols = slice(c, min(c + 256, last))
            made = lax.dot_general(a_own[...], b_own[:, cols], TN, preferred_element_type=f32)
            made += lax.dot_general(a_oth[...], b_oth[:, cols], TN, preferred_element_type=f32)
            stop = start + cols.stop - cols.start
            put_blocks(stage, slice(start, stop), made.astype(bf16), planes)
            send(start, stop)
            start = stop
    for copy in copies:
        copy.wait()


def vector_columns_kernel(
    into_ref, own_rows, oth_rows, own, core, across, cross, second, second_core, up_own, up_oth,
    out_ref, stage, sem,
):
    width = up_own.shape[1]
    rows = ((own[...] + core[...]) + (across[...] + cross[...]))[0:2]
    rows = [rows, second[...] + second_core[...], up_own[...] + up_oth[...], jnp.zeros((121, width), f32)]
    rows = jnp.concatenate(rows, axis=0).T
    owner = lax.broadcasted_iota(jnp.int32, (width, LOCAL), 0) // (width // SUBS)
    feature = lax.broadcasted_iota(jnp.int32, (width, LOCAL), 1)
    at = lax.broadcasted_iota(jnp.int32, (LOCAL, 128), 1)
    wanted = lax.broadcasted_iota(jnp.int32, (LOCAL, 128), 0) % 8
    for first, place in ((0, 16), (2 * LOCAL, 24)):
        cols = slice(first, first + LOCAL)
        sums = jnp.sum(own_rows[:, cols].astype(f32), axis=0, keepdims=True)
        sums += jnp.sum(oth_rows[:, cols].astype(f32), axis=0, keepdims=True)
        mine = jnp.where(owner == feature // 8, sums, 0.0).astype(bf16)
        pick = jnp.where(at == wanted + place, 1.0, 0.0).astype(bf16)
        rows += jnp.dot(mine, pick, preferred_element_type=f32)
    stage[...] = rows.astype(bf16)
    copy = pltpu.make_async_copy(stage, out_ref.at[:, pl.ds(3 * LOCAL, 128)], sem)
    copy.start()
    copy.wait()


def vector_columns(into, *arrays):
    hbm = pl.BlockSpec(memory_space=pltpu.HBM)
    vmem = pl.BlockSpec(memory_space=pltpu.VMEM)
    return pl.pallas_call(
        vector_columns_kernel,
        out_shape=pltpu.HBM(into.shape, into.dtype),
        in_specs=[hbm] + [vmem] * len(arrays),
        out_specs=hbm,
        scratch_shapes=[pltpu.VMEM((into.shape[0], 128), bf16), pltpu.SemaphoreType.DMA(())],
        input_output_aliases={0: 0},
        compiler_params=pltpu.CompilerParams(vmem_limit_bytes=LIMIT * 2**20),
        cost_estimate=pl.CostEstimate(flops=1, bytes_accessed=1, transcendentals=0),
        name="vector_columns",
    )(*hold([into]), *arrays)


def weight_grads(parts, late=(), planes=True, spare=0):
    width = parts[0][0].shape[1]
    spans = [p[4] for p in parts]
    args = [x for p in parts for x in p[:4]]
    columns = sum(last - first for first, last in spans)
    hbm = pl.BlockSpec(memory_space=pltpu.HBM)
    n = len(args)

    def body(*refs):
        out_ref, rest = refs[n + len(late)], refs[n + len(late) + 1 :]
        stages, in_sems, stage, sems = rest[:n], rest[n], rest[n + 1], rest[n + 2]
        arriving = [pieces_of(refs[i], stages[i], in_sems, 2 * i, 2) for i in range(n)]
        for copies in arriving:
            for copy in copies:
                copy.start()
        weight_grads_kernel(spans, planes, arriving, *stages, out_ref, stage, sems)

    return pl.pallas_call(
        body,
        out_shape=pltpu.HBM((width, columns + spare), bf16),
        in_specs=[hbm] * (n + len(late)),
        out_specs=hbm,
        scratch_shapes=[pltpu.VMEM(x.shape, x.dtype) for x in args]
        + [
            pltpu.SemaphoreType.DMA((2 * n,)),
            pltpu.VMEM((width, columns), bf16),
            pltpu.SemaphoreType.DMA((16,)),
        ],
        compiler_params=pltpu.CompilerParams(vmem_limit_bytes=LIMIT * 2**20),
        cost_estimate=pl.CostEstimate(flops=1, bytes_accessed=1, transcendentals=0),
        name="weight_grads",
    )(*hold(args + list(late)))


def plane_sum_kernel(y_ref, moved_ref, own_ref, oth_ref):
    for half, ref in ((y_ref[0], own_ref), (1 - y_ref[0], oth_ref)):
        ref[...] = jnp.sum(moved_ref[:, half].astype(f32), axis=0).astype(ref.dtype)


def last_sums_kernel(
    moved_ref, one_own, one_oth, two_own, two_oth, three_own, three_oth,
    up_ref, down_ref, out_ref, qkv_ref, gains_ref, shifts_ref, up_bias_ref, qv_ref,
):
    one = one_own[...] + one_oth[...].astype(f32)
    two = two_own[...] + two_oth[...].astype(f32)
    three = three_own[...] + three_oth[...].astype(f32)
    width = up_ref.shape[1]
    up_ref[:, :P_ONE] = one
    up_ref[:, P_ONE:] = two[:, : width - P_ONE]
    down_ref[:, :P_TWO] = two[:, width - P_ONE :]

    def summed(first, last):
        return jnp.sum(moved_ref[:, :, first:last].astype(f32), axis=0)

    down_ref[:, P_TWO:] = three[:, : width - P_TWO]
    out_ref[...] = three[:, width - P_TWO :]
    at = 0
    for i in range(3):
        qkv_ref[i] = summed(at + i * LOCAL, at + (i + 1) * LOCAL)
    rows = summed(at + 3 * LOCAL, at + 3 * LOCAL + 128)
    small = rows.T
    gains_ref[0:1, :] = small[0:1]
    gains_ref[1:2, :] = small[2:3]
    shifts_ref[0:1, :] = small[1:2]
    shifts_ref[1:4, :] = small[3:6]
    up_bias_ref[...] = small[6:7]
    qv_ref[0:1, :] = rows[0:1, 16:24]
    qv_ref[1:2, :] = rows[0:1, 24:32]


def per_device(
    tokens,
    sub_blocks,
    w_qkv,
    qv_bias,
    w_out,
    w_up,
    up_bias,
    w_down,
    ln_gains,
    row_biases,
    cotangent,
):
    width = tokens.shape[1]
    ctx = lax.axis_index("ctx").astype(jnp.int32)
    core = (lax.axis_index("tp") % 2).astype(jnp.int32)
    core_s = core.reshape(1)
    y_low = (ctx // 4 % 2).reshape(1)

    def swap(x):
        return lax.ppermute(x, "tp", CORE_SWAP)

    def across(x):
        return lax.ppermute(x, "tp", YHI_SWAP)

    def exchange(x):
        return lax.all_to_all(x, "ctx", 0, 0, tiled=True)

    def plane_exchange(blocks):
        return lax.all_to_all(blocks, "ctx", 0, 0, axis_index_groups=PLANES, tiled=True)

    def plane_sum(moved):
        own, oth = kernel_call(
            plane_sum_kernel,
            [((32, moved.shape[1]), f32), ((32, moved.shape[1]), bf16)],
            name="plane_sum",
            brought=((1, 4),),
        )(y_low, moved.reshape(16, 2, 32, -1))
        return own, lax.ppermute(oth, "ctx", YLO_SWAP)

    own_row = lax.dynamic_index_in_dim(sub_blocks, ctx // 8, 0, False)
    order = jnp.arange(SUBS, dtype=jnp.int32)
    holder = jnp.sum(
        jnp.where(own_row[:, None] == order[None, :], order[:, None], 0), axis=0
    ).astype(jnp.int32)
    scalars = jnp.concatenate([holder, core_s, own_row])

    split_tokens = tokens.reshape(GROUPS, 2, HALF, width)
    w_own = w_qkv.transpose(1, 0, 2)
    w_oth = swap(w_own)
    b_oth = swap(qv_bias)
    wo_own = w_out
    wo_oth = swap(w_out)

    first, low_own = kernel_call(
        project_own_kernel,
        [((16, 96, 128), bf16), ((ROWS, width), bf16)],
        name="project_own",
        brought=((1, 4), (2, 3), (3, 1), (4, 1), (5, 1)),
        lazy=True,
    )(core_s, split_tokens, w_own, ln_gains, row_biases, qv_bias)
    (send,) = kernel_call(
        project_oth_kernel,
        [((SUBS, 96, 128), bf16)],
        stored=(0,),
        name="project_oth",
    )(core_s, low_own, w_oth, b_oth, first)
    mine = exchange(send)
    theirs = swap(mine)

    mine, theirs, mixed, lse = kernel_call(
        attend_kernel,
        [
            ((SUBS, 96, 128), bf16),
            ((SUBS, 96, 128), bf16),
            ((SUBS, 32, 128), bf16),
            ((8, TILE), f32),
        ],
        [
            pltpu.VMEM((2048, HEAD), bf16),
            pltpu.VMEM((4096, HEAD), bf16),
            pltpu.VMEM((4096, 128), bf16),
            pltpu.SemaphoreType.DMA((2,)),
        ],
        name="attend",
        stored=(2, 3),
        direct=(0, 1),
    )(scalars, mine, theirs)
    mixed_back = exchange(mixed)
    cot_own, cot_oth = kernel_call(
        split_kernel,
        [((ROWS, width), bf16), ((ROWS, width), bf16)],
        stored=(0, 1),
        name="split_rows",
        late=(mixed,),
    )(core_s, cotangent.reshape(GROUPS, 2, HALF, width))
    heads_own, heads_oth, attn_part = kernel_call(
        out_kernel,
        [((ROWS, LOCAL), bf16), ((ROWS, LOCAL), bf16), ((ROWS, width), bf16)],
        stored=(0, 1),
        lazy=True,
        name="project_out",
        late=(cot_own,),
    )(core_s, mixed_back, wo_own, wo_oth)
    attn_recv = across(attn_part)
    up_here, down_here, fetched = fetch(w_up, w_down, heads_own)
    residual, normed_two_own = kernel_call(
        second_norm_kernel,
        [((ROWS, width), f32), ((ROWS, width), bf16)],
        stored=(0,),
        lazy=True,
        name="second_norm",
        late=(fetched,),
    )(core_s, attn_part, attn_recv, split_tokens, ln_gains, row_biases)
    normed_two_oth = swap(normed_two_own)

    half_outs = [((ROWS, width), bf16)] * 3 + [((1, width), f32)]
    bias_rows = up_bias.reshape(8, -1)
    active_own, grad_hidden_own, gn_two_own, up_sums_own = kernel_call(
        feed_own_kernel, half_outs, scalars=0, stored=(0, 1, 2, 3), lazy=True, name="feed_own"
    )(normed_two_own, cot_own, up_here, bias_rows, down_here)
    active_oth, grad_hidden_oth, gn_two_oth, up_sums_oth, blocks_one = kernel_call(
        feed_oth_kernel,
        half_outs + [((width, P_ONE), bf16)],
        scalars=0,
        stored=(0, 1, 2, 3, 4),
        brought=((6, 2),),
        lazy=True,
        name="feed_oth",
    )(normed_two_oth, cot_oth, up_here, bias_rows, down_here, normed_two_own, grad_hidden_own)
    gn_two_chip = (gn_two_own.astype(f32) + swap(gn_two_oth).astype(f32)).astype(bf16)
    up_parts = (normed_two_own, normed_two_oth, grad_hidden_own, grad_hidden_oth)
    down_parts = (cot_own, cot_oth, active_own, active_oth)
    gn_two_recv = across(gn_two_chip)
    moved_one = plane_exchange(blocks_one)
    blocks_two = weight_grads(
        [up_parts + ((P_ONE, width),), down_parts + ((0, P_TWO),)], late=(blocks_one,)
    )

    mlp_own, mlp_oth = kernel_call(
        feed_out_kernel,
        [((ROWS, width), bf16), ((ROWS, width), bf16)],
        scalars=0,
        stored=(0, 1),
        brought=((0, 2), (1, 2), (2, 4)),
        lazy=True,
        name="feed_out",
    )(active_own, active_oth, w_down)

    grad_residual, grad_attn, grad_heads, second_sums = kernel_call(
        residual_grads_kernel,
        [
            ((ROWS, width), f32),
            ((ROWS, width), bf16),
            ((SUBS, 32, 128), bf16),
            ((4, width), f32),
        ],
        stored=(0, 1, 2, 3),
        lazy=True,
        name="residual_grads",
        late=(blocks_two, mlp_own),
    )(core_s, gn_two_chip, gn_two_recv, residual, cot_own, ln_gains, wo_own, wo_oth)
    grad_mixed = exchange(held(grad_heads, moved_one))

    grad_attn_oth = swap(grad_attn)
    heads_recv = swap(heads_oth)
    mlp_chip = (mlp_own.astype(f32) + swap(mlp_oth).astype(f32)).astype(bf16)
    mlp_recv = across(mlp_chip)
    moved_two = plane_exchange(held(blocks_two, mlp_chip))


    dq, kept, given = kernel_call(
        attend_back_kernel,
        [((2048, HEAD), bf16), ((2048, 128), f32), ((2048, 128), bf16)],
        [
            ((2048, 128), bf16),
            ((2048, 128), bf16),
            ((4096, 128), bf16),
            ((HEAD, 4096), bf16),
            ((8, TILE), f32),
            ((4096, 128), f32),
        ],
        name="attend_back",
        brought=((1, 4), (2, 4), (3, 2), (4, 2), (5, 1)),
        lazy=True,
    )(scalars, mine, theirs, grad_mixed, mixed, lse)
    (packed,) = kernel_call(
        pack_grads_kernel,
        [((SUBS, 96, 128), bf16)],
        stored=(0,),
        name="pack_grads",
        late=(mlp_recv,),
    )(scalars, dq, kept, swap(given))
    packed = held(packed, moved_two)
    grads_back = exchange(packed)

    blocks_three = weight_grads(
        [
            down_parts + ((P_TWO, width),),
            (grad_attn, grad_attn_oth, heads_own, heads_recv, (0, LOCAL)),
        ],
        late=(packed,),
    )
    second_core = swap(second_sums)
    normed_own, normed_oth = kernel_call(
        first_norm_kernel,
        [((ROWS, width), bf16), ((ROWS, width), bf16)],
        name="first_norm",
        stored=(0, 1),
        late=(packed,),
    )(core_s, split_tokens, ln_gains, row_biases)
    sums_one = plane_sum(moved_one)
    sums_two = plane_sum(moved_two)

    rows_own, rows_oth, gn_one_part = kernel_call(
        token_grads_kernel,
        [((ROWS, 3 * LOCAL), bf16), ((ROWS, 3 * LOCAL), bf16), ((ROWS, width), bf16)],
        stored=(0, 1),
        name="token_grads",
        brought=((1, 4), (2, 3), (3, 3)),
        lazy=True,
    )(core_s, grads_back, w_own, w_oth)
    rows_recv = swap(rows_oth)
    moved_three = plane_exchange(
        held(blocks_three, normed_own, sums_one[1], sums_two[1], second_core)
    )
    (first_sums,) = kernel_call(first_sums_kernel, [((8, width), f32)], name="first_sums")(
        core_s, gn_one_part, split_tokens
    )
    sums_parts = (
        first_sums,
        swap(first_sums),
        across(first_sums),
        lax.ppermute(first_sums, "tp", CROSS_SWAP),
    )
    blocks_last = weight_grads(
        [(normed_own, normed_oth, rows_own, rows_recv, (0, 3 * LOCAL))], planes=False, spare=128
    )
    blocks_last = vector_columns(
        blocks_last, rows_own, rows_recv, *sums_parts, second_sums, second_core, up_sums_own, up_sums_oth
    )
    gn_one_recv = across(gn_one_part)
    blocks_last = held(blocks_last, moved_three, gn_one_recv)
    moved_last = exchange(blocks_last)

    layer_own, rms_own = kernel_call(
        layer_kernel,
        [((ROWS, width), f32), ((3, ROWS), f32)],
        scalars=0,
        name="layer_out",
        late=(blocks_last,),
    )(residual, attn_part, attn_recv, mlp_chip, mlp_recv, row_biases)
    layer_out = join_rows(core_s, layer_own, swap(layer_own))
    (rms_rows,) = kernel_call(
        rms_join_kernel, [((3, 2 * ROWS), f32)], name="rms_join"
    )(core_s, rms_own, swap(rms_own))
    (input_own,) = kernel_call(input_grads_kernel, [((ROWS, width), f32)], name="input_grads")(
        core_s, gn_one_part, gn_one_recv, grad_residual, split_tokens, ln_gains
    )
    input_grad = join_rows(core_s, input_own, swap(input_own))
    (
        grad_up,
        grad_down,
        grad_out,
        grad_qkv,
        grad_gains,
        grad_shifts,
        grad_up_bias,
        grad_qv_bias,
    ) = kernel_call(
        last_sums_kernel,
        [
            ((32, width), f32),
            ((32, width), f32),
            ((32, LOCAL), f32),
            ((3, 32, LOCAL), f32),
            ((2, 32), f32),
            ((4, 32), f32),
            ((1, 32), f32),
            ((2, 8), f32),
        ],
        scalars=0,
        name="last_sums",
        late=(layer_out, input_grad, rms_rows),
    )(moved_last.reshape(SUBS, 32, -1), *sums_one, *sums_two, *plane_sum(moved_three))
    return (
        layer_out,
        input_grad,
        rms_rows,
        grad_qkv.transpose(1, 0, 2),
        grad_qv_bias,
        grad_out.T,
        grad_up,
        grad_up_bias[0],
        grad_down.T,
        grad_gains,
        grad_shifts,
    )


def solution(mesh):
    return jax.shard_map(
        per_device,
        mesh=mesh,
        in_specs=(
            P("ctx", None),
            P(),
            P(None, None, "tp"),
            P(None, "tp"),
            P("tp", None),
            P(None, "tp"),
            P("tp"),
            P("tp", None),
            P(),
            P(),
            P("ctx", None),
        ),
        out_specs=(
            P("ctx", None),
            P("ctx", None),
            P(None, "ctx"),
            P("ctx", None, "tp"),
            P(None, ("tp", "ctx")),
            P("tp", "ctx"),
            P("ctx", "tp"),
            P(("tp", "ctx")),
            P("tp", "ctx"),
            P(None, "ctx"),
            P(None, "ctx"),
        ),
        check_vma=False,
    )
```

```python
import jax
import jax.numpy as jnp
from jax import lax
from jax.experimental import pallas as pl
from jax.experimental.pallas import tpu as pltpu
from jax.sharding import PartitionSpec as P

HEAD = 64
SUBS = 32
HALF = 64
GROUPS = 4
ROWS = GROUPS * HALF
LOCAL = 256
P_ONE = 640
P_TWO = 384
LIMIT = 36
TILE = 256
CHUNK = 512
EPSILON = 1e-05
RMS_EPSILON = 1e-06
LOG_SHRINK = 10 * 0.6931471805599453
SHRINK = 2.0**-10
CORE_SWAP = [(0, 1), (1, 0), (2, 3), (3, 2)]
YHI_SWAP = [(0, 2), (2, 0), (1, 3), (3, 1)]
YLO_SWAP = [(j, j ^ 4) for j in range(SUBS)]
CROSS_SWAP = [(0, 3), (3, 0), (1, 2), (2, 1)]
PLANES = [[z * 8 + y * 4 + x for z in range(4) for x in range(4)] for y in range(2)]
NT = (((1,), (1,)), ((), ()))
TN = (((0,), (0,)), ((), ()))
bf16 = jnp.bfloat16
f32 = jnp.float32


def norm_parts(values):
    centre = jnp.mean(values, axis=-1, keepdims=True)
    centred = values - centre
    spread = jnp.mean(centred * centred, axis=-1, keepdims=True)
    inverse = lax.rsqrt(spread + EPSILON)
    return centred * inverse, inverse


def norm_back(grad_normed, unit_rows, inverse, gain):
    grad_unit = grad_normed * gain
    first_mean = jnp.mean(grad_unit, axis=-1, keepdims=True)
    second_mean = jnp.mean(grad_unit * unit_rows, axis=-1, keepdims=True)
    return inverse * (grad_unit - first_mean - unit_rows * second_mean)


def hold(arrays):
    return [pltpu.with_memory_space_constraint(x, pltpu.HBM) for x in arrays]


def order(arrays):
    return [x if x.size * x.dtype.itemsize < 2**18 else hold([x])[0] for x in arrays]


def pieces_of(ref, stage, sems, first, pieces):
    step = ref.shape[0] // pieces
    return [
        pltpu.make_async_copy(
            ref.at[pl.ds(i * step, step)], stage.at[pl.ds(i * step, step)], sems.at[first + i]
        )
        for i in range(pieces)
    ]


def with_copies(body, n_in, n_late, n_out, stored, brought, lazy):
    def kernel(*refs):
        ins, outs = list(refs[:n_in]), list(refs[n_in + n_late : n_in + n_late + n_out])
        rest = refs[n_in + n_late + n_out :]
        arriving = {}
        if brought:
            stages, in_sems, rest = rest[: len(brought)], rest[len(brought)], rest[len(brought) + 1 :]
            first = 0
            for stage, (o, pieces) in zip(stages, brought):
                arriving[o] = pieces_of(ins[o], stage, in_sems, first, pieces)
                ins[o] = stage
                first += pieces
            for copies in arriving.values():
                for copy in copies:
                    copy.start()
        stages, rest = rest[: len(stored)], rest[len(stored) :]
        copies = []
        if stored:
            sems, rest = rest[0], rest[1:]
            copies = [
                pltpu.make_async_copy(stage, outs[o], sems.at[i])
                for i, (stage, o) in enumerate(zip(stages, stored))
            ]
        for stage, o in zip(stages, stored):
            outs[o] = stage
        leaving = dict(zip(stored, copies))
        if lazy:
            body(arriving, leaving, *ins, *outs, *rest)
        else:
            for arrivals in arriving.values():
                for copy in arrivals:
                    copy.wait()
            body(*ins, *outs, *rest)
        for copy in leaving.values():
            copy.start()
        for copy in copies:
            copy.wait()

    return kernel


def kernel_call(
    body, outs, scratch=(), scalars=1, name=None, stored=(), late=(), brought=(), lazy=False, direct=()
):
    smem = pl.BlockSpec(memory_space=pltpu.SMEM)
    vmem = pl.BlockSpec(memory_space=pltpu.VMEM)
    hbm = pl.BlockSpec(memory_space=pltpu.HBM)
    shapes = [x if hasattr(x, "memory_space") or not isinstance(x, tuple) else pltpu.VMEM(*x) for x in scratch]
    if stored:
        shapes = (
            [pltpu.VMEM(*outs[o]) for o in stored]
            + [pltpu.SemaphoreType.DMA((len(stored),))]
            + shapes
        )

    def call(*args):
        args, more, specs = list(args), [], [smem] * scalars + [vmem] * (len(args) - scalars)
        for o, _ in brought:
            specs[o] = hbm
            more.append(pltpu.VMEM(args[o].shape, args[o].dtype))
            (args[o],) = hold([args[o]])
        if brought:
            more.append(pltpu.SemaphoreType.DMA((sum(pieces for _, pieces in brought),)))
        return pl.pallas_call(
            with_copies(body, len(args), len(late), len(outs), stored, brought, lazy),
            out_shape=[
                pltpu.HBM(s, d) if o in stored + direct else jax.ShapeDtypeStruct(s, d)
                for o, (s, d) in enumerate(outs)
            ],
            in_specs=specs + [pl.BlockSpec(memory_space=pl.ANY)] * len(late),
            out_specs=[hbm if o in stored + direct else vmem for o in range(len(outs))],
            scratch_shapes=more + shapes,
            compiler_params=pltpu.CompilerParams(vmem_limit_bytes=LIMIT * 2**20),
            cost_estimate=pl.CostEstimate(flops=1, bytes_accessed=1, transcendentals=0),
            name=name,
        )(*args, *order(late))

    return call


def held(x, *late):
    hbm = pl.BlockSpec(memory_space=pltpu.HBM)
    return pl.pallas_call(
        lambda *refs: None,
        out_shape=pltpu.HBM(x.shape, x.dtype),
        in_specs=[hbm] + [pl.BlockSpec(memory_space=pl.ANY)] * len(late),
        out_specs=hbm,
        input_output_aliases={0: 0},
        cost_estimate=pl.CostEstimate(flops=1, bytes_accessed=1, transcendentals=0),
        name="held",
    )(*hold([x]), *late)


def fold(rows):
    return jnp.concatenate([rows[:32], rows[32:]], axis=1)


def unfold(packed):
    return jnp.concatenate([packed[:, :HEAD], packed[:, HEAD:]], axis=0)


def project_own_kernel(arriving, leaving, core_ref, x_ref, w_ref, gains, shifts, b_ref, send_ref, low_ref):
    for o in (1, 3, 4, 5):
        for copy in arriving[o]:
            copy.wait()
    x = x_ref[:, core_ref[0]].reshape(ROWS, -1).astype(f32)
    unit, _ = norm_parts(x)
    low = (unit * gains[0:1].astype(f32) + shifts[0:1].astype(f32)).astype(bf16)
    low_ref[...] = low
    for w in arriving[2]:
        w.wait()
    for g, h, qk, v in projected(low, w_ref, b_ref):
        send_ref[g * 4 + h, 0:64, :] = qk
        send_ref[g * 4 + h, 64:96, :] = v


def project_oth_kernel(core_ref, low_ref, w_ref, b_ref, first_ref, send_ref):
    core = core_ref[0]
    for g in range(GROUPS):
        for h in range(4):
            send_ref[g * 8 + core * 4 + h] = first_ref[g * 4 + h]
    for g, h, qk, v in projected(low_ref[...], w_ref, b_ref):
        block = g * 8 + (1 - core) * 4 + h
        send_ref[block, 0:64, :] = qk
        send_ref[block, 64:96, :] = v


def projected(low, w_ref, b_ref):
    q = jnp.dot(low, w_ref[0], preferred_element_type=f32) + b_ref[0:1].astype(f32)
    k = jnp.dot(low, w_ref[1], preferred_element_type=f32)
    v = jnp.dot(low, w_ref[2], preferred_element_type=f32) + b_ref[1:2].astype(f32)
    for g in range(GROUPS):
        for h in range(4):
            rows = slice(g * HALF, (g + 1) * HALF)
            cols = slice(h * HEAD, (h + 1) * HEAD)
            qk = jnp.concatenate([q[rows, cols], k[rows, cols]], axis=1)
            yield g, h, qk.astype(bf16), fold(v[rows, cols]).astype(bf16)


def pair_masks(core, transposed):
    shape = (CHUNK, TILE) if transposed else (TILE, CHUNK)
    q = lax.broadcasted_iota(jnp.int32, shape, 1 if transposed else 0)
    key = lax.broadcasted_iota(jnp.int32, shape, 0 if transposed else 1)
    other = key >= TILE
    k = jnp.where(other, key - TILE, key)
    q_sub = lax.shift_right_logical(q, 6)
    k_sub = lax.shift_right_logical(k, 6)
    prompt = (other & (q_sub + core > k_sub)) | (jnp.logical_not(other) & (q >= k))
    cont = prompt & (lax.shift_right_logical(q, 7) == lax.shift_right_logical(k, 7))
    return prompt, cont


def chunks_of(tile, prompt, cont):
    if tile < 4:
        return [(j, None) for j in range(tile)] + [(tile, prompt)]
    return [(j, None) for j in range(4)] + [(tile, cont)]


def places(sc_ref, d):
    p = sc_ref[SUBS + 1 + d]
    at = lax.shift_right_logical(p, 2) * CHUNK + (p & 3) * HALF
    return pl.ds(pl.multiple_of(p * HALF, HALF), HALF), pl.multiple_of(at, HALF)


def attend_kernel(
    sc_ref, own_ref, oth_ref, own_kept, oth_kept, out_ref, lse_ref, q_s, k_s, v_s, kept_sems
):
    keeping = [
        pltpu.make_async_copy(ref, kept, kept_sems.at[i])
        for i, (ref, kept) in enumerate(((own_ref, own_kept), (oth_ref, oth_kept)))
    ]
    for copy in keeping:
        copy.start()
    core = sc_ref[SUBS]
    const = jnp.full((HALF, HEAD), SHRINK, bf16)
    for p in range(SUBS):
        d = sc_ref[p]
        at = p // 4 * CHUNK + p % 4 * HALF
        q_s[p * HALF : (p + 1) * HALF, :] = own_ref[d, 0:64, :HEAD] * jnp.asarray(0.125, bf16)
        for ref, start in ((own_ref, at), (oth_ref, at + TILE)):
            k_s[start : start + HALF, :] = ref[d, 0:64, HEAD:]
            v = unfold(ref[d, 64:96, :]) * jnp.asarray(SHRINK, bf16)
            v_s[start : start + HALF, :] = jnp.concatenate([v, const], axis=1)
    prompt, cont = pair_masks(core, False)
    for t in range(8):
        q = q_s[t * TILE : (t + 1) * TILE, :]
        total = None
        for j, mask in chunks_of(t, prompt, cont):
            keys = slice(j * CHUNK, (j + 1) * CHUNK)
            s = lax.dot_general(q, k_s[keys, :], NT, preferred_element_type=f32)
            w = jnp.exp(s)
            if mask is not None:
                w = jnp.where(mask, w, 0.0)
            part = jnp.dot(w.astype(bf16), v_s[keys, :], preferred_element_type=f32)
            total = part if total is None else total + part
        mixed = total[:, :HEAD] / total[:, HEAD:]
        lse_ref[t : t + 1, :] = jnp.log(total.T[HEAD : HEAD + 1, :]) + LOG_SHRINK
        for i in range(4):
            out_ref[sc_ref[t * 4 + i]] = fold(mixed[i * HALF : (i + 1) * HALF]).astype(bf16)
    for copy in keeping:
        copy.wait()


def attend_back_kernel(
    arriving, leaving, sc_ref, own_ref, oth_ref, do_ref, o_ref, lse_ref,
    dq_ref, keep_ref, send_ref,
    q_s, do_s, vk_s, kt_s, inner_s, acc_s,
):
    core = sc_ref[SUBS]
    zero = jnp.zeros((HALF, HEAD), bf16)
    for o, ref, shift in ((1, own_ref, 0), (2, oth_ref, TILE)):
        for d in range(SUBS):
            if d % 8 == 0:
                arriving[o][d // 8].wait()
            rows, at = places(sc_ref, d)
            if o == 1:
                q = ref[d, 0:64, :HEAD] * jnp.asarray(0.125, bf16)
                q_s[rows, :] = jnp.concatenate([zero, q], axis=1)
            vk_s[pl.ds(at + shift, HALF), :] = jnp.concatenate(
                [unfold(ref[d, 64:96, :]), ref[d, 0:64, HEAD:]], axis=1
            )
    for d in range(SUBS):
        if d % 16 == 0:
            arriving[3][d // 16].wait()
        rows, _ = places(sc_ref, d)
        do_s[rows, :] = jnp.concatenate([unfold(do_ref[d]), zero], axis=1)
    for j in range(8):
        keys = slice(j * CHUNK, (j + 1) * CHUNK)
        kt_s[:, keys] = vk_s[keys, :].T[HEAD:, :]
    for o in (4, 5):
        for copy in arriving[o]:
            copy.wait()
    for t in range(8):
        both = []
        for i in range(4):
            d = sc_ref[t * 4 + i]
            both.append(unfold(do_ref[d].astype(f32) * o_ref[d].astype(f32)))
        inner_s[t : t + 1, :] = jnp.sum(jnp.concatenate(both, axis=0).T, axis=0, keepdims=True)
    prompt, cont = pair_masks(core, True)
    started = set()
    for t in range(8):
        tile = slice(t * TILE, (t + 1) * TILE)
        q = q_s[tile, :]
        grad = do_s[tile, :]
        lse = lse_ref[t : t + 1, :]
        inner = inner_s[t : t + 1, :]
        dq = None
        for j, mask in chunks_of(t, prompt, cont):
            keys = slice(j * CHUNK, (j + 1) * CHUNK)
            vk = vk_s[keys, :]
            s = lax.dot_general(vk, q, NT, preferred_element_type=f32)
            a = jnp.exp(s - lse)
            if mask is not None:
                a = jnp.where(mask, a, 0.0)
            dp = lax.dot_general(vk, grad, NT, preferred_element_type=f32)
            ds = (a * (dp - inner)).astype(bf16)
            part = jnp.dot(a.astype(bf16), grad, preferred_element_type=f32) + jnp.dot(
                ds, q, preferred_element_type=f32
            )
            if j in started:
                acc_s[keys, :] += part
            else:
                acc_s[keys, :] = part
                started.add(j)
            dq_part = jnp.dot(kt_s[:, keys], ds, preferred_element_type=f32)
            dq = dq_part if dq is None else dq + dq_part
        dq_ref[tile, :] = (dq * 0.125).T.astype(bf16)
    for j in range(8):
        keep_ref[j * TILE : (j + 1) * TILE, :] = acc_s[j * CHUNK : j * CHUNK + TILE, :]
        send_ref[j * TILE : (j + 1) * TILE, :] = acc_s[
            j * CHUNK + TILE : (j + 1) * CHUNK, :
        ].astype(bf16)


def pack_grads_kernel(sc_ref, dq_ref, keep_ref, recv_ref, out_ref):
    for p in range(SUBS):
        rows = slice(p * HALF, (p + 1) * HALF)
        summed = (keep_ref[rows, :] + recv_ref[rows, :].astype(f32)).astype(bf16)
        d = sc_ref[p]
        out_ref[d, 0:64, :] = jnp.concatenate([dq_ref[rows, :], summed[:, HEAD:]], axis=1)
        out_ref[d, 64:96, :] = fold(summed[:, :HEAD])


def out_kernel(
    arriving, leaving, core_ref, recv_ref, own_w, oth_w, own_ref, oth_ref, part_ref
):
    core = core_ref[0]
    for half, ref in ((core, own_ref), (1 - core, oth_ref)):
        for g in range(GROUPS):
            heads = [unfold(recv_ref[g * 8 + half * 4 + h]) for h in range(4)]
            ref[g * HALF : (g + 1) * HALF, :] = jnp.concatenate(heads, axis=1)
    for o in (0, 1):
        leaving.pop(o).start()
    part = jnp.dot(own_ref[...], own_w[...], preferred_element_type=f32) + jnp.dot(
        oth_ref[...], oth_w[...], preferred_element_type=f32
    )
    part_ref[...] = part.astype(bf16)


def split_kernel(core_ref, rows_ref, own_ref, oth_ref):
    own_ref[...] = rows_ref[:, core_ref[0]].reshape(own_ref.shape)
    oth_ref[...] = rows_ref[:, 1 - core_ref[0]].reshape(oth_ref.shape)


def first_norm_kernel(core_ref, x_ref, gains, shifts, own_ref, oth_ref):
    for half, low_ref in ((core_ref[0], own_ref), (1 - core_ref[0], oth_ref)):
        unit, _ = norm_parts(x_ref[:, half].reshape(ROWS, -1).astype(f32))
        low_ref[...] = (unit * gains[0:1].astype(f32) + shifts[0:1].astype(f32)).astype(bf16)


def layer_kernel(
    residual_ref, part_ref, part_recv_ref, mlp_ref, mlp_recv_ref, shifts, layer_ref, rms_ref
):
    attn = (part_ref[...].astype(f32) + part_recv_ref[...].astype(f32)) + shifts[1:2].astype(f32)
    mlp = (mlp_ref[...].astype(f32) + mlp_recv_ref[...].astype(f32)) + shifts[3:4].astype(f32)
    layer = residual_ref[...] + mlp
    layer_ref[...] = layer
    for i, rows in enumerate((layer, attn, mlp)):
        squares = rows * rows
        folded = sum(squares[:, c : c + 128] for c in range(0, squares.shape[1], 128))
        mean = jnp.sum(folded.T, axis=0, keepdims=True) / squares.shape[1]
        rms_ref[i : i + 1, :] = jnp.sqrt(mean + RMS_EPSILON)


def rms_join_kernel(core_ref, own_ref, oth_ref, out_ref):
    first = core_ref[0] == 0
    own, oth = own_ref[...], oth_ref[...]
    low, high = jnp.where(first, own, oth), jnp.where(first, oth, own)
    pieces = []
    for g in range(GROUPS):
        pieces += [rows[:, g * HALF : (g + 1) * HALF] for rows in (low, high)]
    out_ref[...] = jnp.concatenate(pieces, axis=1)


def second_norm_kernel(
    arriving, leaving, core_ref, part_ref, recv_ref, x_ref, gains, shifts, residual_ref, low_ref
):
    x = x_ref[:, core_ref[0]].reshape(ROWS, -1).astype(f32)
    branch = (part_ref[...].astype(f32) + recv_ref[...].astype(f32)) + shifts[1:2].astype(f32)
    residual = x + branch
    residual_ref[...] = residual
    leaving.pop(0).start()
    unit, _ = norm_parts(residual)
    low_ref[...] = (unit * gains[1:2].astype(f32) + shifts[2:3].astype(f32)).astype(bf16)


def put_blocks(stage, to, made, planes):
    if planes:
        for j in range(SUBS):
            at = (j // 8 * 8 + j % 4 * 2 + j // 4 % 2) * 32
            stage[at : at + 32, to] = made[j * 32 : (j + 1) * 32]
    else:
        stage[:, to] = made


def fetch_kernel(first_ref, second_ref, first_out, second_out, done_ref, sems):
    done_ref[...] = jnp.zeros_like(done_ref)
    copies = []
    for i, (ref, out) in enumerate(((first_ref, first_out), (second_ref, second_out))):
        for j in range(4):
            rows = pl.ds(j * 256, 256)
            copies.append(pltpu.make_async_copy(ref.at[rows], out.at[rows], sems.at[4 * i + j]))
    for copy in copies:
        copy.start()
    for copy in copies:
        copy.wait()


def fetch(first, second, late):
    hbm = pl.BlockSpec(memory_space=pltpu.HBM)
    vmem = pl.BlockSpec(memory_space=pltpu.VMEM)
    return pl.pallas_call(
        lambda a, b, unused, *rest: fetch_kernel(a, b, *rest),
        out_shape=[pltpu.VMEM(x.shape, x.dtype) for x in (first, second)]
        + [jax.ShapeDtypeStruct((8, 128), f32)],
        in_specs=[hbm] * 3,
        out_specs=[vmem] * 3,
        scratch_shapes=[pltpu.SemaphoreType.DMA((8,))],
        compiler_params=pltpu.CompilerParams(vmem_limit_bytes=LIMIT * 2**20),
        cost_estimate=pl.CostEstimate(flops=1, bytes_accessed=1, transcendentals=0),
        name="fetch",
    )(*hold((first, second, late)))


def feed_half(rows_ref, cot_ref, up_ref, bias_ref, down_ref, active_ref, grad_ref, back_ref, sums_ref):
    total = None
    for c in range(4):
        cols = slice(c * 256, (c + 1) * 256)
        up = up_ref[:, cols]
        bias = jnp.concatenate([bias_ref[2 * c + b : 2 * c + b + 1] for b in range(2)], axis=1)
        hidden = jnp.dot(rows_ref[...], up, preferred_element_type=f32) + bias.astype(f32)
        grad_active = lax.dot_general(
            cot_ref[...], down_ref[cols, :], NT, preferred_element_type=f32
        )
        share = 0.5 + 0.5 * lax.erf(hidden * 0.7071067811865476)
        density = jnp.exp(hidden * hidden * -0.5) * 0.3989422804014327
        active_ref[:, cols] = (hidden * share).astype(bf16)
        grad = (grad_active * (share + hidden * density)).astype(bf16)
        grad_ref[:, cols] = grad
        sums_ref[0:1, cols] = jnp.sum(grad.astype(f32), axis=0, keepdims=True)
        part = lax.dot_general(grad, up, NT, preferred_element_type=f32)
        total = part if total is None else total + part
    back_ref[...] = total.astype(back_ref.dtype)


def feed_own_kernel(arriving, leaving, *refs):
    feed_half(*refs)


def feed_oth_kernel(
    arriving, leaving, rows_ref, cot_ref, up_ref, bias_ref, down_ref, own_ref, own_grad,
    active_ref, grad_ref, back_ref, sums_ref, blocks_ref,
):
    feed_half(
        rows_ref, cot_ref, up_ref, bias_ref, down_ref, active_ref, grad_ref, back_ref, sums_ref
    )
    for o in range(4):
        leaving.pop(o).start()
    for copy in arriving[6]:
        copy.wait()
    for c in range(0, P_ONE, 256):
        cols = slice(c, min(c + 256, P_ONE))
        made = lax.dot_general(own_ref[...], own_grad[:, cols], TN, preferred_element_type=f32)
        made += lax.dot_general(rows_ref[...], grad_ref[:, cols], TN, preferred_element_type=f32)
        put_blocks(blocks_ref, cols, made.astype(bf16), True)
    leaving.pop(4).start()


def feed_out_kernel(arriving, leaving, own_ref, oth_ref, down_ref, own_out, oth_out):
    for o in (0, 1, 2):
        for copy in arriving[o]:
            copy.wait()
    for o, ref, out_ref in ((0, own_ref, own_out), (1, oth_ref, oth_out)):
        made = jnp.dot(ref[...], down_ref[...], preferred_element_type=f32)
        out_ref[...] = made.astype(bf16)
        leaving.pop(o).start()


def residual_grads_kernel(
    arriving, leaving, core_ref, own_ref, recv_ref, residual_ref, cot_ref, gains, own_w, oth_w,
    grad_ref, low_ref, send_ref, sums_ref,
):
    core = core_ref[0]
    unit, inverse = norm_parts(residual_ref[...])
    grad_normed = own_ref[...].astype(f32) + recv_ref[...].astype(f32)
    cot = cot_ref[...].astype(f32)
    grad = cot + norm_back(grad_normed, unit, inverse, gains[1:2].astype(f32))
    grad_ref[...] = grad
    low = grad.astype(bf16)
    low_ref[...] = low
    sums = [grad_normed * unit, low.astype(f32), grad_normed, cot]
    for i, rows in enumerate(sums):
        sums_ref[i : i + 1, :] = jnp.sum(rows, axis=0, keepdims=True)
    for o in (0, 1, 3):
        leaving.pop(o).start()
    for half, w_ref in ((core, own_w), (1 - core, oth_w)):
        made = lax.dot_general(low, w_ref[...], NT, preferred_element_type=f32)
        for g in range(GROUPS):
            for h in range(4):
                block = made[g * HALF : (g + 1) * HALF, h * HEAD : (h + 1) * HEAD]
                send_ref[g * 8 + half * 4 + h] = fold(block).astype(bf16)


def token_grads_kernel(arriving, leaving, core_ref, recv_ref, own_w, oth_w, own_ref, oth_ref, part_ref):
    core = core_ref[0]
    part = None
    for copy in arriving[1]:
        copy.wait()
    for half, w_ref, ref in ((core, own_w, own_ref), (1 - core, oth_w, oth_ref)):
        for g in range(GROUPS):
            rows = slice(g * HALF, (g + 1) * HALF)
            blocks = [recv_ref.at[g * 8 + half * 4 + h] for h in range(4)]
            pieces = (
                [b[0:64, :HEAD] for b in blocks]
                + [b[0:64, HEAD:] for b in blocks]
                + [unfold(b[64:96, :]) for b in blocks]
            )
            ref[rows, :] = jnp.concatenate(pieces, axis=1)
        leaving.pop(0 if ref is own_ref else 1).start()
        for i in range(3):
            arriving[2 if w_ref is own_w else 3][i].wait()
            made = lax.dot_general(
                ref[:, i * LOCAL : (i + 1) * LOCAL], w_ref[i], NT, preferred_element_type=f32
            )
            part = made if part is None else part + made
    part_ref[...] = part.astype(bf16)


def first_sums_kernel(core_ref, part_ref, x_ref, sums_ref):
    unit, _ = norm_parts(x_ref[:, core_ref[0]].reshape(ROWS, -1).astype(f32))
    part = part_ref[...].astype(f32)
    sums_ref[0:1, :] = jnp.sum(part * unit, axis=0, keepdims=True)
    sums_ref[1:2, :] = jnp.sum(part, axis=0, keepdims=True)
    sums_ref[2:8, :] = jnp.zeros((6, part.shape[1]), f32)


def input_grads_kernel(core_ref, part_ref, recv_ref, grad_ref, x_ref, gains, out_ref):
    x = x_ref[:, core_ref[0]].reshape(ROWS, -1).astype(f32)
    unit, inverse = norm_parts(x)
    grad_normed = part_ref[...].astype(f32) + recv_ref[...].astype(f32)
    out_ref[...] = grad_ref[...] + norm_back(grad_normed, unit, inverse, gains[0:1].astype(f32))


def join_kernel(core_ref, own_ref, oth_ref, out_ref, sems):
    core = core_ref[0]
    copies = []
    for i, (ref, half) in enumerate(((own_ref, core), (oth_ref, 1 - core))):
        for g in range(GROUPS):
            rows = pl.ds(g * HALF, HALF)
            at = i * GROUPS + g
            copies.append(pltpu.make_async_copy(ref.at[rows], out_ref.at[g, half], sems.at[at]))
    for copy in copies:
        copy.start()
    for copy in copies:
        copy.wait()


def join_rows(core_s, own, oth):
    width = own.shape[1]
    vmem = pl.BlockSpec(memory_space=pltpu.VMEM)
    joined = pl.pallas_call(
        join_kernel,
        out_shape=pltpu.HBM((GROUPS, 2, HALF, width), own.dtype),
        in_specs=[pl.BlockSpec(memory_space=pltpu.SMEM), vmem, vmem],
        out_specs=pl.BlockSpec(memory_space=pltpu.HBM),
        scratch_shapes=[pltpu.SemaphoreType.DMA((2 * GROUPS,))],
        compiler_params=pltpu.CompilerParams(vmem_limit_bytes=8 * 2**20),
        cost_estimate=pl.CostEstimate(flops=1, bytes_accessed=1, transcendentals=0),
        name="join_rows",
    )(core_s, own, oth)
    return joined.reshape(2 * ROWS, width)


def weight_grads_kernel(spans, planes, arriving, *refs):
    out_ref, stage, sems = refs[-3:]
    copies = []

    def send(start, stop):
        copies.append(
            pltpu.make_async_copy(
                stage.at[:, pl.ds(start, stop - start)],
                out_ref.at[:, pl.ds(start, stop - start)],
                sems.at[len(copies)],
            )
        )
        copies[-1].start()

    start = 0
    for i, (first, last) in enumerate(spans):
        a_own, a_oth, b_own, b_oth = refs[4 * i : 4 * i + 4]
        for o in range(4 * i, 4 * i + 4):
            for copy in arriving[o]:
                copy.wait()
        for c in range(first, last, 256):
            cols = slice(c, min(c + 256, last))
            made = lax.dot_general(a_own[...], b_own[:, cols], TN, preferred_element_type=f32)
            made += lax.dot_general(a_oth[...], b_oth[:, cols], TN, preferred_element_type=f32)
            stop = start + cols.stop - cols.start
            put_blocks(stage, slice(start, stop), made.astype(bf16), planes)
            send(start, stop)
            start = stop
    for copy in copies:
        copy.wait()


def last_grads_kernel(arriving, a_own, a_oth, b_own, b_oth, out_ref, stage, sems):
    copies = []
    for copies_in in arriving:
        for copy in copies_in:
            copy.wait()
    for k in range(3):
        cols = slice(k * 256, (k + 1) * 256)
        made = lax.dot_general(a_own[...], b_own[:, cols], TN, preferred_element_type=f32)
        made += lax.dot_general(a_oth[...], b_oth[:, cols], TN, preferred_element_type=f32)
        made = made.astype(bf16)
        for d in range(SUBS):
            for i in range(2):
                stage[d, k * 64 + i * 32 : k * 64 + i * 32 + 32, :] = made[
                    d * 32 : (d + 1) * 32, i * 128 : (i + 1) * 128
                ]
        part = pl.ds(k * 64, 64)
        copies.append(pltpu.make_async_copy(stage.at[:, part], out_ref.at[:, part], sems.at[k]))
        copies[-1].start()
    for copy in copies:
        copy.wait()


def last_grads(*args):
    hbm = pl.BlockSpec(memory_space=pltpu.HBM)

    def body(*refs):
        arriving = [pieces_of(refs[i], refs[5 + i], refs[9], 2 * i, 2) for i in range(4)]
        for copies in arriving:
            for copy in copies:
                copy.start()
        last_grads_kernel(arriving, *refs[5:9], refs[4], refs[10], refs[11])

    return pl.pallas_call(
        body,
        out_shape=pltpu.HBM((SUBS, 208, 128), bf16),
        in_specs=[hbm] * 4,
        out_specs=hbm,
        scratch_shapes=[pltpu.VMEM(x.shape, x.dtype) for x in args]
        + [
            pltpu.SemaphoreType.DMA((8,)),
            pltpu.VMEM((SUBS, 192, 128), bf16),
            pltpu.SemaphoreType.DMA((3,)),
        ],
        compiler_params=pltpu.CompilerParams(vmem_limit_bytes=LIMIT * 2**20),
        cost_estimate=pl.CostEstimate(flops=1, bytes_accessed=1, transcendentals=0),
        name="last_grads",
    )(*hold(args))


def vector_rows_kernel(
    into_ref, own_rows, oth_rows, own, core, across, cross, second, second_core, up_own, up_oth,
    out_ref, stage, sem,
):
    rows = ((own[...] + core[...]) + (across[...] + cross[...]))[0:2]
    rows = [rows, second[...] + second_core[...], up_own[...] + up_oth[...]]
    rows = jnp.concatenate(rows + [jnp.zeros((1, up_own.shape[1]), f32)], axis=0)
    pairs = []
    for first in (0, 2 * LOCAL):
        cols = slice(first, first + LOCAL)
        pairs.append(
            jnp.sum(own_rows[:, cols].astype(f32), axis=0, keepdims=True)
            + jnp.sum(oth_rows[:, cols].astype(f32), axis=0, keepdims=True)
        )
    pairs = jnp.concatenate(pairs + [jnp.zeros((6, LOCAL), f32)], axis=0)
    for d in range(SUBS):
        piece = jnp.concatenate([rows[:, d * 32 : (d + 1) * 32], jnp.zeros((8, 96), f32)], axis=1)
        bias = jnp.concatenate([pairs[:, d * 8 : (d + 1) * 8], jnp.zeros((8, 120), f32)], axis=1)
        stage[d] = jnp.concatenate([piece, bias], axis=0).astype(bf16)
    copy = pltpu.make_async_copy(stage, out_ref.at[:, pl.ds(192, 16)], sem)
    copy.start()
    copy.wait()


def vector_rows(into, *arrays):
    hbm = pl.BlockSpec(memory_space=pltpu.HBM)
    vmem = pl.BlockSpec(memory_space=pltpu.VMEM)
    return pl.pallas_call(
        vector_rows_kernel,
        out_shape=pltpu.HBM(into.shape, into.dtype),
        in_specs=[hbm] + [vmem] * len(arrays),
        out_specs=hbm,
        scratch_shapes=[pltpu.VMEM((SUBS, 16, 128), bf16), pltpu.SemaphoreType.DMA(())],
        input_output_aliases={0: 0},
        compiler_params=pltpu.CompilerParams(vmem_limit_bytes=LIMIT * 2**20),
        cost_estimate=pl.CostEstimate(flops=1, bytes_accessed=1, transcendentals=0),
        name="vector_rows",
    )(*hold([into]), *arrays)


def weight_grads(parts, late=(), planes=True, spare=0):
    width = parts[0][0].shape[1]
    spans = [p[4] for p in parts]
    args = [x for p in parts for x in p[:4]]
    columns = sum(last - first for first, last in spans)
    hbm = pl.BlockSpec(memory_space=pltpu.HBM)
    n = len(args)

    def body(*refs):
        out_ref, rest = refs[n + len(late)], refs[n + len(late) + 1 :]
        stages, in_sems, stage, sems = rest[:n], rest[n], rest[n + 1], rest[n + 2]
        arriving = [pieces_of(refs[i], stages[i], in_sems, 2 * i, 2) for i in range(n)]
        for copies in arriving:
            for copy in copies:
                copy.start()
        weight_grads_kernel(spans, planes, arriving, *stages, out_ref, stage, sems)

    return pl.pallas_call(
        body,
        out_shape=pltpu.HBM((width, columns + spare), bf16),
        in_specs=[hbm] * (n + len(late)),
        out_specs=hbm,
        scratch_shapes=[pltpu.VMEM(x.shape, x.dtype) for x in args]
        + [
            pltpu.SemaphoreType.DMA((2 * n,)),
            pltpu.VMEM((width, columns), bf16),
            pltpu.SemaphoreType.DMA((16,)),
        ],
        compiler_params=pltpu.CompilerParams(vmem_limit_bytes=LIMIT * 2**20),
        cost_estimate=pl.CostEstimate(flops=1, bytes_accessed=1, transcendentals=0),
        name="weight_grads",
    )(*hold(args + list(late)))


def plane_sum_kernel(y_ref, moved_ref, own_ref, oth_ref):
    for half, ref in ((y_ref[0], own_ref), (1 - y_ref[0], oth_ref)):
        ref[...] = jnp.sum(moved_ref[:, half].astype(f32), axis=0).astype(ref.dtype)


def last_sums_kernel(
    moved_ref, one_own, one_oth, two_own, two_oth, three_own, three_oth,
    up_ref, down_ref, out_ref, qkv_ref, gains_ref, shifts_ref, up_bias_ref, qv_ref,
):
    one = one_own[...] + one_oth[...].astype(f32)
    two = two_own[...] + two_oth[...].astype(f32)
    three = three_own[...] + three_oth[...].astype(f32)
    width = up_ref.shape[1]
    up_ref[:, :P_ONE] = one
    up_ref[:, P_ONE:] = two[:, : width - P_ONE]
    down_ref[:, :P_TWO] = two[:, width - P_ONE :]

    down_ref[:, P_TWO:] = three[:, : width - P_TWO]
    out_ref[...] = three[:, width - P_TWO :]
    summed = jnp.sum(moved_ref[...].astype(f32), axis=0)
    for i in range(6):
        qkv_ref[i // 2, :, i % 2 * 128 : i % 2 * 128 + 128] = summed[i * 32 : (i + 1) * 32]
    small = summed[192:208]
    gains_ref[0:1, :] = small[0:1, :32]
    gains_ref[1:2, :] = small[2:3, :32]
    shifts_ref[0:1, :] = small[1:2, :32]
    shifts_ref[1:4, :] = small[3:6, :32]
    up_bias_ref[...] = small[6:7, :32]
    qv_ref[...] = small[8:10, :8]


def per_device(
    tokens,
    sub_blocks,
    w_qkv,
    qv_bias,
    w_out,
    w_up,
    up_bias,
    w_down,
    ln_gains,
    row_biases,
    cotangent,
):
    width = tokens.shape[1]
    ctx = lax.axis_index("ctx").astype(jnp.int32)
    core = (lax.axis_index("tp") % 2).astype(jnp.int32)
    core_s = core.reshape(1)
    y_low = (ctx // 4 % 2).reshape(1)

    def swap(x):
        return lax.ppermute(x, "tp", CORE_SWAP)

    def across(x):
        return lax.ppermute(x, "tp", YHI_SWAP)

    def exchange(x):
        return lax.all_to_all(x, "ctx", 0, 0, tiled=True)

    def plane_exchange(blocks):
        return lax.all_to_all(blocks, "ctx", 0, 0, axis_index_groups=PLANES, tiled=True)

    def plane_sum(moved):
        own, oth = kernel_call(
            plane_sum_kernel,
            [((32, moved.shape[1]), f32), ((32, moved.shape[1]), bf16)],
            name="plane_sum",
            brought=((1, 4),),
        )(y_low, moved.reshape(16, 2, 32, -1))
        return own, lax.ppermute(oth, "ctx", YLO_SWAP)

    own_row = lax.dynamic_index_in_dim(sub_blocks, ctx // 8, 0, False)
    order = jnp.arange(SUBS, dtype=jnp.int32)
    holder = jnp.sum(
        jnp.where(own_row[:, None] == order[None, :], order[:, None], 0), axis=0
    ).astype(jnp.int32)
    scalars = jnp.concatenate([holder, core_s, own_row])

    split_tokens = tokens.reshape(GROUPS, 2, HALF, width)
    w_own = w_qkv.transpose(1, 0, 2)
    w_oth = swap(w_own)
    b_oth = swap(qv_bias)
    wo_own = w_out
    wo_oth = swap(w_out)

    first, low_own = kernel_call(
        project_own_kernel,
        [((16, 96, 128), bf16), ((ROWS, width), bf16)],
        name="project_own",
        brought=((1, 4), (2, 3), (3, 1), (4, 1), (5, 1)),
        lazy=True,
    )(core_s, split_tokens, w_own, ln_gains, row_biases, qv_bias)
    (send,) = kernel_call(
        project_oth_kernel,
        [((SUBS, 96, 128), bf16)],
        stored=(0,),
        name="project_oth",
    )(core_s, low_own, w_oth, b_oth, first)
    mine = exchange(send)
    theirs = swap(mine)

    mine, theirs, mixed, lse = kernel_call(
        attend_kernel,
        [
            ((SUBS, 96, 128), bf16),
            ((SUBS, 96, 128), bf16),
            ((SUBS, 32, 128), bf16),
            ((8, TILE), f32),
        ],
        [
            pltpu.VMEM((2048, HEAD), bf16),
            pltpu.VMEM((4096, HEAD), bf16),
            pltpu.VMEM((4096, 128), bf16),
            pltpu.SemaphoreType.DMA((2,)),
        ],
        name="attend",
        stored=(2, 3),
        direct=(0, 1),
    )(scalars, mine, theirs)
    mixed_back = exchange(mixed)
    cot_own, cot_oth = kernel_call(
        split_kernel,
        [((ROWS, width), bf16), ((ROWS, width), bf16)],
        stored=(0, 1),
        name="split_rows",
        late=(mixed,),
    )(core_s, cotangent.reshape(GROUPS, 2, HALF, width))
    heads_own, heads_oth, attn_part = kernel_call(
        out_kernel,
        [((ROWS, LOCAL), bf16), ((ROWS, LOCAL), bf16), ((ROWS, width), bf16)],
        stored=(0, 1),
        lazy=True,
        name="project_out",
        late=(cot_own,),
    )(core_s, mixed_back, wo_own, wo_oth)
    attn_recv = across(attn_part)
    up_here, down_here, fetched = fetch(w_up, w_down, heads_own)
    residual, normed_two_own = kernel_call(
        second_norm_kernel,
        [((ROWS, width), f32), ((ROWS, width), bf16)],
        stored=(0,),
        lazy=True,
        name="second_norm",
        late=(fetched,),
    )(core_s, attn_part, attn_recv, split_tokens, ln_gains, row_biases)
    normed_two_oth = swap(normed_two_own)

    half_outs = [((ROWS, width), bf16)] * 3 + [((1, width), f32)]
    bias_rows = up_bias.reshape(8, -1)
    active_own, grad_hidden_own, gn_two_own, up_sums_own = kernel_call(
        feed_own_kernel, half_outs, scalars=0, stored=(0, 1, 2, 3), lazy=True, name="feed_own"
    )(normed_two_own, cot_own, up_here, bias_rows, down_here)
    active_oth, grad_hidden_oth, gn_two_oth, up_sums_oth, blocks_one = kernel_call(
        feed_oth_kernel,
        half_outs + [((width, P_ONE), bf16)],
        scalars=0,
        stored=(0, 1, 2, 3, 4),
        brought=((6, 2),),
        lazy=True,
        name="feed_oth",
    )(normed_two_oth, cot_oth, up_here, bias_rows, down_here, normed_two_own, grad_hidden_own)
    gn_two_chip = (gn_two_own.astype(f32) + swap(gn_two_oth).astype(f32)).astype(bf16)
    up_parts = (normed_two_own, normed_two_oth, grad_hidden_own, grad_hidden_oth)
    down_parts = (cot_own, cot_oth, active_own, active_oth)
    gn_two_recv = across(gn_two_chip)
    moved_one = plane_exchange(blocks_one)
    blocks_two = weight_grads(
        [up_parts + ((P_ONE, width),), down_parts + ((0, P_TWO),)], late=(blocks_one,)
    )

    mlp_own, mlp_oth = kernel_call(
        feed_out_kernel,
        [((ROWS, width), bf16), ((ROWS, width), bf16)],
        scalars=0,
        stored=(0, 1),
        brought=((0, 2), (1, 2), (2, 4)),
        lazy=True,
        name="feed_out",
    )(active_own, active_oth, w_down)

    grad_residual, grad_attn, grad_heads, second_sums = kernel_call(
        residual_grads_kernel,
        [
            ((ROWS, width), f32),
            ((ROWS, width), bf16),
            ((SUBS, 32, 128), bf16),
            ((4, width), f32),
        ],
        stored=(0, 1, 2, 3),
        lazy=True,
        name="residual_grads",
        late=(blocks_two, mlp_own),
    )(core_s, gn_two_chip, gn_two_recv, residual, cot_own, ln_gains, wo_own, wo_oth)
    grad_mixed = exchange(held(grad_heads, moved_one))

    grad_attn_oth = swap(grad_attn)
    heads_recv = swap(heads_oth)
    mlp_chip = (mlp_own.astype(f32) + swap(mlp_oth).astype(f32)).astype(bf16)
    mlp_recv = across(mlp_chip)
    moved_two = plane_exchange(held(blocks_two, mlp_chip))


    dq, kept, given = kernel_call(
        attend_back_kernel,
        [((2048, HEAD), bf16), ((2048, 128), f32), ((2048, 128), bf16)],
        [
            ((2048, 128), bf16),
            ((2048, 128), bf16),
            ((4096, 128), bf16),
            ((HEAD, 4096), bf16),
            ((8, TILE), f32),
            ((4096, 128), f32),
        ],
        name="attend_back",
        brought=((1, 4), (2, 4), (3, 2), (4, 2), (5, 1)),
        lazy=True,
    )(scalars, mine, theirs, grad_mixed, mixed, lse)
    (packed,) = kernel_call(
        pack_grads_kernel,
        [((SUBS, 96, 128), bf16)],
        stored=(0,),
        name="pack_grads",
        late=(mlp_recv,),
    )(scalars, dq, kept, swap(given))
    packed = held(packed, moved_two)
    grads_back = exchange(packed)

    blocks_three = weight_grads(
        [
            down_parts + ((P_TWO, width),),
            (grad_attn, grad_attn_oth, heads_own, heads_recv, (0, LOCAL)),
        ],
        late=(packed,),
    )
    second_core = swap(second_sums)
    normed_own, normed_oth = kernel_call(
        first_norm_kernel,
        [((ROWS, width), bf16), ((ROWS, width), bf16)],
        name="first_norm",
        stored=(0, 1),
        late=(packed,),
    )(core_s, split_tokens, ln_gains, row_biases)
    sums_one = plane_sum(moved_one)
    sums_two = plane_sum(moved_two)

    rows_own, rows_oth, gn_one_part = kernel_call(
        token_grads_kernel,
        [((ROWS, 3 * LOCAL), bf16), ((ROWS, 3 * LOCAL), bf16), ((ROWS, width), bf16)],
        stored=(0, 1),
        name="token_grads",
        brought=((1, 4), (2, 3), (3, 3)),
        lazy=True,
    )(core_s, grads_back, w_own, w_oth)
    rows_recv = swap(rows_oth)
    moved_three = plane_exchange(
        held(blocks_three, normed_own, sums_one[1], sums_two[1], second_core)
    )
    (first_sums,) = kernel_call(first_sums_kernel, [((8, width), f32)], name="first_sums")(
        core_s, gn_one_part, split_tokens
    )
    sums_parts = (
        first_sums,
        swap(first_sums),
        across(first_sums),
        lax.ppermute(first_sums, "tp", CROSS_SWAP),
    )
    blocks_last = last_grads(normed_own, normed_oth, rows_own, rows_recv)
    blocks_last = vector_rows(
        blocks_last, rows_own, rows_recv, *sums_parts, second_sums, second_core, up_sums_own, up_sums_oth
    )
    gn_one_recv = across(gn_one_part)
    blocks_last = held(blocks_last, moved_three, gn_one_recv)
    moved_last = exchange(blocks_last)

    layer_own, rms_own = kernel_call(
        layer_kernel,
        [((ROWS, width), f32), ((3, ROWS), f32)],
        scalars=0,
        name="layer_out",
        late=(blocks_last,),
    )(residual, attn_part, attn_recv, mlp_chip, mlp_recv, row_biases)
    layer_out = join_rows(core_s, layer_own, swap(layer_own))
    (rms_rows,) = kernel_call(
        rms_join_kernel, [((3, 2 * ROWS), f32)], name="rms_join"
    )(core_s, rms_own, swap(rms_own))
    (input_own,) = kernel_call(input_grads_kernel, [((ROWS, width), f32)], name="input_grads")(
        core_s, gn_one_part, gn_one_recv, grad_residual, split_tokens, ln_gains
    )
    input_grad = join_rows(core_s, input_own, swap(input_own))
    (
        grad_up,
        grad_down,
        grad_out,
        grad_qkv,
        grad_gains,
        grad_shifts,
        grad_up_bias,
        grad_qv_bias,
    ) = kernel_call(
        last_sums_kernel,
        [
            ((32, width), f32),
            ((32, width), f32),
            ((32, LOCAL), f32),
            ((3, 32, LOCAL), f32),
            ((2, 32), f32),
            ((4, 32), f32),
            ((1, 32), f32),
            ((2, 8), f32),
        ],
        scalars=0,
        name="last_sums",
        late=(layer_out, input_grad, rms_rows),
    )(moved_last, *sums_one, *sums_two, *plane_sum(moved_three))
    return (
        layer_out,
        input_grad,
        rms_rows,
        grad_qkv.transpose(1, 0, 2),
        grad_qv_bias,
        grad_out.T,
        grad_up,
        grad_up_bias[0],
        grad_down.T,
        grad_gains,
        grad_shifts,
    )


def solution(mesh):
    return jax.shard_map(
        per_device,
        mesh=mesh,
        in_specs=(
            P("ctx", None),
            P(),
            P(None, None, "tp"),
            P(None, "tp"),
            P("tp", None),
            P(None, "tp"),
            P("tp"),
            P("tp", None),
            P(),
            P(),
            P("ctx", None),
        ),
        out_specs=(
            P("ctx", None),
            P("ctx", None),
            P(None, "ctx"),
            P("ctx", None, "tp"),
            P(None, ("tp", "ctx")),
            P("tp", "ctx"),
            P("ctx", "tp"),
            P(("tp", "ctx")),
            P("tp", "ctx"),
            P(None, "ctx"),
            P(None, "ctx"),
        ),
        check_vma=False,
    )
```

```python
import jax
import jax.numpy as jnp
from jax import lax
from jax.experimental import pallas as pl
from jax.experimental.pallas import tpu as pltpu
from jax.sharding import PartitionSpec as P

HEAD = 64
SUBS = 32
HALF = 64
GROUPS = 4
ROWS = GROUPS * HALF
LOCAL = 256
P_ONE = 640
P_TWO = 512
LIMIT = 36
TILE = 256
CHUNK = 512
EPSILON = 1e-05
RMS_EPSILON = 1e-06
LOG_SHRINK = 10 * 0.6931471805599453
SHRINK = 2.0**-10
CORE_SWAP = [(0, 1), (1, 0), (2, 3), (3, 2)]
YHI_SWAP = [(0, 2), (2, 0), (1, 3), (3, 1)]
YLO_SWAP = [(j, j ^ 4) for j in range(SUBS)]
CROSS_SWAP = [(0, 3), (3, 0), (1, 2), (2, 1)]
PLANES = [[z * 8 + y * 4 + x for z in range(4) for x in range(4)] for y in range(2)]
NT = (((1,), (1,)), ((), ()))
TN = (((0,), (0,)), ((), ()))
bf16 = jnp.bfloat16
f32 = jnp.float32


def norm_parts(values):
    centre = jnp.mean(values, axis=-1, keepdims=True)
    centred = values - centre
    spread = jnp.mean(centred * centred, axis=-1, keepdims=True)
    inverse = lax.rsqrt(spread + EPSILON)
    return centred * inverse, inverse


def norm_back(grad_normed, unit_rows, inverse, gain):
    grad_unit = grad_normed * gain
    first_mean = jnp.mean(grad_unit, axis=-1, keepdims=True)
    second_mean = jnp.mean(grad_unit * unit_rows, axis=-1, keepdims=True)
    return inverse * (grad_unit - first_mean - unit_rows * second_mean)


def hold(arrays):
    return [pltpu.with_memory_space_constraint(x, pltpu.HBM) for x in arrays]


def order(arrays):
    return [x if x.size * x.dtype.itemsize < 2**18 else hold([x])[0] for x in arrays]


def pieces_of(ref, stage, sems, first, pieces):
    step = ref.shape[0] // pieces
    return [
        pltpu.make_async_copy(
            ref.at[pl.ds(i * step, step)], stage.at[pl.ds(i * step, step)], sems.at[first + i]
        )
        for i in range(pieces)
    ]


def with_copies(body, n_in, n_late, n_out, stored, brought, lazy):
    def kernel(*refs):
        ins, outs = list(refs[:n_in]), list(refs[n_in + n_late : n_in + n_late + n_out])
        rest = refs[n_in + n_late + n_out :]
        arriving = {}
        if brought:
            stages, in_sems, rest = rest[: len(brought)], rest[len(brought)], rest[len(brought) + 1 :]
            first = 0
            for stage, (o, pieces) in zip(stages, brought):
                arriving[o] = pieces_of(ins[o], stage, in_sems, first, pieces)
                ins[o] = stage
                first += pieces
            for copies in arriving.values():
                for copy in copies:
                    copy.start()
        stages, rest = rest[: len(stored)], rest[len(stored) :]
        copies = []
        if stored:
            sems, rest = rest[0], rest[1:]
            copies = [
                pltpu.make_async_copy(stage, outs[o], sems.at[i])
                for i, (stage, o) in enumerate(zip(stages, stored))
            ]
        for stage, o in zip(stages, stored):
            outs[o] = stage
        leaving = dict(zip(stored, copies))
        if lazy:
            body(arriving, leaving, *ins, *outs, *rest)
        else:
            for arrivals in arriving.values():
                for copy in arrivals:
                    copy.wait()
            body(*ins, *outs, *rest)
        for copy in leaving.values():
            copy.start()
        for copy in copies:
            copy.wait()

    return kernel


def kernel_call(
    body, outs, scratch=(), scalars=1, name=None, stored=(), late=(), brought=(), lazy=False, direct=()
):
    smem = pl.BlockSpec(memory_space=pltpu.SMEM)
    vmem = pl.BlockSpec(memory_space=pltpu.VMEM)
    hbm = pl.BlockSpec(memory_space=pltpu.HBM)
    shapes = [x if hasattr(x, "memory_space") or not isinstance(x, tuple) else pltpu.VMEM(*x) for x in scratch]
    if stored:
        shapes = (
            [pltpu.VMEM(*outs[o]) for o in stored]
            + [pltpu.SemaphoreType.DMA((len(stored),))]
            + shapes
        )

    def call(*args):
        args, more, specs = list(args), [], [smem] * scalars + [vmem] * (len(args) - scalars)
        for o, _ in brought:
            specs[o] = hbm
            more.append(pltpu.VMEM(args[o].shape, args[o].dtype))
            (args[o],) = hold([args[o]])
        if brought:
            more.append(pltpu.SemaphoreType.DMA((sum(pieces for _, pieces in brought),)))
        return pl.pallas_call(
            with_copies(body, len(args), len(late), len(outs), stored, brought, lazy),
            out_shape=[
                pltpu.HBM(s, d) if o in stored + direct else jax.ShapeDtypeStruct(s, d)
                for o, (s, d) in enumerate(outs)
            ],
            in_specs=specs + [pl.BlockSpec(memory_space=pl.ANY)] * len(late),
            out_specs=[hbm if o in stored + direct else vmem for o in range(len(outs))],
            scratch_shapes=more + shapes,
            compiler_params=pltpu.CompilerParams(vmem_limit_bytes=LIMIT * 2**20),
            cost_estimate=pl.CostEstimate(flops=1, bytes_accessed=1, transcendentals=0),
            name=name,
        )(*args, *order(late))

    return call


def held(x, *late):
    hbm = pl.BlockSpec(memory_space=pltpu.HBM)
    return pl.pallas_call(
        lambda *refs: None,
        out_shape=pltpu.HBM(x.shape, x.dtype),
        in_specs=[hbm] + [pl.BlockSpec(memory_space=pl.ANY)] * len(late),
        out_specs=hbm,
        input_output_aliases={0: 0},
        cost_estimate=pl.CostEstimate(flops=1, bytes_accessed=1, transcendentals=0),
        name="held",
    )(*hold([x]), *late)


def fold(rows):
    return jnp.concatenate([rows[:32], rows[32:]], axis=1)


def unfold(packed):
    return jnp.concatenate([packed[:, :HEAD], packed[:, HEAD:]], axis=0)


def project_own_kernel(arriving, leaving, core_ref, x_ref, w_ref, gains, shifts, b_ref, send_ref, low_ref):
    for o in (1, 3, 4, 5):
        for copy in arriving[o]:
            copy.wait()
    x = x_ref[:, core_ref[0]].reshape(ROWS, -1).astype(f32)
    unit, _ = norm_parts(x)
    low = (unit * gains[0:1].astype(f32) + shifts[0:1].astype(f32)).astype(bf16)
    low_ref[...] = low
    for w in arriving[2]:
        w.wait()
    for g, h, qk, v in projected(low, w_ref, b_ref):
        send_ref[g * 4 + h, 0:64, :] = qk
        send_ref[g * 4 + h, 64:96, :] = v


def project_oth_kernel(core_ref, low_ref, w_ref, b_ref, first_ref, send_ref):
    core = core_ref[0]
    for g in range(GROUPS):
        for h in range(4):
            send_ref[g * 8 + core * 4 + h] = first_ref[g * 4 + h]
    for g, h, qk, v in projected(low_ref[...], w_ref, b_ref):
        block = g * 8 + (1 - core) * 4 + h
        send_ref[block, 0:64, :] = qk
        send_ref[block, 64:96, :] = v


def projected(low, w_ref, b_ref):
    q = jnp.dot(low, w_ref[0], preferred_element_type=f32) + b_ref[0:1].astype(f32)
    k = jnp.dot(low, w_ref[1], preferred_element_type=f32)
    v = jnp.dot(low, w_ref[2], preferred_element_type=f32) + b_ref[1:2].astype(f32)
    for g in range(GROUPS):
        for h in range(4):
            rows = slice(g * HALF, (g + 1) * HALF)
            cols = slice(h * HEAD, (h + 1) * HEAD)
            qk = jnp.concatenate([q[rows, cols], k[rows, cols]], axis=1)
            yield g, h, qk.astype(bf16), fold(v[rows, cols]).astype(bf16)


def pair_masks(core, transposed):
    shape = (CHUNK, TILE) if transposed else (TILE, CHUNK)
    q = lax.broadcasted_iota(jnp.int32, shape, 1 if transposed else 0)
    key = lax.broadcasted_iota(jnp.int32, shape, 0 if transposed else 1)
    other = key >= TILE
    k = jnp.where(other, key - TILE, key)
    q_sub = lax.shift_right_logical(q, 6)
    k_sub = lax.shift_right_logical(k, 6)
    prompt = (other & (q_sub + core > k_sub)) | (jnp.logical_not(other) & (q >= k))
    cont = prompt & (lax.shift_right_logical(q, 7) == lax.shift_right_logical(k, 7))
    return prompt, cont


def chunks_of(tile, prompt, cont):
    if tile < 4:
        return [(j, None) for j in range(tile)] + [(tile, prompt)]
    return [(j, None) for j in range(4)] + [(tile, cont)]


def places(sc_ref, d):
    p = sc_ref[SUBS + 1 + d]
    at = lax.shift_right_logical(p, 2) * CHUNK + (p & 3) * HALF
    return pl.ds(pl.multiple_of(p * HALF, HALF), HALF), pl.multiple_of(at, HALF)


def attend_kernel(
    sc_ref, own_ref, oth_ref, own_kept, oth_kept, out_ref, lse_ref, q_s, k_s, v_s, kept_sems
):
    keeping = [
        pltpu.make_async_copy(ref, kept, kept_sems.at[i])
        for i, (ref, kept) in enumerate(((own_ref, own_kept), (oth_ref, oth_kept)))
    ]
    for copy in keeping:
        copy.start()
    core = sc_ref[SUBS]
    const = jnp.full((HALF, HEAD), SHRINK, bf16)
    for p in range(SUBS):
        d = sc_ref[p]
        at = p // 4 * CHUNK + p % 4 * HALF
        q_s[p * HALF : (p + 1) * HALF, :] = own_ref[d, 0:64, :HEAD] * jnp.asarray(0.125, bf16)
        for ref, start in ((own_ref, at), (oth_ref, at + TILE)):
            k_s[start : start + HALF, :] = ref[d, 0:64, HEAD:]
            v = unfold(ref[d, 64:96, :]) * jnp.asarray(SHRINK, bf16)
            v_s[start : start + HALF, :] = jnp.concatenate([v, const], axis=1)
    prompt, cont = pair_masks(core, False)
    for t in range(8):
        q = q_s[t * TILE : (t + 1) * TILE, :]
        total = None
        for j, mask in chunks_of(t, prompt, cont):
            keys = slice(j * CHUNK, (j + 1) * CHUNK)
            s = lax.dot_general(q, k_s[keys, :], NT, preferred_element_type=f32)
            w = jnp.exp(s)
            if mask is not None:
                w = jnp.where(mask, w, 0.0)
            part = jnp.dot(w.astype(bf16), v_s[keys, :], preferred_element_type=f32)
            total = part if total is None else total + part
        mixed = total[:, :HEAD] / total[:, HEAD:]
        lse_ref[t : t + 1, :] = jnp.log(total.T[HEAD : HEAD + 1, :]) + LOG_SHRINK
        for i in range(4):
            out_ref[sc_ref[t * 4 + i]] = fold(mixed[i * HALF : (i + 1) * HALF]).astype(bf16)
    for copy in keeping:
        copy.wait()


def attend_back_kernel(
    arriving, leaving, sc_ref, own_ref, oth_ref, do_ref, o_ref, lse_ref,
    dq_ref, keep_ref, send_ref,
    q_s, do_s, vk_s, kt_s, inner_s, acc_s,
):
    core = sc_ref[SUBS]
    zero = jnp.zeros((HALF, HEAD), bf16)
    for o, ref, shift in ((1, own_ref, 0), (2, oth_ref, TILE)):
        for d in range(SUBS):
            if d % 8 == 0:
                arriving[o][d // 8].wait()
            rows, at = places(sc_ref, d)
            if o == 1:
                q = ref[d, 0:64, :HEAD] * jnp.asarray(0.125, bf16)
                q_s[rows, :] = jnp.concatenate([zero, q], axis=1)
            vk_s[pl.ds(at + shift, HALF), :] = jnp.concatenate(
                [unfold(ref[d, 64:96, :]), ref[d, 0:64, HEAD:]], axis=1
            )
    for d in range(SUBS):
        if d % 16 == 0:
            arriving[3][d // 16].wait()
        rows, _ = places(sc_ref, d)
        do_s[rows, :] = jnp.concatenate([unfold(do_ref[d]), zero], axis=1)
    for j in range(8):
        keys = slice(j * CHUNK, (j + 1) * CHUNK)
        kt_s[:, keys] = vk_s[keys, :].T[HEAD:, :]
    for o in (4, 5):
        for copy in arriving[o]:
            copy.wait()
    for t in range(8):
        both = []
        for i in range(4):
            d = sc_ref[t * 4 + i]
            both.append(unfold(do_ref[d].astype(f32) * o_ref[d].astype(f32)))
        inner_s[t : t + 1, :] = jnp.sum(jnp.concatenate(both, axis=0).T, axis=0, keepdims=True)
    prompt, cont = pair_masks(core, True)
    started = set()
    for t in range(8):
        tile = slice(t * TILE, (t + 1) * TILE)
        q = q_s[tile, :]
        grad = do_s[tile, :]
        lse = lse_ref[t : t + 1, :]
        inner = inner_s[t : t + 1, :]
        dq = None
        for j, mask in chunks_of(t, prompt, cont):
            keys = slice(j * CHUNK, (j + 1) * CHUNK)
            vk = vk_s[keys, :]
            s = lax.dot_general(vk, q, NT, preferred_element_type=f32)
            a = jnp.exp(s - lse)
            if mask is not None:
                a = jnp.where(mask, a, 0.0)
            dp = lax.dot_general(vk, grad, NT, preferred_element_type=f32)
            ds = (a * (dp - inner)).astype(bf16)
            part = jnp.dot(a.astype(bf16), grad, preferred_element_type=f32) + jnp.dot(
                ds, q, preferred_element_type=f32
            )
            if j in started:
                acc_s[keys, :] += part
            else:
                acc_s[keys, :] = part
                started.add(j)
            dq_part = jnp.dot(kt_s[:, keys], ds, preferred_element_type=f32)
            dq = dq_part if dq is None else dq + dq_part
        dq_ref[tile, :] = (dq * 0.125).T.astype(bf16)
    for j in range(8):
        keep_ref[j * TILE : (j + 1) * TILE, :] = acc_s[j * CHUNK : j * CHUNK + TILE, :]
        send_ref[j * TILE : (j + 1) * TILE, :] = acc_s[
            j * CHUNK + TILE : (j + 1) * CHUNK, :
        ].astype(bf16)


def pack_grads_kernel(sc_ref, dq_ref, keep_ref, recv_ref, out_ref):
    for p in range(SUBS):
        rows = slice(p * HALF, (p + 1) * HALF)
        summed = (keep_ref[rows, :] + recv_ref[rows, :].astype(f32)).astype(bf16)
        d = sc_ref[p]
        out_ref[d, 0:64, :] = jnp.concatenate([dq_ref[rows, :], summed[:, HEAD:]], axis=1)
        out_ref[d, 64:96, :] = fold(summed[:, :HEAD])


def out_kernel(
    arriving, leaving, core_ref, recv_ref, own_w, oth_w, own_ref, oth_ref, part_ref
):
    core = core_ref[0]
    for half, ref in ((core, own_ref), (1 - core, oth_ref)):
        for g in range(GROUPS):
            heads = [unfold(recv_ref[g * 8 + half * 4 + h]) for h in range(4)]
            ref[g * HALF : (g + 1) * HALF, :] = jnp.concatenate(heads, axis=1)
    for o in (0, 1):
        leaving.pop(o).start()
    part = jnp.dot(own_ref[...], own_w[...], preferred_element_type=f32) + jnp.dot(
        oth_ref[...], oth_w[...], preferred_element_type=f32
    )
    part_ref[...] = part.astype(bf16)


def split_kernel(core_ref, rows_ref, own_ref, oth_ref):
    own_ref[...] = rows_ref[:, core_ref[0]].reshape(own_ref.shape)
    oth_ref[...] = rows_ref[:, 1 - core_ref[0]].reshape(oth_ref.shape)


def first_norm_kernel(core_ref, x_ref, gains, shifts, own_ref, oth_ref):
    for half, low_ref in ((core_ref[0], own_ref), (1 - core_ref[0], oth_ref)):
        unit, _ = norm_parts(x_ref[:, half].reshape(ROWS, -1).astype(f32))
        low_ref[...] = (unit * gains[0:1].astype(f32) + shifts[0:1].astype(f32)).astype(bf16)


def layer_kernel(
    residual_ref, part_ref, part_recv_ref, mlp_ref, mlp_recv_ref, shifts, layer_ref, rms_ref
):
    attn = (part_ref[...].astype(f32) + part_recv_ref[...].astype(f32)) + shifts[1:2].astype(f32)
    mlp = (mlp_ref[...].astype(f32) + mlp_recv_ref[...].astype(f32)) + shifts[3:4].astype(f32)
    layer = residual_ref[...] + mlp
    layer_ref[...] = layer
    for i, rows in enumerate((layer, attn, mlp)):
        squares = rows * rows
        folded = sum(squares[:, c : c + 128] for c in range(0, squares.shape[1], 128))
        mean = jnp.sum(folded.T, axis=0, keepdims=True) / squares.shape[1]
        rms_ref[i : i + 1, :] = jnp.sqrt(mean + RMS_EPSILON)


def rms_join_kernel(core_ref, own_ref, oth_ref, out_ref):
    first = core_ref[0] == 0
    own, oth = own_ref[...], oth_ref[...]
    low, high = jnp.where(first, own, oth), jnp.where(first, oth, own)
    pieces = []
    for g in range(GROUPS):
        pieces += [rows[:, g * HALF : (g + 1) * HALF] for rows in (low, high)]
    out_ref[...] = jnp.concatenate(pieces, axis=1)


def second_norm_kernel(
    arriving, leaving, core_ref, part_ref, recv_ref, x_ref, gains, shifts, residual_ref, low_ref
):
    x = x_ref[:, core_ref[0]].reshape(ROWS, -1).astype(f32)
    branch = (part_ref[...].astype(f32) + recv_ref[...].astype(f32)) + shifts[1:2].astype(f32)
    residual = x + branch
    residual_ref[...] = residual
    leaving.pop(0).start()
    unit, _ = norm_parts(residual)
    low_ref[...] = (unit * gains[1:2].astype(f32) + shifts[2:3].astype(f32)).astype(bf16)


def put_blocks(stage, to, made, planes):
    if planes:
        for j in range(SUBS):
            at = (j // 8 * 8 + j % 4 * 2 + j // 4 % 2) * 32
            stage[at : at + 32, to] = made[j * 32 : (j + 1) * 32]
    else:
        stage[:, to] = made


def fetch_kernel(first_ref, second_ref, first_out, second_out, done_ref, sems):
    done_ref[...] = jnp.zeros_like(done_ref)
    copies = []
    for i, (ref, out) in enumerate(((first_ref, first_out), (second_ref, second_out))):
        for j in range(4):
            rows = pl.ds(j * 256, 256)
            copies.append(pltpu.make_async_copy(ref.at[rows], out.at[rows], sems.at[4 * i + j]))
    for copy in copies:
        copy.start()
    for copy in copies:
        copy.wait()


def fetch(first, second, late):
    hbm = pl.BlockSpec(memory_space=pltpu.HBM)
    vmem = pl.BlockSpec(memory_space=pltpu.VMEM)
    return pl.pallas_call(
        lambda a, b, unused, *rest: fetch_kernel(a, b, *rest),
        out_shape=[pltpu.VMEM(x.shape, x.dtype) for x in (first, second)]
        + [jax.ShapeDtypeStruct((8, 128), f32)],
        in_specs=[hbm] * 3,
        out_specs=[vmem] * 3,
        scratch_shapes=[pltpu.SemaphoreType.DMA((8,))],
        compiler_params=pltpu.CompilerParams(vmem_limit_bytes=LIMIT * 2**20),
        cost_estimate=pl.CostEstimate(flops=1, bytes_accessed=1, transcendentals=0),
        name="fetch",
    )(*hold((first, second, late)))


def feed_half(rows_ref, cot_ref, up_ref, bias_ref, down_ref, active_ref, grad_ref, back_ref, sums_ref):
    total = None
    for c in range(4):
        cols = slice(c * 256, (c + 1) * 256)
        up = up_ref[:, cols]
        bias = jnp.concatenate([bias_ref[2 * c + b : 2 * c + b + 1] for b in range(2)], axis=1)
        hidden = jnp.dot(rows_ref[...], up, preferred_element_type=f32) + bias.astype(f32)
        grad_active = lax.dot_general(
            cot_ref[...], down_ref[cols, :], NT, preferred_element_type=f32
        )
        share = 0.5 + 0.5 * lax.erf(hidden * 0.7071067811865476)
        density = jnp.exp(hidden * hidden * -0.5) * 0.3989422804014327
        active_ref[:, cols] = (hidden * share).astype(bf16)
        grad = (grad_active * (share + hidden * density)).astype(bf16)
        grad_ref[:, cols] = grad
        sums_ref[0:1, cols] = jnp.sum(grad.astype(f32), axis=0, keepdims=True)
        part = lax.dot_general(grad, up, NT, preferred_element_type=f32)
        total = part if total is None else total + part
    back_ref[...] = total.astype(back_ref.dtype)


def feed_own_kernel(arriving, leaving, *refs):
    feed_half(*refs)


def feed_oth_kernel(
    arriving, leaving, rows_ref, cot_ref, up_ref, bias_ref, down_ref, own_ref, own_grad,
    active_ref, grad_ref, back_ref, sums_ref, blocks_ref,
):
    feed_half(
        rows_ref, cot_ref, up_ref, bias_ref, down_ref, active_ref, grad_ref, back_ref, sums_ref
    )
    for o in range(4):
        leaving.pop(o).start()
    for copy in arriving[6]:
        copy.wait()
    for c in range(0, P_ONE, 256):
        cols = slice(c, min(c + 256, P_ONE))
        made = lax.dot_general(own_ref[...], own_grad[:, cols], TN, preferred_element_type=f32)
        made += lax.dot_general(rows_ref[...], grad_ref[:, cols], TN, preferred_element_type=f32)
        put_blocks(blocks_ref, cols, made.astype(bf16), True)
    leaving.pop(4).start()


def feed_out_kernel(arriving, leaving, own_ref, oth_ref, down_ref, own_out, oth_out):
    for o in (0, 1, 2):
        for copy in arriving[o]:
            copy.wait()
    for o, ref, out_ref in ((0, own_ref, own_out), (1, oth_ref, oth_out)):
        made = jnp.dot(ref[...], down_ref[...], preferred_element_type=f32)
        out_ref[...] = made.astype(bf16)
        leaving.pop(o).start()


def residual_grads_kernel(
    arriving, leaving, core_ref, own_ref, recv_ref, residual_ref, cot_ref, gains, own_w, oth_w,
    grad_ref, low_ref, send_ref, sums_ref,
):
    core = core_ref[0]
    unit, inverse = norm_parts(residual_ref[...])
    grad_normed = own_ref[...].astype(f32) + recv_ref[...].astype(f32)
    cot = cot_ref[...].astype(f32)
    grad = cot + norm_back(grad_normed, unit, inverse, gains[1:2].astype(f32))
    grad_ref[...] = grad
    low = grad.astype(bf16)
    low_ref[...] = low
    sums = [grad_normed * unit, low.astype(f32), grad_normed, cot]
    for i, rows in enumerate(sums):
        sums_ref[i : i + 1, :] = jnp.sum(rows, axis=0, keepdims=True)
    for o in (0, 1, 3):
        leaving.pop(o).start()
    for half, w_ref in ((core, own_w), (1 - core, oth_w)):
        made = lax.dot_general(low, w_ref[...], NT, preferred_element_type=f32)
        for g in range(GROUPS):
            for h in range(4):
                block = made[g * HALF : (g + 1) * HALF, h * HEAD : (h + 1) * HEAD]
                send_ref[g * 8 + half * 4 + h] = fold(block).astype(bf16)


def token_grads_kernel(arriving, leaving, core_ref, recv_ref, own_w, oth_w, own_ref, oth_ref, part_ref):
    core = core_ref[0]
    part = None
    for copy in arriving[1]:
        copy.wait()
    for half, w_ref, ref in ((core, own_w, own_ref), (1 - core, oth_w, oth_ref)):
        for g in range(GROUPS):
            rows = slice(g * HALF, (g + 1) * HALF)
            blocks = [recv_ref.at[g * 8 + half * 4 + h] for h in range(4)]
            pieces = (
                [b[0:64, :HEAD] for b in blocks]
                + [b[0:64, HEAD:] for b in blocks]
                + [unfold(b[64:96, :]) for b in blocks]
            )
            ref[rows, :] = jnp.concatenate(pieces, axis=1)
        leaving.pop(0 if ref is own_ref else 1).start()
        for i in range(3):
            arriving[2 if w_ref is own_w else 3][i].wait()
            made = lax.dot_general(
                ref[:, i * LOCAL : (i + 1) * LOCAL], w_ref[i], NT, preferred_element_type=f32
            )
            part = made if part is None else part + made
    part_ref[...] = part.astype(bf16)


def first_sums_kernel(core_ref, part_ref, x_ref, sums_ref):
    unit, _ = norm_parts(x_ref[:, core_ref[0]].reshape(ROWS, -1).astype(f32))
    part = part_ref[...].astype(f32)
    sums_ref[0:1, :] = jnp.sum(part * unit, axis=0, keepdims=True)
    sums_ref[1:2, :] = jnp.sum(part, axis=0, keepdims=True)
    sums_ref[2:8, :] = jnp.zeros((6, part.shape[1]), f32)


def input_grads_kernel(core_ref, part_ref, recv_ref, grad_ref, x_ref, gains, out_ref):
    x = x_ref[:, core_ref[0]].reshape(ROWS, -1).astype(f32)
    unit, inverse = norm_parts(x)
    grad_normed = part_ref[...].astype(f32) + recv_ref[...].astype(f32)
    out_ref[...] = grad_ref[...] + norm_back(grad_normed, unit, inverse, gains[0:1].astype(f32))


def join_kernel(core_ref, own_ref, oth_ref, out_ref, sems):
    core = core_ref[0]
    copies = []
    for i, (ref, half) in enumerate(((own_ref, core), (oth_ref, 1 - core))):
        for g in range(GROUPS):
            rows = pl.ds(g * HALF, HALF)
            at = i * GROUPS + g
            copies.append(pltpu.make_async_copy(ref.at[rows], out_ref.at[g, half], sems.at[at]))
    for copy in copies:
        copy.start()
    for copy in copies:
        copy.wait()


def join_rows(core_s, own, oth):
    width = own.shape[1]
    vmem = pl.BlockSpec(memory_space=pltpu.VMEM)
    joined = pl.pallas_call(
        join_kernel,
        out_shape=pltpu.HBM((GROUPS, 2, HALF, width), own.dtype),
        in_specs=[pl.BlockSpec(memory_space=pltpu.SMEM), vmem, vmem],
        out_specs=pl.BlockSpec(memory_space=pltpu.HBM),
        scratch_shapes=[pltpu.SemaphoreType.DMA((2 * GROUPS,))],
        compiler_params=pltpu.CompilerParams(vmem_limit_bytes=8 * 2**20),
        cost_estimate=pl.CostEstimate(flops=1, bytes_accessed=1, transcendentals=0),
        name="join_rows",
    )(core_s, own, oth)
    return joined.reshape(2 * ROWS, width)


def weight_grads_kernel(spans, planes, arriving, *refs):
    out_ref, stage, sems = refs[-3:]
    copies = []

    def send(start, stop):
        copies.append(
            pltpu.make_async_copy(
                stage.at[:, pl.ds(start, stop - start)],
                out_ref.at[:, pl.ds(start, stop - start)],
                sems.at[len(copies)],
            )
        )
        copies[-1].start()

    start = 0
    for i, (first, last) in enumerate(spans):
        a_own, a_oth, b_own, b_oth = refs[4 * i : 4 * i + 4]
        for o in range(4 * i, 4 * i + 4):
            for copy in arriving[o]:
                copy.wait()
        for c in range(first, last, 256):
            cols = slice(c, min(c + 256, last))
            made = lax.dot_general(a_own[...], b_own[:, cols], TN, preferred_element_type=f32)
            made += lax.dot_general(a_oth[...], b_oth[:, cols], TN, preferred_element_type=f32)
            stop = start + cols.stop - cols.start
            put_blocks(stage, slice(start, stop), made.astype(bf16), planes)
            send(start, stop)
            start = stop
    for copy in copies:
        copy.wait()


def last_grads_kernel(arriving, a_own, a_oth, b_own, b_oth, out_ref, stage, sems):
    copies = []
    for copies_in in arriving:
        for copy in copies_in:
            copy.wait()
    for k in range(3):
        cols = slice(k * 256, (k + 1) * 256)
        made = lax.dot_general(a_own[...], b_own[:, cols], TN, preferred_element_type=f32)
        made += lax.dot_general(a_oth[...], b_oth[:, cols], TN, preferred_element_type=f32)
        made = made.astype(bf16)
        for d in range(SUBS):
            for i in range(2):
                stage[d, k * 64 + i * 32 : k * 64 + i * 32 + 32, :] = made[
                    d * 32 : (d + 1) * 32, i * 128 : (i + 1) * 128
                ]
        part = pl.ds(k * 64, 64)
        copies.append(pltpu.make_async_copy(stage.at[:, part], out_ref.at[:, part], sems.at[k]))
        copies[-1].start()
    for copy in copies:
        copy.wait()


def last_grads(*args):
    hbm = pl.BlockSpec(memory_space=pltpu.HBM)

    def body(*refs):
        arriving = [pieces_of(refs[i], refs[5 + i], refs[9], 2 * i, 2) for i in range(4)]
        for copies in arriving:
            for copy in copies:
                copy.start()
        last_grads_kernel(arriving, *refs[5:9], refs[4], refs[10], refs[11])

    return pl.pallas_call(
        body,
        out_shape=pltpu.HBM((SUBS, 208, 128), bf16),
        in_specs=[hbm] * 4,
        out_specs=hbm,
        scratch_shapes=[pltpu.VMEM(x.shape, x.dtype) for x in args]
        + [
            pltpu.SemaphoreType.DMA((8,)),
            pltpu.VMEM((SUBS, 192, 128), bf16),
            pltpu.SemaphoreType.DMA((3,)),
        ],
        compiler_params=pltpu.CompilerParams(vmem_limit_bytes=LIMIT * 2**20),
        cost_estimate=pl.CostEstimate(flops=1, bytes_accessed=1, transcendentals=0),
        name="last_grads",
    )(*hold(args))


def vector_rows_kernel(
    into_ref, own_rows, oth_rows, own, core, across, cross, second, second_core, up_own, up_oth,
    out_ref, stage, sem,
):
    rows = ((own[...] + core[...]) + (across[...] + cross[...]))[0:2]
    rows = [rows, second[...] + second_core[...], up_own[...] + up_oth[...]]
    rows = jnp.concatenate(rows + [jnp.zeros((1, up_own.shape[1]), f32)], axis=0)
    pairs = []
    for first in (0, 2 * LOCAL):
        cols = slice(first, first + LOCAL)
        pairs.append(
            jnp.sum(own_rows[:, cols].astype(f32), axis=0, keepdims=True)
            + jnp.sum(oth_rows[:, cols].astype(f32), axis=0, keepdims=True)
        )
    pairs = jnp.concatenate(pairs + [jnp.zeros((6, LOCAL), f32)], axis=0)
    for d in range(SUBS):
        piece = jnp.concatenate([rows[:, d * 32 : (d + 1) * 32], jnp.zeros((8, 96), f32)], axis=1)
        bias = jnp.concatenate([pairs[:, d * 8 : (d + 1) * 8], jnp.zeros((8, 120), f32)], axis=1)
        stage[d] = jnp.concatenate([piece, bias], axis=0).astype(bf16)
    copy = pltpu.make_async_copy(stage, out_ref.at[:, pl.ds(192, 16)], sem)
    copy.start()
    copy.wait()


def vector_rows(into, *arrays):
    hbm = pl.BlockSpec(memory_space=pltpu.HBM)
    vmem = pl.BlockSpec(memory_space=pltpu.VMEM)
    return pl.pallas_call(
        vector_rows_kernel,
        out_shape=pltpu.HBM(into.shape, into.dtype),
        in_specs=[hbm] + [vmem] * len(arrays),
        out_specs=hbm,
        scratch_shapes=[pltpu.VMEM((SUBS, 16, 128), bf16), pltpu.SemaphoreType.DMA(())],
        input_output_aliases={0: 0},
        compiler_params=pltpu.CompilerParams(vmem_limit_bytes=LIMIT * 2**20),
        cost_estimate=pl.CostEstimate(flops=1, bytes_accessed=1, transcendentals=0),
        name="vector_rows",
    )(*hold([into]), *arrays)


def weight_grads(parts, late=(), planes=True, spare=0):
    width = parts[0][0].shape[1]
    spans = [p[4] for p in parts]
    args = [x for p in parts for x in p[:4]]
    columns = sum(last - first for first, last in spans)
    hbm = pl.BlockSpec(memory_space=pltpu.HBM)
    n = len(args)

    def body(*refs):
        out_ref, rest = refs[n + len(late)], refs[n + len(late) + 1 :]
        stages, in_sems, stage, sems = rest[:n], rest[n], rest[n + 1], rest[n + 2]
        arriving = [pieces_of(refs[i], stages[i], in_sems, 2 * i, 2) for i in range(n)]
        for copies in arriving:
            for copy in copies:
                copy.start()
        weight_grads_kernel(spans, planes, arriving, *stages, out_ref, stage, sems)

    return pl.pallas_call(
        body,
        out_shape=pltpu.HBM((width, columns + spare), bf16),
        in_specs=[hbm] * (n + len(late)),
        out_specs=hbm,
        scratch_shapes=[pltpu.VMEM(x.shape, x.dtype) for x in args]
        + [
            pltpu.SemaphoreType.DMA((2 * n,)),
            pltpu.VMEM((width, columns), bf16),
            pltpu.SemaphoreType.DMA((16,)),
        ],
        compiler_params=pltpu.CompilerParams(vmem_limit_bytes=LIMIT * 2**20),
        cost_estimate=pl.CostEstimate(flops=1, bytes_accessed=1, transcendentals=0),
        name="weight_grads",
    )(*hold(args + list(late)))


def plane_sum_kernel(y_ref, moved_ref, own_ref, oth_ref):
    for half, ref in ((y_ref[0], own_ref), (1 - y_ref[0], oth_ref)):
        ref[...] = jnp.sum(moved_ref[:, half].astype(f32), axis=0).astype(ref.dtype)


def last_sums_kernel(
    moved_ref, one_own, one_oth, two_own, two_oth, three_own, three_oth,
    up_ref, down_ref, out_ref, qkv_ref, gains_ref, shifts_ref, up_bias_ref, qv_ref,
):
    one = one_own[...] + one_oth[...].astype(f32)
    two = two_own[...] + two_oth[...].astype(f32)
    three = three_own[...] + three_oth[...].astype(f32)
    width = up_ref.shape[1]
    up_ref[:, :P_ONE] = one
    up_ref[:, P_ONE:] = two[:, : width - P_ONE]
    down_ref[:, :P_TWO] = two[:, width - P_ONE :]

    down_ref[:, P_TWO:] = three[:, : width - P_TWO]
    out_ref[...] = three[:, width - P_TWO :]
    summed = jnp.sum(moved_ref[...].astype(f32), axis=0)
    for i in range(6):
        qkv_ref[i // 2, :, i % 2 * 128 : i % 2 * 128 + 128] = summed[i * 32 : (i + 1) * 32]
    small = summed[192:208]
    gains_ref[0:1, :] = small[0:1, :32]
    gains_ref[1:2, :] = small[2:3, :32]
    shifts_ref[0:1, :] = small[1:2, :32]
    shifts_ref[1:4, :] = small[3:6, :32]
    up_bias_ref[...] = small[6:7, :32]
    qv_ref[...] = small[8:10, :8]


def per_device(
    tokens,
    sub_blocks,
    w_qkv,
    qv_bias,
    w_out,
    w_up,
    up_bias,
    w_down,
    ln_gains,
    row_biases,
    cotangent,
):
    width = tokens.shape[1]
    ctx = lax.axis_index("ctx").astype(jnp.int32)
    core = (lax.axis_index("tp") % 2).astype(jnp.int32)
    core_s = core.reshape(1)
    y_low = (ctx // 4 % 2).reshape(1)

    def swap(x):
        return lax.ppermute(x, "tp", CORE_SWAP)

    def across(x):
        return lax.ppermute(x, "tp", YHI_SWAP)

    def exchange(x):
        return lax.all_to_all(x, "ctx", 0, 0, tiled=True)

    def plane_exchange(blocks):
        return lax.all_to_all(blocks, "ctx", 0, 0, axis_index_groups=PLANES, tiled=True)

    def plane_sum(moved):
        own, oth = kernel_call(
            plane_sum_kernel,
            [((32, moved.shape[1]), f32), ((32, moved.shape[1]), bf16)],
            name="plane_sum",
            brought=((1, 4),),
        )(y_low, moved.reshape(16, 2, 32, -1))
        return own, lax.ppermute(oth, "ctx", YLO_SWAP)

    own_row = lax.dynamic_index_in_dim(sub_blocks, ctx // 8, 0, False)
    order = jnp.arange(SUBS, dtype=jnp.int32)
    holder = jnp.sum(
        jnp.where(own_row[:, None] == order[None, :], order[:, None], 0), axis=0
    ).astype(jnp.int32)
    scalars = jnp.concatenate([holder, core_s, own_row])

    split_tokens = tokens.reshape(GROUPS, 2, HALF, width)
    w_own = w_qkv.transpose(1, 0, 2)
    w_oth = swap(w_own)
    b_oth = swap(qv_bias)
    wo_own = w_out
    wo_oth = swap(w_out)

    first, low_own = kernel_call(
        project_own_kernel,
        [((16, 96, 128), bf16), ((ROWS, width), bf16)],
        name="project_own",
        brought=((1, 4), (2, 3), (3, 1), (4, 1), (5, 1)),
        lazy=True,
    )(core_s, split_tokens, w_own, ln_gains, row_biases, qv_bias)
    (send,) = kernel_call(
        project_oth_kernel,
        [((SUBS, 96, 128), bf16)],
        stored=(0,),
        name="project_oth",
    )(core_s, low_own, w_oth, b_oth, first)
    mine = exchange(send)
    theirs = swap(mine)

    mine, theirs, mixed, lse = kernel_call(
        attend_kernel,
        [
            ((SUBS, 96, 128), bf16),
            ((SUBS, 96, 128), bf16),
            ((SUBS, 32, 128), bf16),
            ((8, TILE), f32),
        ],
        [
            pltpu.VMEM((2048, HEAD), bf16),
            pltpu.VMEM((4096, HEAD), bf16),
            pltpu.VMEM((4096, 128), bf16),
            pltpu.SemaphoreType.DMA((2,)),
        ],
        name="attend",
        stored=(2, 3),
        direct=(0, 1),
    )(scalars, mine, theirs)
    mixed_back = exchange(mixed)
    cot_own, cot_oth = kernel_call(
        split_kernel,
        [((ROWS, width), bf16), ((ROWS, width), bf16)],
        stored=(0, 1),
        name="split_rows",
        late=(mixed,),
    )(core_s, cotangent.reshape(GROUPS, 2, HALF, width))
    heads_own, heads_oth, attn_part = kernel_call(
        out_kernel,
        [((ROWS, LOCAL), bf16), ((ROWS, LOCAL), bf16), ((ROWS, width), bf16)],
        stored=(0, 1),
        lazy=True,
        name="project_out",
        late=(cot_own,),
    )(core_s, mixed_back, wo_own, wo_oth)
    attn_recv = across(attn_part)
    up_here, down_here, fetched = fetch(w_up, w_down, heads_own)
    residual, normed_two_own = kernel_call(
        second_norm_kernel,
        [((ROWS, width), f32), ((ROWS, width), bf16)],
        stored=(0,),
        lazy=True,
        name="second_norm",
        late=(fetched,),
    )(core_s, attn_part, attn_recv, split_tokens, ln_gains, row_biases)
    normed_two_oth = swap(normed_two_own)

    half_outs = [((ROWS, width), bf16)] * 3 + [((1, width), f32)]
    bias_rows = up_bias.reshape(8, -1)
    active_own, grad_hidden_own, gn_two_own, up_sums_own = kernel_call(
        feed_own_kernel, half_outs, scalars=0, stored=(0, 1, 2, 3), lazy=True, name="feed_own"
    )(normed_two_own, cot_own, up_here, bias_rows, down_here)
    active_oth, grad_hidden_oth, gn_two_oth, up_sums_oth, blocks_one = kernel_call(
        feed_oth_kernel,
        half_outs + [((width, P_ONE), bf16)],
        scalars=0,
        stored=(0, 1, 2, 3, 4),
        brought=((6, 2),),
        lazy=True,
        name="feed_oth",
    )(normed_two_oth, cot_oth, up_here, bias_rows, down_here, normed_two_own, grad_hidden_own)
    gn_two_chip = (gn_two_own.astype(f32) + swap(gn_two_oth).astype(f32)).astype(bf16)
    up_parts = (normed_two_own, normed_two_oth, grad_hidden_own, grad_hidden_oth)
    down_parts = (cot_own, cot_oth, active_own, active_oth)
    gn_two_recv = across(gn_two_chip)
    moved_one = plane_exchange(blocks_one)
    blocks_two = weight_grads(
        [up_parts + ((P_ONE, width),), down_parts + ((0, P_TWO),)], late=(blocks_one,)
    )

    mlp_own, mlp_oth = kernel_call(
        feed_out_kernel,
        [((ROWS, width), bf16), ((ROWS, width), bf16)],
        scalars=0,
        stored=(0, 1),
        brought=((0, 2), (1, 2), (2, 4)),
        lazy=True,
        name="feed_out",
    )(active_own, active_oth, w_down)

    grad_residual, grad_attn, grad_heads, second_sums = kernel_call(
        residual_grads_kernel,
        [
            ((ROWS, width), f32),
            ((ROWS, width), bf16),
            ((SUBS, 32, 128), bf16),
            ((4, width), f32),
        ],
        stored=(0, 1, 2, 3),
        lazy=True,
        name="residual_grads",
        late=(blocks_two, mlp_own),
    )(core_s, gn_two_chip, gn_two_recv, residual, cot_own, ln_gains, wo_own, wo_oth)
    grad_mixed = exchange(held(grad_heads, moved_one))

    grad_attn_oth = swap(grad_attn)
    heads_recv = swap(heads_oth)
    mlp_chip = (mlp_own.astype(f32) + swap(mlp_oth).astype(f32)).astype(bf16)
    mlp_recv = across(mlp_chip)
    moved_two = plane_exchange(held(blocks_two, mlp_chip))


    dq, kept, given = kernel_call(
        attend_back_kernel,
        [((2048, HEAD), bf16), ((2048, 128), f32), ((2048, 128), bf16)],
        [
            ((2048, 128), bf16),
            ((2048, 128), bf16),
            ((4096, 128), bf16),
            ((HEAD, 4096), bf16),
            ((8, TILE), f32),
            ((4096, 128), f32),
        ],
        name="attend_back",
        brought=((1, 4), (2, 4), (3, 2), (4, 2), (5, 1)),
        lazy=True,
    )(scalars, mine, theirs, grad_mixed, mixed, lse)
    (packed,) = kernel_call(
        pack_grads_kernel,
        [((SUBS, 96, 128), bf16)],
        stored=(0,),
        name="pack_grads",
        late=(mlp_recv,),
    )(scalars, dq, kept, swap(given))
    packed = held(packed, moved_two)
    grads_back = exchange(packed)

    blocks_three = weight_grads(
        [
            down_parts + ((P_TWO, width),),
            (grad_attn, grad_attn_oth, heads_own, heads_recv, (0, LOCAL)),
        ],
        late=(packed,),
    )
    second_core = swap(second_sums)
    normed_own, normed_oth = kernel_call(
        first_norm_kernel,
        [((ROWS, width), bf16), ((ROWS, width), bf16)],
        name="first_norm",
        stored=(0, 1),
        late=(packed,),
    )(core_s, split_tokens, ln_gains, row_biases)
    sums_one = plane_sum(moved_one)
    sums_two = plane_sum(moved_two)

    rows_own, rows_oth, gn_one_part = kernel_call(
        token_grads_kernel,
        [((ROWS, 3 * LOCAL), bf16), ((ROWS, 3 * LOCAL), bf16), ((ROWS, width), bf16)],
        stored=(0, 1),
        name="token_grads",
        brought=((1, 4), (2, 3), (3, 3)),
        lazy=True,
    )(core_s, grads_back, w_own, w_oth)
    rows_recv = swap(rows_oth)
    moved_three = plane_exchange(
        held(blocks_three, normed_own, sums_one[1], sums_two[1], second_core)
    )
    (first_sums,) = kernel_call(first_sums_kernel, [((8, width), f32)], name="first_sums")(
        core_s, gn_one_part, split_tokens
    )
    sums_parts = (
        first_sums,
        swap(first_sums),
        across(first_sums),
        lax.ppermute(first_sums, "tp", CROSS_SWAP),
    )
    blocks_last = last_grads(normed_own, normed_oth, rows_own, rows_recv)
    blocks_last = vector_rows(
        blocks_last, rows_own, rows_recv, *sums_parts, second_sums, second_core, up_sums_own, up_sums_oth
    )
    gn_one_recv = across(gn_one_part)
    blocks_last = held(blocks_last, moved_three, gn_one_recv)
    moved_last = exchange(blocks_last)

    layer_own, rms_own = kernel_call(
        layer_kernel,
        [((ROWS, width), f32), ((3, ROWS), f32)],
        scalars=0,
        name="layer_out",
        late=(blocks_last,),
    )(residual, attn_part, attn_recv, mlp_chip, mlp_recv, row_biases)
    layer_out = join_rows(core_s, layer_own, swap(layer_own))
    (rms_rows,) = kernel_call(
        rms_join_kernel, [((3, 2 * ROWS), f32)], name="rms_join"
    )(core_s, rms_own, swap(rms_own))
    (input_own,) = kernel_call(input_grads_kernel, [((ROWS, width), f32)], name="input_grads")(
        core_s, gn_one_part, gn_one_recv, grad_residual, split_tokens, ln_gains
    )
    input_grad = join_rows(core_s, input_own, swap(input_own))
    (
        grad_up,
        grad_down,
        grad_out,
        grad_qkv,
        grad_gains,
        grad_shifts,
        grad_up_bias,
        grad_qv_bias,
    ) = kernel_call(
        last_sums_kernel,
        [
            ((32, width), f32),
            ((32, width), f32),
            ((32, LOCAL), f32),
            ((3, 32, LOCAL), f32),
            ((2, 32), f32),
            ((4, 32), f32),
            ((1, 32), f32),
            ((2, 8), f32),
        ],
        scalars=0,
        name="last_sums",
        late=(layer_out, input_grad, rms_rows),
    )(moved_last, *sums_one, *sums_two, *plane_sum(moved_three))
    return (
        layer_out,
        input_grad,
        rms_rows,
        grad_qkv.transpose(1, 0, 2),
        grad_qv_bias,
        grad_out.T,
        grad_up,
        grad_up_bias[0],
        grad_down.T,
        grad_gains,
        grad_shifts,
    )


def solution(mesh):
    return jax.shard_map(
        per_device,
        mesh=mesh,
        in_specs=(
            P("ctx", None),
            P(),
            P(None, None, "tp"),
            P(None, "tp"),
            P("tp", None),
            P(None, "tp"),
            P("tp"),
            P("tp", None),
            P(),
            P(),
            P("ctx", None),
        ),
        out_specs=(
            P("ctx", None),
            P("ctx", None),
            P(None, "ctx"),
            P("ctx", None, "tp"),
            P(None, ("tp", "ctx")),
            P("tp", "ctx"),
            P("ctx", "tp"),
            P(("tp", "ctx")),
            P("tp", "ctx"),
            P(None, "ctx"),
            P(None, "ctx"),
        ),
        check_vma=False,
    )
```
